32 devices in a mesh: groups: 2 (over y), blk: 16 (over z, x, core).
Axes of the slice: x: 2, y: 2, z: 4, core: 2. Of those that a mesh axis runs over, the one named last changes fastest.
Arguments:
- image_embeds: bfloat16 [4096, 1152], P(('groups', 'blk')), parts along dimension 0, may hold values from -100 to 100
- text_embeds: bfloat16 [4096, 1152], P(('groups', 'blk')), parts along dimension 0, may hold values from -20 to 20
- log_temp: float32 [1], replicated, may hold values from 3.7 to 4.6
- bias: float32 [1], replicated, may hold values from -3.5 to -1.5
Outputs:
- grad_image: bfloat16 [4096, 1152], P(('groups', 'blk')), parts along dimension 0
- grad_text: bfloat16 [4096, 1152], P(('groups', 'blk')), parts along dimension 0
- grad_temp: float32 [2], P('groups'), parts along dimension 0
- grad_bias: float32 [2], P('groups'), parts along dimension 0
The draws below stay inside these ranges and needn't reach their ends.
There are 2 independent parts, one for each index of `groups`. The reference program is written for one: setup_inputs(seed, part) draws one part's arguments, and reference() takes and returns one part's arrays. A program takes and returns all parts, laid end to end along the dimension named above; an argument that names none is the same for every part. Nothing has to cross between parts.
All inputs are finite; a program needn't handle non-finite values.
Results may differ from the reference program's by a relative error of at most 0.0034.
Values may be sent and summed in bfloat16 or wider, within the bound.
No kernel may reach another device: no remote copies, remote signals or barrier semaphores. Data moves between devices by JAX's collectives and lax.ppermute only.
A program may use at most 64 MiB of HBM per device.

```python
import jax
import jax.numpy as jnp
from jax import lax

D = 1152
ROWS = 128
TOKENS = 2048


def shared_parts(key, scale_low, scale_high):
    keys = jax.random.split(key, 4)
    common = jnp.clip(jax.random.normal(keys[0], (TOKENS, D), jnp.float32), -4.0, 4.0)
    weight = jax.random.uniform(keys[1], (TOKENS, 1), jnp.float32, 0.0, 0.5)
    spread = jnp.exp(jax.random.uniform(keys[2], (D,), jnp.float32, jnp.log(scale_low), jnp.log(scale_high)))
    direction = jnp.clip(jax.random.normal(keys[3], (D,), jnp.float32), -3.0, 3.0)
    return (common, weight, spread, direction)


def blend_noise(key, common, weight, uniform_width):
    if uniform_width > 0.0:
        private = jax.random.uniform(key, (TOKENS, D), jnp.float32, -uniform_width, uniform_width)
    else:
        private = jnp.clip(jax.random.normal(key, (TOKENS, D), jnp.float32), -4.0, 4.0)
    return jnp.sqrt(weight) * common + jnp.sqrt(1.0 - weight) * private


def draw_image_embeds(key, part):
    scale_low, scale_high, uniform_width, reach, pull_low, pull_high = (0.35, 2.8, 0.0, 2.0, 0.15, 0.35)
    common, weight, spread, direction = shared_parts(key, scale_low, scale_high)
    key = jax.random.fold_in(key, 11)
    keys = jax.random.split(key, 3)
    blended = blend_noise(keys[0], common, weight, uniform_width)
    blocks_all = TOKENS // ROWS
    block_ids = jnp.arange(TOKENS, dtype=jnp.int32) // ROWS
    jitter = jax.random.uniform(keys[1], (blocks_all,), jnp.float32)
    powers = reach * (block_ids.astype(jnp.float32) + jitter[block_ids]) / float(blocks_all)
    pull = jax.random.uniform(keys[2], (TOKENS, 1), jnp.float32, pull_low, pull_high)
    values = jnp.power(spread[None, :], powers[:, None]) * (blended + pull * direction[None, :])
    return values.astype(jnp.bfloat16)


def draw_text_embeds(key, part):
    scale_low, scale_high, uniform_width, pull_low, pull_high = (0.35, 2.8, 0.0, -0.3, 0.3)
    common, weight, spread, direction = shared_parts(key, scale_low, scale_high)
    key = jax.random.fold_in(key, 23)
    keys = jax.random.split(key, 2)
    blended = blend_noise(keys[0], common, weight, uniform_width)
    blocks_all = TOKENS // ROWS
    block_ids = jnp.arange(TOKENS, dtype=jnp.int32) // ROWS
    jitter = jax.random.uniform(keys[1], (blocks_all,), jnp.float32)
    ramp = (block_ids.astype(jnp.float32) + jitter[block_ids]) / float(blocks_all)
    pull = pull_low + (pull_high - pull_low) * ramp
    values = spread[None, :] * (blended + pull[:, None] * direction[None, :])
    return values.astype(jnp.bfloat16)


def setup_inputs(seed: int = 0, part: int = 0) -> dict:
    arg_keys = jax.random.split(jax.random.key(seed), 5)
    part_keys = jax.random.split(jax.random.fold_in(arg_keys[4], part), 5)
    return {
        "image_embeds": draw_image_embeds(jax.random.fold_in(jax.random.fold_in(arg_keys[4], part), 71), part),
        "text_embeds": draw_text_embeds(jax.random.fold_in(jax.random.fold_in(arg_keys[4], part), 71), part),
        "log_temp": jnp.clip(jax.random.uniform(arg_keys[2], (1,), jnp.float32, 3.7, 4.6), 3.7, 4.6),
        "bias": jnp.clip(jax.random.uniform(arg_keys[3], (1,), jnp.float32, -3.5, -1.5), -3.5, -1.5),
    }


def unit_rows(values):
    wide = values.astype(jnp.float32)
    inverse = lax.rsqrt(lax.optimization_barrier(jnp.sum(wide * wide, axis=1, keepdims=True)) + 1e-06)
    return (wide * inverse, inverse)

def reference(image_embeds, text_embeds, log_temp, bias):
    unit_img, inv_img = unit_rows(image_embeds)
    unit_txt, inv_txt = unit_rows(text_embeds)
    img_b = unit_img.astype(jnp.bfloat16)
    txt_b = unit_txt.astype(jnp.bfloat16)
    temp = jnp.exp(log_temp[0])
    shift_b = bias[0]
    columns = jnp.arange(TOKENS, dtype=jnp.int32)
    blocks = TOKENS // ROWS

    def block_step(carry, index):
        txt_acc, sum_g, sum_gl = carry
        first = (index * ROWS).astype(jnp.int32)
        rows_b = lax.dynamic_slice_in_dim(img_b, first, ROWS, 0)
        cosine = jnp.dot(rows_b, txt_b.T, preferred_element_type=jnp.float32)
        scaled = temp * cosine
        logits = scaled + shift_b
        row_ids = first + jnp.arange(ROWS, dtype=jnp.int32)
        sign = jnp.where(row_ids[:, None] == columns[None, :], 1.0, -1.0)
        grads = -sign * jax.nn.sigmoid(-sign * logits)
        grads_b = grads.astype(jnp.bfloat16)
        img_part = jnp.dot(grads_b, txt_b, preferred_element_type=jnp.float32)
        txt_part = jnp.dot(grads_b.T, rows_b, preferred_element_type=jnp.float32)
        return ((txt_acc + txt_part, sum_g + jnp.sum(grads), sum_gl + jnp.sum(grads * scaled)), img_part)
    init = (jnp.zeros((TOKENS, D), jnp.float32), jnp.zeros((), jnp.float32), jnp.zeros((), jnp.float32))
    (txt_acc, sum_g, sum_gl), img_parts = lax.scan(block_step, init, jnp.arange(blocks, dtype=jnp.int32))
    d_img = temp * img_parts.reshape(TOKENS, D)
    d_txt = temp * txt_acc
    grad_image = ((d_img - unit_img * lax.optimization_barrier(jnp.sum(unit_img * d_img, axis=1, keepdims=True))) * inv_img).astype(jnp.bfloat16)
    grad_text = ((d_txt - unit_txt * lax.optimization_barrier(jnp.sum(unit_txt * d_txt, axis=1, keepdims=True))) * inv_txt).astype(jnp.bfloat16)
    pairs = float(TOKENS) * float(TOKENS)
    grad_temp = jnp.reshape(sum_gl / pairs, (1,))
    grad_bias = jnp.reshape(sum_g / pairs, (1,))
    return (grad_image, grad_text, grad_temp, grad_bias)
```

```python
import functools

import jax
import jax.numpy as jnp
from jax import lax
from jax.experimental import pallas as pl
from jax.experimental.pallas import tpu as pltpu
from jax.sharding import PartitionSpec as P

VMEM_BYTES = 48 * 1024 * 1024


def swapped(x, bit):
    count = lax.axis_size("blk")
    return lax.ppermute(x, "blk", [(i, i ^ bit) for i in range(count)])


def gathered(block, bits):
    blocks = [block]
    for bit in bits:
        blocks = blocks + [swapped(b, bit) for b in blocks]
    return blocks


def unit_rows(values):
    wide = values.astype(jnp.float32)
    inverse = lax.rsqrt(jnp.sum(wide * wide, axis=1, keepdims=True) + 1e-06)
    return (wide * inverse, inverse)


def lane_sums(values):
    rows = jnp.sum(values.reshape(values.shape[0] // 8, 8, values.shape[1]), axis=0)
    total = rows[:, :128]
    for start in range(128, values.shape[1], 128):
        total = total + rows[:, start : start + 128]
    return total


def tile_kernel(n_img, n_txt, rows, *refs):
    imgs = refs[:n_img]
    txts = refs[n_img : n_img + n_txt]
    log_temp, bias = refs[n_img + n_txt : n_img + n_txt + 2]
    img_keep, img_send, txt_keep, txt_send, sums = refs[n_img + n_txt + 2 : n_img + n_txt + 7]
    img_b, txt_b, grad_b = refs[n_img + n_txt + 7 :]
    for k in range(n_img):
        img_b[k * rows : (k + 1) * rows] = unit_rows(imgs[k][...])[0].astype(jnp.bfloat16)
    for k in range(n_txt):
        txt_b[k * rows : (k + 1) * rows] = unit_rows(txts[k][...])[0].astype(jnp.bfloat16)
    temp = jnp.exp(log_temp[...])
    shift_b = bias[...]
    sum_g = jnp.zeros((8, 128), jnp.float32)
    sum_gl = jnp.zeros((8, 128), jnp.float32)
    step = 2 * rows
    half = n_img // 2 * rows
    for start in range(0, n_img * rows, step):
        panel = img_b[start : start + step]
        cosine = lax.dot_general(
            panel, txt_b[...], (((1,), (1,)), ((), ())), preferred_element_type=jnp.float32
        )
        scaled = temp * cosine
        logits = scaled + shift_b
        if start == 0:
            at_row = lax.broadcasted_iota(jnp.int32, logits.shape, 0)
            at_col = lax.broadcasted_iota(jnp.int32, logits.shape, 1)
            own = jnp.logical_and(at_row == at_col, at_row < rows)
            sign = jnp.where(own, 1.0, -1.0)
            grads = -sign * jax.nn.sigmoid(-sign * logits)
        else:
            grads = jax.nn.sigmoid(logits)
        sum_g = sum_g + lane_sums(grads)
        sum_gl = sum_gl + lane_sums(grads * scaled)
        grads_b = grads.astype(jnp.bfloat16)
        grad_b[start : start + step] = grads_b
        part = jnp.dot(grads_b, txt_b[...], preferred_element_type=jnp.float32)
        if start < half:
            img_keep[start : start + step] = part
        else:
            img_send[start - half : start - half + step] = part.astype(jnp.bfloat16)
    sums[0:8] = sum_g
    sums[8:16] = sum_gl
    half = n_txt // 2 * rows
    for start in range(0, n_txt * rows, step):
        part = lax.dot_general(
            grad_b[:, start : start + step],
            img_b[...],
            (((0,), (0,)), ((), ())),
            preferred_element_type=jnp.float32,
        )
        if start < half:
            txt_keep[start : start + step] = part
        else:
            txt_send[start - half : start - half + step] = part.astype(jnp.bfloat16)


def tile_call(imgs, txts, log_temp, bias):
    rows, width = imgs[0].shape
    n_img, n_txt = len(imgs), len(txts)
    half_img, half_txt = n_img // 2 * rows, n_txt // 2 * rows
    pairs = n_img * n_txt * rows * rows
    return pl.pallas_call(
        functools.partial(tile_kernel, n_img, n_txt, rows),
        out_shape=(
            jax.ShapeDtypeStruct((half_img, width), jnp.float32),
            jax.ShapeDtypeStruct((half_img, width), jnp.bfloat16),
            jax.ShapeDtypeStruct((half_txt, width), jnp.float32),
            jax.ShapeDtypeStruct((half_txt, width), jnp.bfloat16),
            jax.ShapeDtypeStruct((16, 128), jnp.float32),
        ),
        in_specs=[pl.BlockSpec(memory_space=pltpu.VMEM)] * (n_img + n_txt + 2),
        out_specs=[pl.BlockSpec(memory_space=pltpu.VMEM)] * 5,
        scratch_shapes=[
            pltpu.VMEM((n_img * rows, width), jnp.bfloat16),
            pltpu.VMEM((n_txt * rows, width), jnp.bfloat16),
            pltpu.VMEM((n_img * rows, n_txt * rows), jnp.bfloat16),
        ],
        compiler_params=pltpu.CompilerParams(vmem_limit_bytes=VMEM_BYTES),
        cost_estimate=pl.CostEstimate(
            flops=6 * pairs * width, bytes_accessed=0, transcendentals=2 * pairs
        ),
    )(*imgs, *txts, log_temp, bias)


def finish_kernel(value, keep, recv, log_temp, out):
    unit, inverse = unit_rows(value[...])
    grad = jnp.exp(log_temp[...]) * (keep[...] + recv[...].astype(jnp.float32))
    along = jnp.sum(unit * grad, axis=1, keepdims=True)
    out[...] = ((grad - unit * along) * inverse).astype(jnp.bfloat16)


def finish_call(value, keep, recv, log_temp):
    return pl.pallas_call(
        finish_kernel,
        out_shape=jax.ShapeDtypeStruct(value.shape, jnp.bfloat16),
        compiler_params=pltpu.CompilerParams(vmem_limit_bytes=VMEM_BYTES),
    )(value, keep, recv, log_temp)


def halved(keep, send, bits):
    for place, bit in enumerate(bits):
        recv = swapped(send, bit)
        if place == len(bits) - 1:
            return keep, recv
        half = keep.shape[0] // 2
        send = (keep[half:] + recv[half:].astype(jnp.float32)).astype(jnp.bfloat16)
        keep = keep[:half] + recv[:half].astype(jnp.float32)


def shards(image_embeds, text_embeds, log_temp, bias):
    rows, width = image_embeds.shape
    count = lax.axis_size("blk")
    depth = count.bit_length() - 1
    all_bits = [1 << place for place in range(depth)]
    split = 1 + depth // 2
    img_bits = all_bits[1:split]
    txt_bits = all_bits[:1] + all_bits[split:]
    temp_in = log_temp.reshape(1, 1)
    txts = gathered(text_embeds, txt_bits[::-1])
    imgs = gathered(image_embeds, img_bits[::-1])
    img_keep, img_send, txt_keep, txt_send, sums = tile_call(imgs, txts, temp_in, bias.reshape(1, 1))
    txt_keep, txt_recv = halved(txt_keep, txt_send, txt_bits)
    img_keep, img_recv = halved(img_keep, img_send, img_bits)
    for bit in all_bits:
        sums = sums + swapped(sums, bit)
    grad_text = finish_call(text_embeds, txt_keep, txt_recv, temp_in)
    grad_image = finish_call(image_embeds, img_keep, img_recv, temp_in)
    pairs = float(rows * count) * float(rows * count)
    grad_bias = jnp.reshape(jnp.sum(sums[:8]) / pairs, (1,))
    grad_temp = jnp.reshape(jnp.sum(sums[8:]) / pairs, (1,))
    return (grad_image, grad_text, grad_temp, grad_bias)


def solution(mesh):
    in_specs = (P(("groups", "blk"), None), P(("groups", "blk"), None), P(), P())
    out_specs = (P(("groups", "blk"), None), P(("groups", "blk"), None), P("groups"), P("groups"))
    return jax.shard_map(shards, mesh=mesh, in_specs=in_specs, out_specs=out_specs, check_vma=False)
```

```python
import functools

import jax
import jax.numpy as jnp
from jax import lax
from jax.experimental import pallas as pl
from jax.experimental.pallas import tpu as pltpu
from jax.sharding import PartitionSpec as P

VMEM_BYTES = 48 * 1024 * 1024


def swapped(x, bit):
    count = lax.axis_size("blk")
    return lax.ppermute(x, "blk", [(i, i ^ bit) for i in range(count)])


def after(value, *others):
    return pl.pallas_call(
        lambda *refs: None,
        out_shape=jax.ShapeDtypeStruct(value.shape, value.dtype),
        in_specs=[pl.BlockSpec(memory_space=pl.ANY)] * (1 + len(others)),
        out_specs=pl.BlockSpec(memory_space=pl.ANY),
        input_output_aliases={0: 0},
    )(value, *others)


def unit_rows(values):
    wide = values.astype(jnp.float32)
    inverse = lax.rsqrt(jnp.sum(wide * wide, axis=1, keepdims=True) + 1e-06)
    return (wide * inverse, inverse)


def lane_sums(values):
    rows = jnp.sum(values.reshape(values.shape[0] // 8, 8, values.shape[1]), axis=0)
    total = rows[:, :128]
    for start in range(128, values.shape[1], 128):
        total = total + rows[:, start : start + 128]
    return total


def own_kernel(value, unit, inverse, *pieces):
    scaled, inv = unit_rows(value[...])
    unit[...] = scaled
    inverse[...] = jnp.broadcast_to(inv, inverse.shape)
    store_pieces(scaled, pieces)


def other_kernel(value, *pieces):
    store_pieces(unit_rows(value[...])[0], pieces)


def store_pieces(values, pieces):
    size = values.shape[0] // len(pieces)
    for place, piece in enumerate(pieces):
        piece[...] = values[place * size : (place + 1) * size].astype(jnp.bfloat16)


def unit_call(value, count, own):
    rows, width = value.shape
    outs = [jax.ShapeDtypeStruct((rows // count, width), jnp.bfloat16)] * count
    if own:
        wide = jax.ShapeDtypeStruct((rows, width), jnp.float32)
        outs = [wide, jax.ShapeDtypeStruct((rows, 128), jnp.float32)] + outs
    return pl.pallas_call(
        own_kernel if own else other_kernel,
        out_shape=outs,
        cost_estimate=pl.CostEstimate(
            flops=4 * rows * width, bytes_accessed=4 * rows * width, transcendentals=rows
        ),
    )(value)


def gathered(value, bits, count):
    raw = [swapped(value, bit) for bit in bits]
    unit, inverse, *own = unit_call(value, count, True)
    blocks = {0: own}
    for place in range(len(bits)):
        blocks[1 << place] = unit_call(raw[place], count, False)
    for offset in range(1 << len(bits)):
        if offset not in blocks:
            high = 1 << (offset.bit_length() - 1)
            low = offset & -offset
            lasts = [high] + [low] * (count - 1)
            blocks[offset] = [
                swapped(blocks[offset ^ last][place], bits[last.bit_length() - 1])
                for place, last in enumerate(lasts)
            ]
    return unit, inverse, [blocks[offset] for offset in range(1 << len(bits))]


def tile_kernel(img_places, txt_places, rows, *refs):
    n_img, n_txt = len(img_places), len(txt_places)
    taken = 0
    sources = []
    for places in (img_places, txt_places):
        pieces = sum(places)
        sources.append(refs[taken : taken + pieces])
        taken += pieces
    log_temp, bias = refs[taken : taken + 2]
    img_parts = refs[taken + 2 : taken + 2 + n_img]
    txt_parts = refs[taken + 2 + n_img : taken + 2 + n_img + n_txt]
    sums, img_b, txt_b, grad_b = refs[taken + 2 + n_img + n_txt :]
    for group, held in zip(sources, (img_b, txt_b)):
        start = 0
        for piece in group:
            end = start + piece.shape[0]
            held[start:end] = piece[...]
            start = end
    temp = jnp.exp(log_temp[...])
    shift_b = bias[...]
    sum_g = jnp.zeros((8, 128), jnp.float32)
    sum_gl = jnp.zeros((8, 128), jnp.float32)
    step = 2 * rows
    for start in range(0, n_img * rows, step):
        panel = img_b[start : start + step]
        cosine = lax.dot_general(
            panel, txt_b[...], (((1,), (1,)), ((), ())), preferred_element_type=jnp.float32
        )
        scaled = temp * cosine
        logits = scaled + shift_b
        if start == 0:
            at_row = lax.broadcasted_iota(jnp.int32, logits.shape, 0)
            at_col = lax.broadcasted_iota(jnp.int32, logits.shape, 1)
            own = jnp.logical_and(at_row == at_col, at_row < rows)
            sign = jnp.where(own, 1.0, -1.0)
            grads = -sign * jax.nn.sigmoid(-sign * logits)
        else:
            grads = jax.nn.sigmoid(logits)
        sum_g = sum_g + lane_sums(grads)
        sum_gl = sum_gl + lane_sums(grads * scaled)
        grads_b = grads.astype(jnp.bfloat16)
        grad_b[start : start + step] = grads_b
        part = jnp.dot(grads_b, txt_b[...], preferred_element_type=jnp.float32)
        for at in range(start // rows, (start + step) // rows):
            out = img_parts[at]
            out[...] = part[at * rows - start : (at + 1) * rows - start].astype(out.dtype)
    sums[0:8] = sum_g
    sums[8:16] = sum_gl
    for start in range(0, n_txt * rows, step):
        part = lax.dot_general(
            grad_b[:, start : start + step],
            img_b[...],
            (((0,), (0,)), ((), ())),
            preferred_element_type=jnp.float32,
        )
        for at in range(start // rows, (start + step) // rows):
            out = txt_parts[at]
            out[...] = part[at * rows - start : (at + 1) * rows - start].astype(out.dtype)


def tile_call(imgs, txts, log_temp, bias):
    rows = sum(piece.shape[0] for piece in imgs[0])
    width = imgs[0][0].shape[1]
    n_img, n_txt = len(imgs), len(txts)
    flat = [piece for block in imgs + txts for piece in block]
    pairs = n_img * n_txt * rows * rows

    def outs(count):
        kinds = [jnp.float32] * (count // 2) + [jnp.bfloat16] * (count // 2)
        return [jax.ShapeDtypeStruct((rows, width), kind) for kind in kinds]

    results = pl.pallas_call(
        functools.partial(
            tile_kernel, [len(block) for block in imgs], [len(block) for block in txts], rows
        ),
        out_shape=outs(n_img) + outs(n_txt) + [jax.ShapeDtypeStruct((16, 128), jnp.float32)],
        in_specs=[pl.BlockSpec(memory_space=pltpu.VMEM)] * (len(flat) + 2),
        out_specs=[pl.BlockSpec(memory_space=pltpu.VMEM)] * (n_img + n_txt + 1),
        scratch_shapes=[
            pltpu.VMEM((n_img * rows, width), jnp.bfloat16),
            pltpu.VMEM((n_txt * rows, width), jnp.bfloat16),
            pltpu.VMEM((n_img * rows, n_txt * rows), jnp.bfloat16),
        ],
        compiler_params=pltpu.CompilerParams(vmem_limit_bytes=VMEM_BYTES),
        cost_estimate=pl.CostEstimate(
            flops=6 * pairs * width, bytes_accessed=0, transcendentals=2 * pairs
        ),
    )(*flat, log_temp, bias)
    return results[:n_img], results[n_img:-1], results[-1]


def finish_kernel(unit, inverse, log_temp, keep, *refs):
    total = keep[...]
    for recv in refs[:-1]:
        total = total + recv[...].astype(jnp.float32)
    grad = jnp.exp(log_temp[...]) * total
    along = jnp.sum(unit[...] * grad, axis=1, keepdims=True)
    refs[-1][...] = ((grad - unit[...] * along) * inverse[:, :1]).astype(jnp.bfloat16)


def finish_call(unit, inverse, log_temp, keep, recvs):
    return pl.pallas_call(
        finish_kernel,
        out_shape=jax.ShapeDtypeStruct(keep.shape, jnp.bfloat16),
        compiler_params=pltpu.CompilerParams(vmem_limit_bytes=VMEM_BYTES),
    )(unit, inverse, log_temp, keep, *recvs)


def add_kernel(keep, recv, *refs):
    refs[-1][...] = (keep[...] + recv[...].astype(jnp.float32)).astype(refs[-1].dtype)


def add_call(keep, recv, dtype, others):
    rest = [pl.BlockSpec(memory_space=pl.ANY)] * len(others)
    return pl.pallas_call(
        add_kernel,
        out_shape=jax.ShapeDtypeStruct(keep.shape, dtype),
        in_specs=[pl.BlockSpec(memory_space=pltpu.VMEM)] * 2 + rest,
        out_specs=pl.BlockSpec(memory_space=pltpu.VMEM),
    )(keep, recv, *others)


def returned(parts, bits, others):
    parts = dict(enumerate(parts))
    recvs = []
    for place in reversed(range(len(bits))):
        arrived = {}
        for offset in range(1, 1 << place):
            send = parts.pop(offset | 1 << place).astype(jnp.bfloat16)
            arrived[offset] = swapped(send, bits[place])
        for offset, recv in arrived.items():
            dtype = jnp.float32 if offset < 1 << place - 1 else jnp.bfloat16
            parts[offset] = add_call(parts[offset], recv, dtype, others)
        send = parts.pop(1 << place).astype(jnp.bfloat16)
        if arrived:
            send = after(send, *[parts[offset] for offset in arrived])
            others = [parts[max(arrived)]]
        recvs.append(swapped(send, bits[place]))
    return parts[0], recvs, others


def shards(image_embeds, text_embeds, log_temp, bias):
    rows, width = image_embeds.shape
    count = lax.axis_size("blk")
    depth = count.bit_length() - 1
    all_bits = [1 << place for place in range(depth)]
    split = 1 + depth // 2
    img_bits = all_bits[1:split][::-1]
    txt_bits = (all_bits[:1] + all_bits[split:])[::-1]
    temp_in = log_temp.reshape(1, 1)
    unit_txt, inv_txt, txts = gathered(text_embeds, txt_bits, 1)
    unit_img, inv_img, imgs = gathered(image_embeds, img_bits, 2)
    img_parts, txt_parts, sums = tile_call(imgs, txts, temp_in, bias.reshape(1, 1))
    txt_keep, txt_recvs, others = returned(txt_parts, txt_bits, [])
    img_keep, img_recvs, others = returned(img_parts, img_bits, others)
    for bit in all_bits:
        sums = sums + swapped(sums, bit)
    grad_text = finish_call(unit_txt, inv_txt, temp_in, txt_keep, txt_recvs)
    grad_image = finish_call(unit_img, inv_img, temp_in, img_keep, img_recvs)
    pairs = float(rows * count) * float(rows * count)
    grad_bias = jnp.reshape(jnp.sum(sums[:8]) / pairs, (1,))
    grad_temp = jnp.reshape(jnp.sum(sums[8:]) / pairs, (1,))
    return (grad_image, grad_text, grad_temp, grad_bias)


def solution(mesh):
    in_specs = (P(("groups", "blk"), None), P(("groups", "blk"), None), P(), P())
    out_specs = (P(("groups", "blk"), None), P(("groups", "blk"), None), P("groups"), P("groups"))
    return jax.shard_map(shards, mesh=mesh, in_specs=in_specs, out_specs=out_specs, check_vma=False)
```

```python
import functools

import jax
import jax.numpy as jnp
from jax import lax
from jax.experimental import pallas as pl
from jax.experimental.pallas import tpu as pltpu
from jax.sharding import PartitionSpec as P

TILE_VMEM = 32 * 1024 * 1024
SMALL_VMEM = 4 * 1024 * 1024
FINISH_COST = 100
LANDED_COST = 100_000_000_000
VMEM = pl.BlockSpec(memory_space=pltpu.VMEM)
ANY = pl.BlockSpec(memory_space=pl.ANY)


def swapped(x, bit):
    count = lax.axis_size("blk")
    return lax.ppermute(x, "blk", [(i, i ^ bit) for i in range(count)])


def after(value, *others, cost=0):
    return pl.pallas_call(
        lambda *refs: None,
        out_shape=jax.ShapeDtypeStruct(value.shape, value.dtype),
        in_specs=[ANY] * (1 + len(others)),
        out_specs=ANY,
        input_output_aliases={0: 0},
        cost_estimate=pl.CostEstimate(flops=cost, bytes_accessed=0, transcendentals=0),
        compiler_params=pltpu.CompilerParams(vmem_limit_bytes=SMALL_VMEM),
    )(value, *others)


def unit_rows(values):
    wide = values.astype(jnp.float32)
    inverse = lax.rsqrt(jnp.sum(wide * wide, axis=1, keepdims=True) + 1e-06)
    return (wide * inverse, inverse)


def lane_sums(values):
    rows = jnp.sum(values.reshape(values.shape[0] // 8, 8, values.shape[1]), axis=0)
    total = rows[:, :128]
    for start in range(128, values.shape[1], 128):
        total = total + rows[:, start : start + 128]
    return total


def own_kernel(value, *refs):
    unit, inverse = refs[-2:]
    scaled, inv = unit_rows(value[...])
    unit[...] = scaled
    inverse[...] = jnp.broadcast_to(inv, inverse.shape)


def piece_kernel(count, value, *refs):
    unit = unit_rows(value[...])[0].astype(jnp.bfloat16)
    size = value.shape[0] // count
    for place, piece in enumerate(refs[-count:]):
        piece[...] = unit[place * size : (place + 1) * size]


def unit_call(kernel, value, outs, others):
    return pl.pallas_call(
        kernel,
        out_shape=outs,
        in_specs=[VMEM] + [ANY] * len(others),
        out_specs=[VMEM] * len(outs),
        compiler_params=pltpu.CompilerParams(vmem_limit_bytes=SMALL_VMEM),
        cost_estimate=pl.CostEstimate(
            flops=4 * value.size, bytes_accessed=4 * value.size, transcendentals=value.shape[0]
        ),
    )(value, *others)


def unit_pieces(value, count, others):
    rows, width = value.shape
    outs = [jax.ShapeDtypeStruct((rows // count, width), jnp.bfloat16)] * count
    return unit_call(functools.partial(piece_kernel, count), value, outs, others)


def unit_wide(value, others):
    wide = jax.ShapeDtypeStruct(value.shape, jnp.float32)
    inverse = jax.ShapeDtypeStruct((value.shape[0], 128), jnp.float32)
    return unit_call(own_kernel, value, [wide, inverse], others)


def piece_of(block, place, count):
    if len(block) == count:
        return block[place]
    size = block[0].shape[0] // count
    return block[0][place * size : (place + 1) * size]


def forwarded(blocks, bits, count):
    for offset in range(1 << len(bits)):
        if offset not in blocks:
            high = 1 << (offset.bit_length() - 1)
            low = offset & -offset
            lasts = [high] + [low] * (count - 1)
            blocks[offset] = [
                swapped(piece_of(blocks[offset ^ last], place, count), bits[last.bit_length() - 1])
                for place, last in enumerate(lasts)
            ]
    return [blocks[offset] for offset in range(1 << len(bits))]


def gathered(image, text, img_bits, txt_bits):
    img_raw = [swapped(image, bit) for bit in img_bits]
    txt_raw = swapped(text, txt_bits[0])
    imgs, txts = {}, {}
    others = []
    for place in reversed(range(1, len(img_bits))):
        imgs[1 << place] = others = unit_pieces(img_raw[place], 2, others[:1])
    txts[0] = unit_pieces(text, 1, others[:1])
    imgs[0] = unit_pieces(image, 1, txts[0])
    for place in range(1, len(txt_bits)):
        txts[1 << place] = [swapped(txts[0][0], txt_bits[place])]
    imgs[1] = unit_pieces(img_raw[0], 2, imgs[0])
    txts[1] = unit_pieces(txt_raw, 1, imgs[1][:1])
    imgs = forwarded(imgs, img_bits, 2)
    txts = forwarded(txts, txt_bits, 1)
    landed = after(imgs[-1][0], *imgs[-1][1:], cost=LANDED_COST)
    imgs[-1][0] = landed
    txts[-1][0] = after(txts[-1][0], landed)
    return imgs, txts


def tile_kernel(img_places, txt_places, rows, *refs):
    n_img, n_txt = len(img_places), len(txt_places)
    taken = 0
    sources = []
    for places in (img_places, txt_places):
        pieces = sum(places)
        sources.append(refs[taken : taken + pieces])
        taken += pieces
    log_temp, bias = refs[taken : taken + 2]
    img_parts = refs[taken + 2 : taken + 2 + n_img]
    txt_parts = refs[taken + 2 + n_img : taken + 2 + n_img + n_txt]
    sums, img_b, txt_b, grad_b = refs[taken + 2 + n_img + n_txt :]
    for group, held in zip(sources, (img_b, txt_b)):
        start = 0
        for piece in group:
            end = start + piece.shape[0]
            held[start:end] = piece[...]
            start = end
    temp = jnp.exp(log_temp[...])
    shift_b = bias[...]
    sum_g = jnp.zeros((8, 128), jnp.float32)
    sum_gl = jnp.zeros((8, 128), jnp.float32)
    step = 2 * rows
    for start in range(0, n_img * rows, step):
        panel = img_b[start : start + step]
        cosine = lax.dot_general(
            panel, txt_b[...], (((1,), (1,)), ((), ())), preferred_element_type=jnp.float32
        )
        scaled = temp * cosine
        logits = scaled + shift_b
        if start == 0:
            at_row = lax.broadcasted_iota(jnp.int32, logits.shape, 0)
            at_col = lax.broadcasted_iota(jnp.int32, logits.shape, 1)
            own = jnp.logical_and(at_row == at_col, at_row < rows)
            sign = jnp.where(own, 1.0, -1.0)
            grads = -sign * jax.nn.sigmoid(-sign * logits)
        else:
            grads = jax.nn.sigmoid(logits)
        sum_g = sum_g + lane_sums(grads)
        sum_gl = sum_gl + lane_sums(grads * scaled)
        grads_b = grads.astype(jnp.bfloat16)
        grad_b[start : start + step] = grads_b
        part = jnp.dot(grads_b, txt_b[...], preferred_element_type=jnp.float32)
        for at in range(start // rows, (start + step) // rows):
            out = img_parts[at]
            out[...] = part[at * rows - start : (at + 1) * rows - start].astype(out.dtype)
    sums[0:8] = sum_g
    sums[8:16] = sum_gl
    for start in range(0, n_txt * rows, step):
        part = lax.dot_general(
            grad_b[:, start : start + step],
            img_b[...],
            (((0,), (0,)), ((), ())),
            preferred_element_type=jnp.float32,
        )
        for at in range(start // rows, (start + step) // rows):
            out = txt_parts[at]
            out[...] = part[at * rows - start : (at + 1) * rows - start].astype(out.dtype)


def tile_call(imgs, txts, log_temp, bias):
    rows = sum(piece.shape[0] for piece in imgs[0])
    width = imgs[0][0].shape[1]
    n_img, n_txt = len(imgs), len(txts)
    flat = [piece for block in imgs + txts for piece in block]
    pairs = n_img * n_txt * rows * rows

    def outs(count):
        kinds = [jnp.float32] * (count // 2) + [jnp.bfloat16] * (count // 2)
        return [jax.ShapeDtypeStruct((rows, width), kind) for kind in kinds]

    results = pl.pallas_call(
        functools.partial(
            tile_kernel, [len(block) for block in imgs], [len(block) for block in txts], rows
        ),
        out_shape=outs(n_img) + outs(n_txt) + [jax.ShapeDtypeStruct((16, 128), jnp.float32)],
        in_specs=[VMEM] * (len(flat) + 2),
        out_specs=[VMEM] * (n_img + n_txt + 1),
        scratch_shapes=[
            pltpu.VMEM((n_img * rows, width), jnp.bfloat16),
            pltpu.VMEM((n_txt * rows, width), jnp.bfloat16),
            pltpu.VMEM((n_img * rows, n_txt * rows), jnp.bfloat16),
        ],
        compiler_params=pltpu.CompilerParams(vmem_limit_bytes=TILE_VMEM),
        cost_estimate=pl.CostEstimate(
            flops=6 * pairs * width, bytes_accessed=0, transcendentals=2 * pairs
        ),
    )(*flat, log_temp, bias)
    return results[:n_img], results[n_img:-1], results[-1]


def finish_kernel(count, *refs):
    unit, inverse, log_temp, keep = refs[:4]
    total = keep[...]
    for recv in refs[4 : 4 + count]:
        total = total + recv[...].astype(jnp.float32)
    grad = jnp.exp(log_temp[...]) * total
    along = jnp.sum(unit[...] * grad, axis=1, keepdims=True)
    out, token = refs[-2:]
    out[...] = ((grad - unit[...] * along) * inverse[:, :1]).astype(jnp.bfloat16)
    token[...] = jnp.zeros(token.shape, jnp.float32)


def finish_call(unit, inverse, log_temp, keep, recvs, others):
    return pl.pallas_call(
        functools.partial(finish_kernel, len(recvs)),
        out_shape=(
            jax.ShapeDtypeStruct(keep.shape, jnp.bfloat16),
            jax.ShapeDtypeStruct((8, 128), jnp.float32),
        ),
        in_specs=[VMEM] * (4 + len(recvs)) + [ANY] * len(others),
        out_specs=[VMEM] * 2,
        compiler_params=pltpu.CompilerParams(vmem_limit_bytes=SMALL_VMEM),
        cost_estimate=pl.CostEstimate(
            flops=FINISH_COST * keep.size, bytes_accessed=0, transcendentals=0
        ),
    )(unit, inverse, log_temp, keep, *recvs, *others)


def add_kernel(keep, recv, sums, sums_recv, *refs):
    refs[-2][...] = (keep[...] + recv[...].astype(jnp.float32)).astype(refs[-2].dtype)
    refs[-1][...] = sums[...] + sums_recv[...]


def add_call(keep, recv, dtype, sums, bit, others):
    return pl.pallas_call(
        add_kernel,
        out_shape=(
            jax.ShapeDtypeStruct(keep.shape, dtype),
            jax.ShapeDtypeStruct(sums.shape, sums.dtype),
        ),
        in_specs=[VMEM] * 4 + [ANY] * len(others),
        out_specs=[VMEM] * 2,
        compiler_params=pltpu.CompilerParams(vmem_limit_bytes=SMALL_VMEM),
        cost_estimate=pl.CostEstimate(
            flops=keep.size, bytes_accessed=keep.size, transcendentals=0
        ),
    )(keep, recv, sums, swapped(sums, bit), *others)


def returned(parts, bits, sums, sum_bits, wait, others):
    parts = dict(enumerate(parts))
    sum_bits = list(sum_bits)
    recvs = []
    for place in reversed(range(len(bits))):
        arrived = {}
        for offset in range(1, 1 << place):
            send = parts.pop(offset | 1 << place).astype(jnp.bfloat16)
            arrived[offset] = swapped(send, bits[place])
        for offset, recv in arrived.items():
            dtype = jnp.float32 if offset < 1 << place - 1 else jnp.bfloat16
            if sum_bits:
                parts[offset], sums = add_call(
                    parts[offset], recv, dtype, sums, sum_bits.pop(0), others
                )
            else:
                parts[offset] = (parts[offset] + recv.astype(jnp.float32)).astype(dtype)
        send = parts.pop(1 << place).astype(jnp.bfloat16)
        if arrived:
            others = [parts[max(arrived)]]
            if wait:
                send = after(send, *[parts[offset] for offset in arrived])
        recvs.append(swapped(send, bits[place]))
    return parts[0], recvs, sums, sum_bits, others


def shards(image_embeds, text_embeds, log_temp, bias):
    rows, width = image_embeds.shape
    count = lax.axis_size("blk")
    depth = count.bit_length() - 1
    all_bits = [1 << place for place in range(depth)]
    split = 1 + depth // 2
    img_bits = all_bits[1:split][::-1]
    txt_bits = (all_bits[:1] + all_bits[split:])[::-1]
    temp_in = log_temp.reshape(1, 1)
    imgs, txts = gathered(image_embeds, text_embeds, img_bits, txt_bits)
    img_parts, txt_parts, sums = tile_call(imgs, txts, temp_in, bias.reshape(1, 1))
    unit_img, inv_img = unit_wide(image_embeds, [sums])
    unit_txt, inv_txt = unit_wide(text_embeds, [sums])
    txt_keep, txt_recvs, sums, left, others = returned(txt_parts, txt_bits, sums, all_bits, False, [])
    img_keep, img_recvs, sums, left, others = returned(img_parts, img_bits, sums, left, True, others)
    for bit in left:
        sums = sums + swapped(sums, bit)
    grad_text, done = finish_call(unit_txt, inv_txt, temp_in, txt_keep, txt_recvs, [])
    grad_image, done = finish_call(unit_img, inv_img, temp_in, img_keep, img_recvs, [done])
    pairs = float(rows * count) * float(rows * count)
    grad_bias = jnp.reshape(jnp.sum(sums[:8]) / pairs, (1,))
    grad_temp = jnp.reshape(jnp.sum(sums[8:]) / pairs, (1,))
    return (grad_image, grad_text, grad_temp, grad_bias)


def solution(mesh):
    in_specs = (P(("groups", "blk"), None), P(("groups", "blk"), None), P(), P())
    out_specs = (P(("groups", "blk"), None), P(("groups", "blk"), None), P("groups"), P("groups"))
    return jax.shard_map(shards, mesh=mesh, in_specs=in_specs, out_specs=out_specs, check_vma=False)
```

```python
import functools

import jax
import jax.numpy as jnp
from jax import lax
from jax.experimental import pallas as pl
from jax.experimental.pallas import tpu as pltpu
from jax.sharding import PartitionSpec as P

TILE_VMEM = 32 * 1024 * 1024
SMALL_VMEM = 4 * 1024 * 1024
GATHER_COST = 4_000_000_000
RETURN_COST = 2_000_000_000
VMEM = pl.BlockSpec(memory_space=pltpu.VMEM)
ANY = pl.BlockSpec(memory_space=pl.ANY)


def swapped(x, bit):
    count = lax.axis_size("blk")
    return lax.ppermute(x, "blk", [(i, i ^ bit) for i in range(count)])


def after(value, *others, cost=0):
    return pl.pallas_call(
        lambda *refs: None,
        out_shape=jax.ShapeDtypeStruct(value.shape, value.dtype),
        in_specs=[ANY] * (1 + len(others)),
        out_specs=ANY,
        input_output_aliases={0: 0},
        cost_estimate=pl.CostEstimate(flops=cost, bytes_accessed=0, transcendentals=0),
        compiler_params=pltpu.CompilerParams(vmem_limit_bytes=SMALL_VMEM),
    )(value, *others)


def unit_rows(values):
    wide = values.astype(jnp.float32)
    inverse = lax.rsqrt(jnp.sum(wide * wide, axis=1, keepdims=True) + 1e-06)
    return (wide * inverse, inverse)


def lane_sums(values):
    rows = jnp.sum(values.reshape(values.shape[0] // 8, 8, values.shape[1]), axis=0)
    total = rows[:, :128]
    for start in range(128, values.shape[1], 128):
        total = total + rows[:, start : start + 128]
    return total


def piece_kernel(count, value, *refs):
    unit = unit_rows(value[...])[0].astype(jnp.bfloat16)
    size = value.shape[0] // count
    for place, piece in enumerate(refs[-count:]):
        piece[...] = unit[place * size : (place + 1) * size]


def unit_call(kernel, value, outs, others):
    return pl.pallas_call(
        kernel,
        out_shape=outs,
        in_specs=[VMEM] + [ANY] * len(others),
        out_specs=[VMEM] * len(outs),
        compiler_params=pltpu.CompilerParams(vmem_limit_bytes=SMALL_VMEM),
        cost_estimate=pl.CostEstimate(
            flops=4 * value.size, bytes_accessed=4 * value.size, transcendentals=value.shape[0]
        ),
    )(value, *others)


def unit_pieces(value, count, others):
    rows, width = value.shape
    outs = [jax.ShapeDtypeStruct((rows // count, width), jnp.bfloat16)] * count
    return unit_call(functools.partial(piece_kernel, count), value, outs, others)


def landed(arrays, costs):
    out = []
    for value, cost in zip(arrays, costs):
        out.append(after(value, *out[-1:], cost=cost))
    return out


def gathered(image, text, img_bits, txt_bits):
    half = image.shape[0] // 2
    raw = [swapped(image[:half], img_bits[0]), swapped(image[half:], img_bits[0])]
    img_raw = [swapped(image, bit) for bit in img_bits[1:]]
    txt_raw = swapped(text, txt_bits[0])
    imgs, txts = {}, {}
    imgs[1] = unit_pieces(raw[0], 1, [])
    others = imgs[1]
    for place, value in enumerate(img_raw):
        imgs[2 << place] = others = unit_pieces(value, 2, others[:1])
    txts[0] = unit_pieces(text, 1, others[:1])
    imgs[0] = unit_pieces(image, 1, txts[0])
    for place in range(1, len(txt_bits)):
        txts[1 << place] = [swapped(txts[0][0], txt_bits[place])]
    imgs[1] = imgs[1] + unit_pieces(raw[1], 1, imgs[0])
    txts[1] = unit_pieces(txt_raw, 1, imgs[1][1:])
    for blocks, bits in ((txts, txt_bits), (imgs, img_bits)):
        for offset in range(1 << len(bits)):
            if offset not in blocks:
                place = offset.bit_length() - 1
                blocks[offset] = [swapped(p, bits[place]) for p in blocks[offset ^ 1 << place]]
    imgs = [imgs[offset] for offset in range(1 << len(img_bits))]
    txts = [txts[offset] for offset in range(1 << len(txt_bits))]
    order = landed([txts[-2][0]] + imgs[-1] + [txts[-1][0]], [GATHER_COST] * 3 + [0])
    txts[-2], imgs[-1], txts[-1] = order[:1], order[1:-1], order[-1:]
    return imgs, txts


def store_part(part, start, outs, cuts, rows):
    for at in range(start // rows, (start + part.shape[0]) // rows):
        size = rows // cuts[at]
        for place in range(cuts[at]):
            out = outs[sum(cuts[:at]) + place]
            first = at * rows - start + place * size
            out[...] = part[first : first + size].astype(out.dtype)


def tile_kernel(img_places, txt_places, img_cuts, txt_cuts, rows, *refs):
    n_img, n_txt = len(img_places), len(txt_places)
    taken = 0
    sources = []
    for places in (img_places, txt_places):
        pieces = sum(places)
        sources.append(refs[taken : taken + pieces])
        taken += pieces
    log_temp, bias = refs[taken : taken + 2]
    taken += 2
    img_parts = refs[taken : taken + sum(img_cuts)]
    taken += sum(img_cuts)
    txt_parts = refs[taken : taken + sum(txt_cuts)]
    sums, img_b, txt_b, grad_b = refs[taken + sum(txt_cuts) :]
    for group, held in zip(sources, (img_b, txt_b)):
        start = 0
        for piece in group:
            end = start + piece.shape[0]
            held[start:end] = piece[...]
            start = end
    temp = jnp.exp(log_temp[...])
    shift_b = bias[...]
    sum_g = jnp.zeros((8, 128), jnp.float32)
    sum_gl = jnp.zeros((8, 128), jnp.float32)
    step = 2 * rows
    for start in range(0, n_img * rows, step):
        panel = img_b[start : start + step]
        cosine = lax.dot_general(
            panel, txt_b[...], (((1,), (1,)), ((), ())), preferred_element_type=jnp.float32
        )
        scaled = temp * cosine
        logits = scaled + shift_b
        if start == 0:
            at_row = lax.broadcasted_iota(jnp.int32, logits.shape, 0)
            at_col = lax.broadcasted_iota(jnp.int32, logits.shape, 1)
            own = jnp.logical_and(at_row == at_col, at_row < rows)
            sign = jnp.where(own, 1.0, -1.0)
            grads = -sign * jax.nn.sigmoid(-sign * logits)
        else:
            grads = jax.nn.sigmoid(logits)
        sum_g = sum_g + lane_sums(grads)
        sum_gl = sum_gl + lane_sums(grads * scaled)
        grads_b = grads.astype(jnp.bfloat16)
        grad_b[start : start + step] = grads_b
        part = jnp.dot(grads_b, txt_b[...], preferred_element_type=jnp.float32)
        store_part(temp * part, start, img_parts, img_cuts, rows)
    sums[0:8] = sum_g
    sums[8:16] = sum_gl
    for start in range(0, n_txt * rows, step):
        part = lax.dot_general(
            grad_b[:, start : start + step],
            img_b[...],
            (((0,), (0,)), ((), ())),
            preferred_element_type=jnp.float32,
        )
        store_part(temp * part, start, txt_parts, txt_cuts, rows)


def tile_call(imgs, txts, log_temp, bias):
    rows = sum(piece.shape[0] for piece in imgs[0])
    width = imgs[0][0].shape[1]
    n_img, n_txt = len(imgs), len(txts)
    flat = [piece for block in imgs + txts for piece in block]
    pairs = n_img * n_txt * rows * rows
    img_cuts = [2 if at > n_img // 2 else 1 for at in range(n_img)]
    txt_cuts = [1] * n_txt
    outs = []
    for cuts in (img_cuts, txt_cuts):
        for at, cut in enumerate(cuts):
            kind = jnp.float32 if at < len(cuts) // 2 else jnp.bfloat16
            outs += [jax.ShapeDtypeStruct((rows // cut, width), kind)] * cut
    results = pl.pallas_call(
        functools.partial(
            tile_kernel,
            [len(block) for block in imgs],
            [len(block) for block in txts],
            img_cuts,
            txt_cuts,
            rows,
        ),
        out_shape=outs + [jax.ShapeDtypeStruct((16, 128), jnp.float32)],
        in_specs=[VMEM] * (len(flat) + 2),
        out_specs=[VMEM] * (len(outs) + 1),
        scratch_shapes=[
            pltpu.VMEM((n_img * rows, width), jnp.bfloat16),
            pltpu.VMEM((n_txt * rows, width), jnp.bfloat16),
            pltpu.VMEM((n_img * rows, n_txt * rows), jnp.bfloat16),
        ],
        compiler_params=pltpu.CompilerParams(vmem_limit_bytes=TILE_VMEM),
        cost_estimate=pl.CostEstimate(
            flops=6 * pairs * width, bytes_accessed=0, transcendentals=2 * pairs
        ),
    )(*flat, log_temp, bias)
    results = list(results)
    sums = results.pop()
    parts = [[results.pop(0) for _ in range(cut)] for cut in img_cuts + txt_cuts]
    return parts[:n_img], parts[n_img:], sums


def finish_kernel(recv_counts, pairs, sums, sums_recv, *refs):
    total = sums[...] + sums_recv[...]
    for place in range(2):
        whole = jnp.sum(total[8 * place : 8 * place + 8], axis=0, keepdims=True)
        refs[place - 2][...] = jnp.sum(whole, axis=1, keepdims=True) / pairs
    outs = refs[-len(recv_counts) - 2 : -2]
    for out, count in zip(outs, recv_counts):
        value, keep = refs[:2]
        rows = value.shape[0]
        total = keep[...]
        start = 0
        pieces = []
        for recv in refs[2 : 2 + count]:
            pieces.append(recv[...].astype(jnp.float32))
            start += recv.shape[0]
            if start % rows == 0:
                total = total + jnp.concatenate(pieces, axis=0)
                pieces = []
        refs = refs[2 + count :]
        unit, inverse = unit_rows(value[...])
        along = jnp.sum(unit * total, axis=1, keepdims=True)
        out[...] = ((total - unit * along) * inverse).astype(jnp.bfloat16)


def finish_call(sums, sums_recv, pairs, sides):
    flat = [array for value, keep, recvs in sides for array in [value, keep] + recvs]
    return pl.pallas_call(
        functools.partial(finish_kernel, [len(recvs) for _, _, recvs in sides], pairs),
        out_shape=[jax.ShapeDtypeStruct(value.shape, jnp.bfloat16) for value, _, _ in sides]
        + [jax.ShapeDtypeStruct((1, 1), jnp.float32)] * 2,
        in_specs=[VMEM] * (2 + len(flat)),
        out_specs=[VMEM] * (2 + len(sides)),
        compiler_params=pltpu.CompilerParams(vmem_limit_bytes=2 * SMALL_VMEM),
    )(sums, sums_recv, *flat)


def add_kernel(count, at, *refs):
    keep, recv = refs[:2]
    out = refs[-count]
    kept = keep[...] if keep.shape == recv.shape else keep[pl.ds(at, recv.shape[0])]
    out[...] = (kept + recv[...].astype(jnp.float32)).astype(out.dtype)
    if count == 2:
        refs[-1][...] = refs[2][...] + refs[3][...]


def add_call(keep, recv, at, dtype, sums, bit, others):
    operands = [keep, recv]
    outs = [jax.ShapeDtypeStruct(recv.shape, dtype)]
    if bit is not None:
        operands += [sums, swapped(sums, bit)]
        outs.append(jax.ShapeDtypeStruct(sums.shape, sums.dtype))
    results = pl.pallas_call(
        functools.partial(add_kernel, len(outs), at),
        out_shape=outs,
        in_specs=[VMEM] * len(operands) + [ANY] * len(others),
        out_specs=[VMEM] * len(outs),
        compiler_params=pltpu.CompilerParams(vmem_limit_bytes=SMALL_VMEM),
        cost_estimate=pl.CostEstimate(
            flops=keep.size, bytes_accessed=keep.size, transcendentals=0
        ),
    )(*operands, *others)
    return results if bit is not None else [results[0], sums]


def returned(parts, bits, sums, sum_bits, others):
    parts = dict(enumerate(parts))
    recvs = []
    for place in reversed(range(len(bits))):
        arrived = []
        for offset in range(1, 1 << place):
            for at, piece in enumerate(parts.pop(offset | 1 << place)):
                arrived.append((offset, at, swapped(piece, bits[place])))
        new = {}
        for offset, at, recv in arrived:
            kept = parts[offset]
            kept = kept[at] if len(kept) > 1 else kept[0]
            kind = jnp.float32 if offset < 1 << (place - 1) else jnp.bfloat16
            bit = sum_bits.pop(0) if len(sum_bits) > 1 else None
            piece, sums = add_call(kept, recv, at * recv.shape[0], kind, sums, bit, others)
            others = [piece]
            new.setdefault(offset, []).append(piece)
        sends = parts.pop(1 << place)
        if len(sends) == 1 and len(arrived) > 1:
            sends = [after(sends[0], piece)]
        recvs.append([swapped(piece, bits[place]) for piece in sends])
        parts.update(new)
    return parts[0][0], recvs, sums, others


def shards(image_embeds, text_embeds, log_temp, bias):
    rows, width = image_embeds.shape
    count = lax.axis_size("blk")
    depth = count.bit_length() - 1
    all_bits = [1 << place for place in range(depth)]
    split = 1 + depth // 2
    img_bits = all_bits[1:split][::-1]
    txt_bits = (all_bits[:1] + all_bits[split:])[::-1]
    imgs, txts = gathered(image_embeds, text_embeds, img_bits, txt_bits)
    img_parts, txt_parts, sums = tile_call(imgs, txts, log_temp.reshape(1, 1), bias.reshape(1, 1))
    left = txt_bits[-1:] + txt_bits[:1] + [bit for bit in all_bits if bit not in (txt_bits[0], txt_bits[-1])]
    txt_keep, txt_recvs, sums, others = returned(txt_parts, txt_bits, sums, left, [])
    img_keep, img_recvs, sums, others = returned(img_parts, img_bits, sums, left, others)
    for bit in left[:-1]:
        sums = sums + swapped(sums, bit)
    sums_recv, txt_recvs, img_recvs = landed_sides(swapped(sums, left[-1]), txt_recvs, img_recvs)
    grad_text, grad_image, grad_bias, grad_temp = finish_call(
        sums,
        sums_recv,
        float(rows * count) * float(rows * count),
        [(text_embeds, txt_keep, txt_recvs), (image_embeds, img_keep, img_recvs)],
    )
    return (grad_image, grad_text, grad_temp.reshape(1), grad_bias.reshape(1))


def landed_sides(sums, txt_recvs, img_recvs):
    txts = [piece for recv in txt_recvs[::-1] for piece in recv]
    imgs = [piece for recv in img_recvs[::-1] for piece in recv]
    order = [sums] + txts + imgs[:1] + imgs[2:] + imgs[1:2]
    costs = [0] * (1 + len(txts)) + [RETURN_COST] + [0] * (len(imgs) - 1)
    sums, *order = landed(order, costs)
    txts, imgs = order[: len(txts)], order[len(txts) :]
    imgs = imgs[:1] + imgs[-1:] + imgs[1:-1]
    return sums, txts[::-1], imgs[2:] + imgs[:2]


def solution(mesh):
    in_specs = (P(("groups", "blk"), None), P(("groups", "blk"), None), P(), P())
    out_specs = (P(("groups", "blk"), None), P(("groups", "blk"), None), P("groups"), P("groups"))
    return jax.shard_map(shards, mesh=mesh, in_specs=in_specs, out_specs=out_specs, check_vma=False)
```

```python
import functools

import jax
import jax.numpy as jnp
from jax import lax
from jax.experimental import pallas as pl
from jax.experimental.pallas import tpu as pltpu
from jax.sharding import PartitionSpec as P

TILE_VMEM = 32 * 1024 * 1024
SMALL_VMEM = 4 * 1024 * 1024
GATHER_COST = 4_000_000_000
RETURN_COST = 600_000_000
VMEM = pl.BlockSpec(memory_space=pltpu.VMEM)
ANY = pl.BlockSpec(memory_space=pl.ANY)


def swapped(x, bit):
    count = lax.axis_size("blk")
    return lax.ppermute(x, "blk", [(i, i ^ bit) for i in range(count)])


def held(values, others, cost=0):
    count = len(values)
    results = pl.pallas_call(
        lambda *refs: None,
        out_shape=[jax.ShapeDtypeStruct(value.shape, value.dtype) for value in values],
        in_specs=[ANY] * (count + len(others)),
        out_specs=[ANY] * count,
        input_output_aliases={place: place for place in range(count)},
        cost_estimate=pl.CostEstimate(flops=cost, bytes_accessed=0, transcendentals=0),
        compiler_params=pltpu.CompilerParams(vmem_limit_bytes=SMALL_VMEM),
    )(*values, *others)
    return list(results)


def unit_rows(values):
    wide = values.astype(jnp.float32)
    inverse = lax.rsqrt(jnp.sum(wide * wide, axis=1, keepdims=True) + 1e-06)
    return (wide * inverse, inverse)


def lane_sums(values):
    rows = jnp.sum(values.reshape(values.shape[0] // 8, 8, values.shape[1]), axis=0)
    total = rows[:, :128]
    for start in range(128, values.shape[1], 128):
        total = total + rows[:, start : start + 128]
    return total


def piece_kernel(count, value, *refs):
    unit = unit_rows(value[...])[0].astype(jnp.bfloat16)
    size = value.shape[0] // count
    for place, piece in enumerate(refs[-count:]):
        piece[...] = unit[place * size : (place + 1) * size]


def unit_call(kernel, value, outs, others):
    return pl.pallas_call(
        kernel,
        out_shape=outs,
        in_specs=[VMEM] + [ANY] * len(others),
        out_specs=[VMEM] * len(outs),
        compiler_params=pltpu.CompilerParams(vmem_limit_bytes=SMALL_VMEM),
        cost_estimate=pl.CostEstimate(
            flops=4 * value.size, bytes_accessed=4 * value.size, transcendentals=value.shape[0]
        ),
    )(value, *others)


def unit_pieces(value, count, others):
    rows, width = value.shape
    outs = [jax.ShapeDtypeStruct((rows // count, width), jnp.bfloat16)] * count
    return unit_call(functools.partial(piece_kernel, count), value, outs, others)


def landed(arrays, costs):
    out = []
    for value, cost in zip(arrays, costs):
        out += held([value], out[-1:], cost)
    return out


def gathered(image, text, img_bits, txt_bits):
    half = image.shape[0] // 2
    raw = [swapped(image[:half], img_bits[0]), swapped(image[half:], img_bits[0])]
    img_raw = [swapped(image, bit) for bit in img_bits[1:]]
    txt_raw = [swapped(text, bit) for bit in txt_bits]
    imgs, txts = {}, {}
    imgs[1] = unit_pieces(raw[0], 1, [])
    others = imgs[1]
    for place, value in enumerate(img_raw):
        imgs[2 << place] = others = unit_pieces(value, 2, others[:1])
    txts[0] = unit_pieces(text, 1, others[:1])
    imgs[0] = unit_pieces(image, 1, txts[0])
    others = imgs[0]
    for place in range(1, len(txt_bits)):
        txts[1 << place] = others = unit_pieces(txt_raw[place], 1, others)
    imgs[1] = imgs[1] + unit_pieces(raw[1], 1, others)
    txts[1] = unit_pieces(txt_raw[0], 1, imgs[1][1:])
    for blocks, bits in ((txts, txt_bits), (imgs, img_bits)):
        for offset in range(1 << len(bits)):
            if offset not in blocks:
                place = offset.bit_length() - 1
                blocks[offset] = [swapped(p, bits[place]) for p in blocks[offset ^ 1 << place]]
    imgs = [imgs[offset] for offset in range(1 << len(img_bits))]
    txts = [txts[offset] for offset in range(1 << len(txt_bits))]
    order = landed(imgs[-1] + txts[-1], [GATHER_COST] * len(imgs[-1]) + [0])
    imgs[-1], txts[-1] = order[:-1], order[-1:]
    return imgs, txts


def store_part(part, start, outs, cuts, rows):
    for at in range(start // rows, (start + part.shape[0]) // rows):
        size = rows // cuts[at]
        for place in range(cuts[at]):
            out = outs[sum(cuts[:at]) + place]
            first = at * rows - start + place * size
            out[...] = part[first : first + size].astype(out.dtype)


def tile_kernel(img_places, txt_places, img_cuts, txt_cuts, rows, *refs):
    n_img, n_txt = len(img_places), len(txt_places)
    taken = 0
    sources = []
    for places in (img_places, txt_places):
        pieces = sum(places)
        sources.append(refs[taken : taken + pieces])
        taken += pieces
    log_temp, bias = refs[taken : taken + 2]
    taken += 2
    img_parts = refs[taken : taken + sum(img_cuts)]
    taken += sum(img_cuts)
    txt_parts = refs[taken : taken + sum(txt_cuts)]
    sums, img_b, txt_b, grad_b = refs[taken + sum(txt_cuts) :]
    for group, held in zip(sources, (img_b, txt_b)):
        start = 0
        for piece in group:
            end = start + piece.shape[0]
            held[start:end] = piece[...]
            start = end
    temp = jnp.exp(log_temp[...])
    shift_b = bias[...]
    sum_g = jnp.zeros((8, 128), jnp.float32)
    sum_gl = jnp.zeros((8, 128), jnp.float32)
    step = 2 * rows
    for start in range(0, n_img * rows, step):
        panel = img_b[start : start + step]
        cosine = lax.dot_general(
            panel, txt_b[...], (((1,), (1,)), ((), ())), preferred_element_type=jnp.float32
        )
        scaled = temp * cosine
        logits = scaled + shift_b
        if start == 0:
            at_row = lax.broadcasted_iota(jnp.int32, logits.shape, 0)
            at_col = lax.broadcasted_iota(jnp.int32, logits.shape, 1)
            own = jnp.logical_and(at_row == at_col, at_row < rows)
            sign = jnp.where(own, 1.0, -1.0)
            grads = -sign * jax.nn.sigmoid(-sign * logits)
        else:
            grads = jax.nn.sigmoid(logits)
        sum_g = sum_g + lane_sums(grads)
        sum_gl = sum_gl + lane_sums(grads * scaled)
        grads_b = grads.astype(jnp.bfloat16)
        grad_b[start : start + step] = grads_b
        part = jnp.dot(grads_b, txt_b[...], preferred_element_type=jnp.float32)
        store_part(temp * part, start, img_parts, img_cuts, rows)
    sums[0:8] = sum_g
    sums[8:16] = sum_gl
    for start in range(0, n_txt * rows, step):
        part = lax.dot_general(
            grad_b[:, start : start + step],
            img_b[...],
            (((0,), (0,)), ((), ())),
            preferred_element_type=jnp.float32,
        )
        store_part(temp * part, start, txt_parts, txt_cuts, rows)


def tile_call(imgs, txts, log_temp, bias):
    rows = sum(piece.shape[0] for piece in imgs[0])
    width = imgs[0][0].shape[1]
    n_img, n_txt = len(imgs), len(txts)
    flat = [piece for block in imgs + txts for piece in block]
    pairs = n_img * n_txt * rows * rows
    img_cuts = [2 if at >= n_img // 2 else 1 for at in range(n_img)]
    txt_cuts = [1] * n_txt
    outs = []
    for cuts in (img_cuts, txt_cuts):
        for at, cut in enumerate(cuts):
            kind = jnp.float32 if at < len(cuts) // 2 else jnp.bfloat16
            outs += [jax.ShapeDtypeStruct((rows // cut, width), kind)] * cut
    results = pl.pallas_call(
        functools.partial(
            tile_kernel,
            [len(block) for block in imgs],
            [len(block) for block in txts],
            img_cuts,
            txt_cuts,
            rows,
        ),
        out_shape=outs + [jax.ShapeDtypeStruct((16, 128), jnp.float32)],
        in_specs=[VMEM] * (len(flat) + 2),
        out_specs=[VMEM] * (len(outs) + 1),
        scratch_shapes=[
            pltpu.VMEM((n_img * rows, width), jnp.bfloat16),
            pltpu.VMEM((n_txt * rows, width), jnp.bfloat16),
            pltpu.VMEM((n_img * rows, n_txt * rows), jnp.bfloat16),
        ],
        compiler_params=pltpu.CompilerParams(vmem_limit_bytes=TILE_VMEM),
        cost_estimate=pl.CostEstimate(
            flops=6 * pairs * width, bytes_accessed=0, transcendentals=2 * pairs
        ),
    )(*flat, log_temp, bias)
    results = list(results)
    sums = results.pop()
    parts = [[results.pop(0) for _ in range(cut)] for cut in img_cuts + txt_cuts]
    return parts[:n_img], parts[n_img:], sums


def finish_kernel(recv_counts, pairs, sums, sums_recv, *refs):
    total = sums[...] + sums_recv[...]
    for place in range(2):
        whole = jnp.sum(total[8 * place : 8 * place + 8], axis=0, keepdims=True)
        refs[place - 2][...] = jnp.sum(whole, axis=1, keepdims=True) / pairs
    outs = refs[-len(recv_counts) - 2 : -2]
    for out, count in zip(outs, recv_counts):
        value, keep = refs[:2]
        rows = value.shape[0]
        total = keep[...]
        start = 0
        pieces = []
        for recv in refs[2 : 2 + count]:
            pieces.append(recv[...].astype(jnp.float32))
            start += recv.shape[0]
            if start % rows == 0:
                total = total + jnp.concatenate(pieces, axis=0)
                pieces = []
        refs = refs[2 + count :]
        unit, inverse = unit_rows(value[...])
        along = jnp.sum(unit * total, axis=1, keepdims=True)
        out[...] = ((total - unit * along) * inverse).astype(jnp.bfloat16)


def finish_call(sums, sums_recv, pairs, sides):
    flat = [array for value, keep, recvs in sides for array in [value, keep] + recvs]
    return pl.pallas_call(
        functools.partial(finish_kernel, [len(recvs) for _, _, recvs in sides], pairs),
        out_shape=[jax.ShapeDtypeStruct(value.shape, jnp.bfloat16) for value, _, _ in sides]
        + [jax.ShapeDtypeStruct((1, 1), jnp.float32)] * 2,
        in_specs=[VMEM] * (2 + len(flat)),
        out_specs=[VMEM] * (2 + len(sides)),
        compiler_params=pltpu.CompilerParams(vmem_limit_bytes=2 * SMALL_VMEM),
    )(sums, sums_recv, *flat)


def add_kernel(count, at, *refs):
    keep, recv = refs[:2]
    out = refs[-count]
    kept = keep[...] if keep.shape == recv.shape else keep[pl.ds(at, recv.shape[0])]
    out[...] = (kept + recv[...].astype(jnp.float32)).astype(out.dtype)
    if count == 2:
        refs[-1][...] = refs[2][...] + refs[3][...]


def add_call(keep, recv, at, dtype, sums, bit, others):
    operands = [keep, recv]
    outs = [jax.ShapeDtypeStruct(recv.shape, dtype)]
    if bit is not None:
        operands += [sums, swapped(sums, bit)]
        outs.append(jax.ShapeDtypeStruct(sums.shape, sums.dtype))
    results = pl.pallas_call(
        functools.partial(add_kernel, len(outs), at),
        out_shape=outs,
        in_specs=[VMEM] * len(operands) + [ANY] * len(others),
        out_specs=[VMEM] * len(outs),
        compiler_params=pltpu.CompilerParams(vmem_limit_bytes=SMALL_VMEM),
        cost_estimate=pl.CostEstimate(
            flops=keep.size, bytes_accessed=keep.size, transcendentals=0
        ),
    )(*operands, *others)
    return results if bit is not None else [results[0], sums]


def returned(parts, bits, sums, sum_bits, others):
    parts = dict(enumerate(parts))
    recvs = []
    for place in reversed(range(len(bits))):
        arrived = []
        for offset in range(1, 1 << place):
            for at, piece in enumerate(parts.pop(offset | 1 << place)):
                arrived.append((offset, at, swapped(piece, bits[place])))
        new = {}
        for offset, at, recv in arrived:
            kept = parts[offset]
            kept = kept[at] if len(kept) > 1 else kept[0]
            kind = jnp.float32 if offset < 1 << (place - 1) else jnp.bfloat16
            bit = sum_bits.pop(0) if len(sum_bits) > 1 else None
            piece, sums = add_call(kept, recv, at * recv.shape[0], kind, sums, bit, others)
            others = [piece]
            new.setdefault(offset, []).append(piece)
        sends = parts.pop(1 << place)
        if len(sends) > 1 and arrived:
            sends = held(sends, [piece])
        recvs.append([swapped(piece, bits[place]) for piece in sends])
        parts.update(new)
    return parts[0][0], recvs, sums, others


def shards(image_embeds, text_embeds, log_temp, bias):
    rows, width = image_embeds.shape
    count = lax.axis_size("blk")
    depth = count.bit_length() - 1
    all_bits = [1 << place for place in range(depth)]
    split = 1 + depth // 2
    img_bits = all_bits[1:split][::-1]
    txt_bits = (all_bits[:1] + all_bits[split:])[::-1]
    imgs, txts = gathered(image_embeds, text_embeds, img_bits, txt_bits)
    img_parts, txt_parts, sums = tile_call(imgs, txts, log_temp.reshape(1, 1), bias.reshape(1, 1))
    left = txt_bits[-1:] + img_bits + txt_bits[-2::-1]
    txt_keep, txt_recvs, sums, others = returned(txt_parts, txt_bits, sums, left, [])
    img_keep, img_recvs, sums, others = returned(img_parts, img_bits, sums, left, others)
    for bit in left[:-1]:
        sums = sums + swapped(sums, bit)
    sums_recv, txt_recvs, img_recvs = landed_sides(swapped(sums, left[-1]), txt_recvs, img_recvs)
    grad_text, grad_image, grad_bias, grad_temp = finish_call(
        sums,
        sums_recv,
        float(rows * count) * float(rows * count),
        [(text_embeds, txt_keep, txt_recvs), (image_embeds, img_keep, img_recvs)],
    )
    return (grad_image, grad_text, grad_temp.reshape(1), grad_bias.reshape(1))


def landed_sides(sums, txt_recvs, img_recvs):
    txts = [piece for recv in txt_recvs for piece in recv]
    imgs = [piece for recv in img_recvs for piece in recv]
    at = len(imgs) - len(img_recvs[-1])
    first = held(imgs[at : at + 1] + txts, [], RETURN_COST)
    return sums, first[1:], imgs[:at] + first[:1] + imgs[at + 1 :]


def solution(mesh):
    in_specs = (P(("groups", "blk"), None), P(("groups", "blk"), None), P(), P())
    out_specs = (P(("groups", "blk"), None), P(("groups", "blk"), None), P("groups"), P("groups"))
    return jax.shard_map(shards, mesh=mesh, in_specs=in_specs, out_specs=out_specs, check_vma=False)
```

```python
import functools

import jax
import jax.numpy as jnp
from jax import lax
from jax.experimental import pallas as pl
from jax.experimental.pallas import tpu as pltpu
from jax.sharding import PartitionSpec as P

TILE_VMEM = 32 * 1024 * 1024
SMALL_VMEM = 4 * 1024 * 1024
GATHER_COST = 4_000_000_000
RETURN_COST = 600_000_000
SUMS_COST = 2_000_000_000
VMEM = pl.BlockSpec(memory_space=pltpu.VMEM)
ANY = pl.BlockSpec(memory_space=pl.ANY)


def swapped(x, bit):
    count = lax.axis_size("blk")
    return lax.ppermute(x, "blk", [(i, i ^ bit) for i in range(count)])


def held(values, others, cost=0):
    count = len(values)
    results = pl.pallas_call(
        lambda *refs: None,
        out_shape=[jax.ShapeDtypeStruct(value.shape, value.dtype) for value in values],
        in_specs=[ANY] * (count + len(others)),
        out_specs=[ANY] * count,
        input_output_aliases={place: place for place in range(count)},
        cost_estimate=pl.CostEstimate(flops=cost, bytes_accessed=0, transcendentals=0),
        compiler_params=pltpu.CompilerParams(vmem_limit_bytes=SMALL_VMEM),
    )(*values, *others)
    return list(results)


def unit_rows(values):
    wide = values.astype(jnp.float32)
    inverse = lax.rsqrt(jnp.sum(wide * wide, axis=1, keepdims=True) + 1e-06)
    return (wide * inverse, inverse)


def lane_sums(values):
    rows = jnp.sum(values.reshape(values.shape[0] // 8, 8, values.shape[1]), axis=0)
    total = rows[:, :128]
    for start in range(128, values.shape[1], 128):
        total = total + rows[:, start : start + 128]
    return total


def piece_kernel(count, value, *refs):
    unit = unit_rows(value[...])[0].astype(jnp.bfloat16)
    size = value.shape[0] // count
    for place, piece in enumerate(refs[-count:]):
        piece[...] = unit[place * size : (place + 1) * size]


def unit_call(kernel, value, outs, others):
    return pl.pallas_call(
        kernel,
        out_shape=outs,
        in_specs=[VMEM] + [ANY] * len(others),
        out_specs=[VMEM] * len(outs),
        compiler_params=pltpu.CompilerParams(vmem_limit_bytes=SMALL_VMEM),
        cost_estimate=pl.CostEstimate(
            flops=4 * value.size, bytes_accessed=4 * value.size, transcendentals=value.shape[0]
        ),
    )(value, *others)


def unit_pieces(value, count, others):
    rows, width = value.shape
    outs = [jax.ShapeDtypeStruct((rows // count, width), jnp.bfloat16)] * count
    return unit_call(functools.partial(piece_kernel, count), value, outs, others)


def landed(arrays, costs):
    out = []
    for value, cost in zip(arrays, costs):
        out += held([value], out[-1:], cost)
    return out


def gathered(image, text, img_bits, txt_bits):
    half = image.shape[0] // 2
    raw = [swapped(image[:half], img_bits[0]), swapped(image[half:], img_bits[0])]
    img_raw = [swapped(image, bit) for bit in img_bits[1:]]
    txt_raw = [swapped(text, bit) for bit in txt_bits]
    imgs, txts = {}, {}
    imgs[1] = unit_pieces(raw[0], 1, [])
    others = imgs[1]
    for place, value in enumerate(img_raw):
        imgs[2 << place] = others = unit_pieces(value, 2, others[:1])
    txts[0] = unit_pieces(text, 1, others[:1])
    imgs[0] = unit_pieces(image, 1, txts[0])
    others = imgs[0]
    for place in range(1, len(txt_bits)):
        txts[1 << place] = others = unit_pieces(txt_raw[place], 1, others)
    imgs[1] = imgs[1] + unit_pieces(raw[1], 1, others)
    txts[1] = unit_pieces(txt_raw[0], 1, imgs[1][1:])
    for blocks, bits in ((txts, txt_bits), (imgs, img_bits)):
        for offset in range(1 << len(bits)):
            if offset not in blocks:
                place = offset.bit_length() - 1
                blocks[offset] = [swapped(p, bits[place]) for p in blocks[offset ^ 1 << place]]
    imgs = [imgs[offset] for offset in range(1 << len(img_bits))]
    txts = [txts[offset] for offset in range(1 << len(txt_bits))]
    order = landed(imgs[-1] + txts[-1], [GATHER_COST] * len(imgs[-1]) + [0])
    imgs[-1], txts[-1] = order[:-1], order[-1:]
    return imgs, txts


def store_part(part, start, outs, cuts, rows):
    for at in range(start // rows, (start + part.shape[0]) // rows):
        size = rows // cuts[at]
        for place in range(cuts[at]):
            out = outs[sum(cuts[:at]) + place]
            first = at * rows - start + place * size
            out[...] = part[first : first + size].astype(out.dtype)


def tile_kernel(img_places, txt_places, img_cuts, txt_cuts, rows, *refs):
    n_img, n_txt = len(img_places), len(txt_places)
    taken = 0
    sources = []
    for places in (img_places, txt_places):
        pieces = sum(places)
        sources.append(refs[taken : taken + pieces])
        taken += pieces
    log_temp, bias = refs[taken : taken + 2]
    taken += 2
    img_parts = refs[taken : taken + sum(img_cuts)]
    taken += sum(img_cuts)
    txt_parts = refs[taken : taken + sum(txt_cuts)]
    sums, img_b, txt_b, grad_b = refs[taken + sum(txt_cuts) :]
    for group, held in zip(sources, (img_b, txt_b)):
        start = 0
        for piece in group:
            end = start + piece.shape[0]
            held[start:end] = piece[...]
            start = end
    temp = jnp.exp(log_temp[...])
    shift_b = bias[...]
    sum_g = jnp.zeros((8, 128), jnp.float32)
    sum_gl = jnp.zeros((8, 128), jnp.float32)
    step = 2 * rows
    for start in range(0, n_img * rows, step):
        panel = img_b[start : start + step]
        cosine = lax.dot_general(
            panel, txt_b[...], (((1,), (1,)), ((), ())), preferred_element_type=jnp.float32
        )
        scaled = temp * cosine
        logits = scaled + shift_b
        if start == 0:
            at_row = lax.broadcasted_iota(jnp.int32, logits.shape, 0)
            at_col = lax.broadcasted_iota(jnp.int32, logits.shape, 1)
            own = jnp.logical_and(at_row == at_col, at_row < rows)
            sign = jnp.where(own, 1.0, -1.0)
            grads = -sign * jax.nn.sigmoid(-sign * logits)
        else:
            grads = jax.nn.sigmoid(logits)
        sum_g = sum_g + lane_sums(grads)
        sum_gl = sum_gl + lane_sums(grads * scaled)
        grads_b = grads.astype(jnp.bfloat16)
        grad_b[start : start + step] = grads_b
        part = jnp.dot(grads_b, txt_b[...], preferred_element_type=jnp.float32)
        store_part(temp * part, start, img_parts, img_cuts, rows)
    sums[0:8] = sum_g
    sums[8:16] = sum_gl
    for start in range(0, n_txt * rows, step):
        part = lax.dot_general(
            grad_b[:, start : start + step],
            img_b[...],
            (((0,), (0,)), ((), ())),
            preferred_element_type=jnp.float32,
        )
        store_part(temp * part, start, txt_parts, txt_cuts, rows)


def tile_call(imgs, txts, log_temp, bias):
    rows = sum(piece.shape[0] for piece in imgs[0])
    width = imgs[0][0].shape[1]
    n_img, n_txt = len(imgs), len(txts)
    flat = [piece for block in imgs + txts for piece in block]
    pairs = n_img * n_txt * rows * rows
    img_cuts = [2 if at >= n_img // 2 else 1 for at in range(n_img)]
    txt_cuts = [1] * n_txt
    outs = []
    for cuts in (img_cuts, txt_cuts):
        for at, cut in enumerate(cuts):
            kind = jnp.float32 if at < len(cuts) // 2 else jnp.bfloat16
            outs += [jax.ShapeDtypeStruct((rows // cut, width), kind)] * cut
    results = pl.pallas_call(
        functools.partial(
            tile_kernel,
            [len(block) for block in imgs],
            [len(block) for block in txts],
            img_cuts,
            txt_cuts,
            rows,
        ),
        out_shape=outs + [jax.ShapeDtypeStruct((16, 128), jnp.float32)],
        in_specs=[VMEM] * (len(flat) + 2),
        out_specs=[VMEM] * (len(outs) + 1),
        scratch_shapes=[
            pltpu.VMEM((n_img * rows, width), jnp.bfloat16),
            pltpu.VMEM((n_txt * rows, width), jnp.bfloat16),
            pltpu.VMEM((n_img * rows, n_txt * rows), jnp.bfloat16),
        ],
        compiler_params=pltpu.CompilerParams(vmem_limit_bytes=TILE_VMEM),
        cost_estimate=pl.CostEstimate(
            flops=6 * pairs * width, bytes_accessed=0, transcendentals=2 * pairs
        ),
    )(*flat, log_temp, bias)
    results = list(results)
    sums = results.pop()
    parts = [[results.pop(0) for _ in range(cut)] for cut in img_cuts + txt_cuts]
    return parts[:n_img], parts[n_img:], sums


def total_kernel(pairs, sums, *outs):
    total = jnp.sum(sums[...], axis=0)
    for place, out in enumerate(outs):
        whole = jnp.sum(total[8 * place : 8 * place + 8], axis=0, keepdims=True)
        out[...] = jnp.sum(whole, axis=1, keepdims=True) / pairs


def total_call(sums, pairs):
    return pl.pallas_call(
        functools.partial(total_kernel, pairs),
        out_shape=[jax.ShapeDtypeStruct((1, 1), jnp.float32)] * 2,
        in_specs=[VMEM],
        out_specs=[VMEM] * 2,
        compiler_params=pltpu.CompilerParams(vmem_limit_bytes=SMALL_VMEM),
        cost_estimate=pl.CostEstimate(flops=SUMS_COST, bytes_accessed=0, transcendentals=0),
    )(sums)


def finish_kernel(recv_counts, *refs):
    outs = refs[-len(recv_counts) :]
    for out, count in zip(outs, recv_counts):
        value, keep = refs[:2]
        rows = value.shape[0]
        total = keep[...]
        start = 0
        pieces = []
        for recv in refs[2 : 2 + count]:
            pieces.append(recv[...].astype(jnp.float32))
            start += recv.shape[0]
            if start % rows == 0:
                total = total + jnp.concatenate(pieces, axis=0)
                pieces = []
        refs = refs[2 + count :]
        unit, inverse = unit_rows(value[...])
        along = jnp.sum(unit * total, axis=1, keepdims=True)
        out[...] = ((total - unit * along) * inverse).astype(jnp.bfloat16)


def finish_call(sides):
    flat = [array for value, keep, recvs in sides for array in [value, keep] + recvs]
    return pl.pallas_call(
        functools.partial(finish_kernel, [len(recvs) for _, _, recvs in sides]),
        out_shape=[jax.ShapeDtypeStruct(value.shape, jnp.bfloat16) for value, _, _ in sides],
        in_specs=[VMEM] * len(flat),
        out_specs=[VMEM] * len(sides),
        compiler_params=pltpu.CompilerParams(vmem_limit_bytes=2 * SMALL_VMEM),
    )(*flat)


def add_kernel(at, keep, recv, *refs):
    out = refs[-1]
    kept = keep[...] if keep.shape == recv.shape else keep[pl.ds(at, recv.shape[0])]
    out[...] = (kept + recv[...].astype(jnp.float32)).astype(out.dtype)


def add_call(keep, recv, at, dtype, others):
    return pl.pallas_call(
        functools.partial(add_kernel, at),
        out_shape=jax.ShapeDtypeStruct(recv.shape, dtype),
        in_specs=[VMEM] * 2 + [ANY] * len(others),
        out_specs=VMEM,
        compiler_params=pltpu.CompilerParams(vmem_limit_bytes=SMALL_VMEM),
        cost_estimate=pl.CostEstimate(
            flops=recv.size, bytes_accessed=recv.size, transcendentals=0
        ),
    )(keep, recv, *others)


def returned(parts, bits, others):
    parts = dict(enumerate(parts))
    recvs = []
    for place in reversed(range(len(bits))):
        arrived = []
        for offset in range(1, 1 << place):
            for at, piece in enumerate(parts.pop(offset | 1 << place)):
                arrived.append((offset, at, swapped(piece, bits[place])))
        new = {}
        for offset, at, recv in arrived:
            kept = parts[offset]
            kept = kept[at] if len(kept) > 1 else kept[0]
            kind = jnp.float32 if offset < 1 << (place - 1) else jnp.bfloat16
            piece = add_call(kept, recv, at * recv.shape[0], kind, others)
            others = [piece]
            new.setdefault(offset, []).append(piece)
        sends = parts.pop(1 << place)
        if len(sends) > 1 and arrived:
            sends = held(sends, [piece])
        recvs.append([swapped(piece, bits[place]) for piece in sends])
        parts.update(new)
    return parts[0][0], recvs, others


def shards(image_embeds, text_embeds, log_temp, bias):
    rows, width = image_embeds.shape
    count = lax.axis_size("blk")
    depth = count.bit_length() - 1
    all_bits = [1 << place for place in range(depth)]
    split = 1 + depth // 2
    img_bits = all_bits[1:split][::-1]
    txt_bits = (all_bits[:1] + all_bits[split:])[::-1]
    imgs, txts = gathered(image_embeds, text_embeds, img_bits, txt_bits)
    img_parts, txt_parts, sums = tile_call(imgs, txts, log_temp.reshape(1, 1), bias.reshape(1, 1))
    pairs = float(rows * count) * float(rows * count)
    grad_bias, grad_temp = total_call(lax.all_gather(sums, "blk"), pairs)
    txt_keep, txt_recvs, others = returned(txt_parts, txt_bits, [])
    img_keep, img_recvs, others = returned(img_parts, img_bits, others)
    txt_recvs, img_recvs = landed_sides(txt_recvs, img_recvs, [grad_bias])
    grad_text, grad_image = finish_call(
        [(text_embeds, txt_keep, txt_recvs), (image_embeds, img_keep, img_recvs)]
    )
    return (grad_image, grad_text, grad_temp.reshape(1), grad_bias.reshape(1))


def landed_sides(txt_recvs, img_recvs, others):
    txts = [piece for recv in txt_recvs for piece in recv]
    imgs = [piece for recv in img_recvs for piece in recv]
    at = len(imgs) - len(img_recvs[-1])
    first = held(imgs[at : at + 1] + txts, others, RETURN_COST)
    return first[1:], imgs[:at] + first[:1] + imgs[at + 1 :]


def solution(mesh):
    in_specs = (P(("groups", "blk"), None), P(("groups", "blk"), None), P(), P())
    out_specs = (P(("groups", "blk"), None), P(("groups", "blk"), None), P("groups"), P("groups"))
    return jax.shard_map(shards, mesh=mesh, in_specs=in_specs, out_specs=out_specs, check_vma=False)
```

```python
import functools

import jax
import jax.numpy as jnp
from jax import lax
from jax.experimental import pallas as pl
from jax.experimental.pallas import tpu as pltpu
from jax.sharding import PartitionSpec as P

TILE_VMEM = 32 * 1024 * 1024
SMALL_VMEM = 4 * 1024 * 1024
GATHER_COST = 20_000_000_000
SUMS_COST = 300_000_000
RETURN_COST = 1_500_000_000
VMEM = pl.BlockSpec(memory_space=pltpu.VMEM)
ANY = pl.BlockSpec(memory_space=pl.ANY)


def swapped(x, bit):
    count = lax.axis_size("blk")
    return lax.ppermute(x, "blk", [(i, i ^ bit) for i in range(count)])


def held(values, others, cost=0):
    count = len(values)
    results = pl.pallas_call(
        lambda *refs: None,
        out_shape=[jax.ShapeDtypeStruct(value.shape, value.dtype) for value in values],
        in_specs=[ANY] * (count + len(others)),
        out_specs=[ANY] * count,
        input_output_aliases={place: place for place in range(count)},
        cost_estimate=pl.CostEstimate(flops=cost, bytes_accessed=0, transcendentals=0),
        compiler_params=pltpu.CompilerParams(vmem_limit_bytes=SMALL_VMEM),
    )(*values, *others)
    return list(results)


def unit_rows(values):
    wide = values.astype(jnp.float32)
    inverse = lax.rsqrt(jnp.sum(wide * wide, axis=1, keepdims=True) + 1e-06)
    return (wide * inverse, inverse)


def lane_sums(values):
    rows = jnp.sum(values.reshape(values.shape[0] // 8, 8, values.shape[1]), axis=0)
    total = rows[:, :128]
    for start in range(128, values.shape[1], 128):
        total = total + rows[:, start : start + 128]
    return total


def piece_kernel(value, *refs):
    unit = unit_rows(value[...])[0].astype(jnp.bfloat16)
    start = 0
    for piece in refs:
        piece[...] = unit[start : start + piece.shape[0]]
        start += piece.shape[0]


def piece_skip_kernel(count, value, *refs):
    piece_kernel(value, *refs[-count:])


def unit_pieces(value, cuts, others):
    rows, width = value.shape
    return pl.pallas_call(
        functools.partial(piece_skip_kernel, len(cuts)),
        out_shape=[jax.ShapeDtypeStruct((cut, width), jnp.bfloat16) for cut in cuts],
        in_specs=[VMEM] + [ANY] * len(others),
        out_specs=[VMEM] * len(cuts),
        compiler_params=pltpu.CompilerParams(vmem_limit_bytes=SMALL_VMEM),
        cost_estimate=pl.CostEstimate(
            flops=4 * value.size, bytes_accessed=4 * value.size, transcendentals=rows
        ),
    )(value, *others)


def gathered(image, text, img_bits, txt_bits):
    img_raw = [swapped(image, bit) for bit in img_bits]
    txt_raw = swapped(text, txt_bits[0])
    rows = image.shape[0]
    cuts = [rows * 5 // 8, rows * 3 // 8]
    imgs, txts = {}, {}
    others = []
    for place in reversed(range(1, len(img_bits))):
        imgs[1 << place] = unit_pieces(img_raw[place], cuts, others)
        others = imgs[1 << place][:1]
    txts[0] = unit_pieces(text, [rows], others)
    imgs[0] = unit_pieces(image, [rows], txts[0])
    for place in range(1, len(txt_bits)):
        txts[1 << place] = [swapped(txts[0][0], txt_bits[place])]
    imgs[1] = unit_pieces(img_raw[0], cuts, imgs[0])
    txts[1] = unit_pieces(txt_raw, [rows], imgs[1][:1])
    for offset in range(1 << len(img_bits)):
        if offset not in imgs:
            high = offset.bit_length() - 1
            low = (offset & -offset).bit_length() - 1
            imgs[offset] = [
                swapped(imgs[offset ^ 1 << high][0], img_bits[high]),
                swapped(imgs[offset ^ 1 << low][1], img_bits[low]),
            ]
    for offset in range(1 << len(txt_bits)):
        if offset not in txts:
            high = offset.bit_length() - 1
            txts[offset] = [swapped(txts[offset ^ 1 << high][0], txt_bits[high])]
    imgs = [imgs[offset] for offset in range(1 << len(img_bits))]
    txts = [txts[offset] for offset in range(1 << len(txt_bits))]
    last = held(imgs[-1][1:], [], GATHER_COST)
    imgs[-1] = held(imgs[-1][:1], last, GATHER_COST) + last
    txts[-1] = held(txts[-1], imgs[-1][:1])
    return imgs, txts


def store_part(part, start, outs, cuts, rows):
    for at in range(start // rows, (start + part.shape[0]) // rows):
        size = rows // cuts[at]
        for place in range(cuts[at]):
            out = outs[sum(cuts[:at]) + place]
            first = at * rows - start + place * size
            out[...] = part[first : first + size].astype(out.dtype)


def tile_kernel(img_places, txt_places, img_cuts, txt_cuts, rows, *refs):
    n_img, n_txt = len(img_places), len(txt_places)
    taken = 0
    sources = []
    for places in (img_places, txt_places):
        pieces = sum(places)
        sources.append(refs[taken : taken + pieces])
        taken += pieces
    log_temp, bias = refs[taken : taken + 2]
    taken += 2
    img_parts = refs[taken : taken + sum(img_cuts)]
    taken += sum(img_cuts)
    txt_parts = refs[taken : taken + sum(txt_cuts)]
    sums, img_b, txt_b, grad_b = refs[taken + sum(txt_cuts) :]
    for group, held in zip(sources, (img_b, txt_b)):
        start = 0
        for piece in group:
            end = start + piece.shape[0]
            held[start:end] = piece[...]
            start = end
    temp = jnp.exp(log_temp[...])
    shift_b = bias[...]
    sum_g = jnp.zeros((8, 128), jnp.float32)
    sum_gl = jnp.zeros((8, 128), jnp.float32)
    step = 2 * rows
    for start in range(0, n_img * rows, step):
        panel = img_b[start : start + step]
        cosine = lax.dot_general(
            panel, txt_b[...], (((1,), (1,)), ((), ())), preferred_element_type=jnp.float32
        )
        scaled = temp * cosine
        logits = scaled + shift_b
        if start == 0:
            at_row = lax.broadcasted_iota(jnp.int32, logits.shape, 0)
            at_col = lax.broadcasted_iota(jnp.int32, logits.shape, 1)
            own = jnp.logical_and(at_row == at_col, at_row < rows)
            sign = jnp.where(own, 1.0, -1.0)
            grads = -sign * jax.nn.sigmoid(-sign * logits)
        else:
            grads = jax.nn.sigmoid(logits)
        sum_g = sum_g + lane_sums(grads)
        sum_gl = sum_gl + lane_sums(grads * scaled)
        grads_b = grads.astype(jnp.bfloat16)
        grad_b[start : start + step] = grads_b
        part = jnp.dot(grads_b, txt_b[...], preferred_element_type=jnp.float32)
        store_part(temp * part, start, img_parts, img_cuts, rows)
    sums[0:8] = sum_g
    sums[8:16] = sum_gl
    for start in range(0, n_txt * rows, step):
        part = lax.dot_general(
            grad_b[:, start : start + step],
            img_b[...],
            (((0,), (0,)), ((), ())),
            preferred_element_type=jnp.float32,
        )
        store_part(temp * part, start, txt_parts, txt_cuts, rows)


def tile_call(imgs, txts, log_temp, bias):
    rows = sum(piece.shape[0] for piece in imgs[0])
    width = imgs[0][0].shape[1]
    n_img, n_txt = len(imgs), len(txts)
    flat = [piece for block in imgs + txts for piece in block]
    pairs = n_img * n_txt * rows * rows
    img_cuts = [1] * n_img
    txt_cuts = [1] * n_txt
    outs = []
    for cuts in (img_cuts, txt_cuts):
        for at, cut in enumerate(cuts):
            kind = jnp.float32 if at < len(cuts) // 2 else jnp.bfloat16
            outs += [jax.ShapeDtypeStruct((rows // cut, width), kind)] * cut
    results = pl.pallas_call(
        functools.partial(
            tile_kernel,
            [len(block) for block in imgs],
            [len(block) for block in txts],
            img_cuts,
            txt_cuts,
            rows,
        ),
        out_shape=outs + [jax.ShapeDtypeStruct((16, 128), jnp.float32)],
        in_specs=[VMEM] * (len(flat) + 2),
        out_specs=[VMEM] * (len(outs) + 1),
        scratch_shapes=[
            pltpu.VMEM((n_img * rows, width), jnp.bfloat16),
            pltpu.VMEM((n_txt * rows, width), jnp.bfloat16),
            pltpu.VMEM((n_img * rows, n_txt * rows), jnp.bfloat16),
        ],
        compiler_params=pltpu.CompilerParams(vmem_limit_bytes=TILE_VMEM),
        cost_estimate=pl.CostEstimate(
            flops=6 * pairs * width, bytes_accessed=0, transcendentals=2 * pairs
        ),
    )(*flat, log_temp, bias)
    results = list(results)
    sums = results.pop()
    parts = [[results.pop(0) for _ in range(cut)] for cut in img_cuts + txt_cuts]
    return parts[:n_img], parts[n_img:], sums


def finish_kernel(recv_counts, pairs, sums, sums_recv, *refs):
    total = sums[...] + sums_recv[...]
    for place in range(2):
        whole = jnp.sum(total[8 * place : 8 * place + 8], axis=0, keepdims=True)
        refs[place - 2][...] = jnp.sum(whole, axis=1, keepdims=True) / pairs
    outs = refs[-len(recv_counts) - 2 : -2]
    for out, count in zip(outs, recv_counts):
        value, keep = refs[:2]
        rows = value.shape[0]
        total = keep[...]
        start = 0
        pieces = []
        for recv in refs[2 : 2 + count]:
            pieces.append(recv[...].astype(jnp.float32))
            start += recv.shape[0]
            if start % rows == 0:
                total = total + jnp.concatenate(pieces, axis=0)
                pieces = []
        refs = refs[2 + count :]
        unit, inverse = unit_rows(value[...])
        along = jnp.sum(unit * total, axis=1, keepdims=True)
        out[...] = ((total - unit * along) * inverse).astype(jnp.bfloat16)


def finish_call(sums, sums_recv, pairs, sides):
    flat = [array for value, keep, recvs in sides for array in [value, keep] + recvs]
    return pl.pallas_call(
        functools.partial(finish_kernel, [len(recvs) for _, _, recvs in sides], pairs),
        out_shape=[jax.ShapeDtypeStruct(value.shape, jnp.bfloat16) for value, _, _ in sides]
        + [jax.ShapeDtypeStruct((1, 1), jnp.float32)] * 2,
        in_specs=[VMEM] * (2 + len(flat)),
        out_specs=[VMEM] * (2 + len(sides)),
        compiler_params=pltpu.CompilerParams(vmem_limit_bytes=2 * SMALL_VMEM),
    )(sums, sums_recv, *flat)


def add_kernel(keep, recv, *refs):
    out = refs[-1]
    out[...] = (keep[...] + recv[...].astype(jnp.float32)).astype(out.dtype)


def sums_kernel(*refs):
    total = refs[0][...]
    for sums in refs[1:-1]:
        total = total + sums[...]
    refs[-1][...] = total


def sums_call(sums):
    return pl.pallas_call(
        sums_kernel,
        out_shape=jax.ShapeDtypeStruct(sums[0].shape, sums[0].dtype),
        in_specs=[VMEM] * len(sums),
        out_specs=VMEM,
        compiler_params=pltpu.CompilerParams(vmem_limit_bytes=SMALL_VMEM),
        cost_estimate=pl.CostEstimate(flops=SUMS_COST, bytes_accessed=0, transcendentals=0),
    )(*sums)


def add_sums_kernel(count, keep, recv, *refs):
    total = refs[0][...]
    for sums_recv in refs[1:count]:
        total = total + sums_recv[...]
    refs[-1][...] = total
    add_kernel(keep, recv, refs[-2])


def add_call(keep, recv, dtype, sums, others):
    outs = [jax.ShapeDtypeStruct(keep.shape, dtype)]
    kernel = add_kernel
    if sums:
        outs.append(jax.ShapeDtypeStruct(sums[0].shape, sums[0].dtype))
        kernel = functools.partial(add_sums_kernel, len(sums))
    return pl.pallas_call(
        kernel,
        out_shape=outs,
        in_specs=[VMEM] * (2 + len(sums)) + [ANY] * len(others),
        out_specs=[VMEM] * len(outs),
        compiler_params=pltpu.CompilerParams(vmem_limit_bytes=SMALL_VMEM),
        cost_estimate=pl.CostEstimate(
            flops=keep.size, bytes_accessed=keep.size, transcendentals=0
        ),
    )(keep, recv, *sums, *others)


def returned(parts, bits, sums, masks, others):
    parts = dict(enumerate(parts))
    sums = [sums] + [swapped(sums, mask) for mask in masks]
    recvs = []
    for place in reversed(range(len(bits))):
        arrived = {}
        for offset in range(1, 1 << place):
            arrived[offset] = swapped(parts.pop(offset | 1 << place), bits[place])
        for offset, recv in arrived.items():
            kind = jnp.float32 if offset < 1 << (place - 1) else jnp.bfloat16
            parts[offset], *total = add_call(
                parts[offset], recv, kind, sums if len(sums) > 1 else [], others
            )
            sums = total or sums
            others = [parts[offset]]
        send = parts.pop(1 << place)
        if arrived and not masks:
            send = held([send], others)[0]
        recvs.append(swapped(send, bits[place]))
    return parts[0], recvs, sums[0], others


def shards(image_embeds, text_embeds, log_temp, bias):
    rows, width = image_embeds.shape
    count = lax.axis_size("blk")
    depth = count.bit_length() - 1
    all_bits = [1 << place for place in range(depth)]
    split = 1 + depth // 2
    img_bits = all_bits[1:split][::-1]
    txt_bits = (all_bits[:1] + all_bits[split:])[::-1]
    imgs, txts = gathered(image_embeds, text_embeds, img_bits, txt_bits)
    img_parts, txt_parts, sums = tile_call(imgs, txts, log_temp.reshape(1, 1), bias.reshape(1, 1))
    img_parts, txt_parts = ([part[0] for part in parts] for parts in (img_parts, txt_parts))
    masks = [sum(bit for at, bit in enumerate(img_bits) if 1 << at & pick) for pick in range(1, 1 << len(img_bits))]
    txt_keep, txt_recvs, sums, others = returned(txt_parts, txt_bits, sums, txt_bits[-1:], [])
    sums = sums_call([sums] + [swapped(sums, mask) for mask in masks])
    img_keep, img_recvs, _, others = returned(img_parts, img_bits, sums, [], others + [sums])
    for bit in txt_bits[1:-1]:
        sums = sums + swapped(sums, bit)
    sums_recv = swapped(sums, txt_bits[0])
    *txt_recvs, sums_recv = held(txt_recvs + [sums_recv], [], RETURN_COST)
    grad_text, grad_image, grad_bias, grad_temp = finish_call(
        sums,
        sums_recv,
        float(rows * count) * float(rows * count),
        [(text_embeds, txt_keep, txt_recvs), (image_embeds, img_keep, img_recvs)],
    )
    return (grad_image, grad_text, grad_temp.reshape(1), grad_bias.reshape(1))


def solution(mesh):
    in_specs = (P(("groups", "blk"), None), P(("groups", "blk"), None), P(), P())
    out_specs = (P(("groups", "blk"), None), P(("groups", "blk"), None), P("groups"), P("groups"))
    return jax.shard_map(shards, mesh=mesh, in_specs=in_specs, out_specs=out_specs, check_vma=False)
```

```python
import functools

import jax
import jax.numpy as jnp
from jax import lax
from jax.experimental import pallas as pl
from jax.experimental.pallas import tpu as pltpu
from jax.sharding import PartitionSpec as P

TILE_VMEM = 32 * 1024 * 1024
SMALL_VMEM = 4 * 1024 * 1024
GATHER_COST = 20_000_000_000
SUMS_COST = 300_000_000
RETURN_COST = 1_000_000_000
VMEM = pl.BlockSpec(memory_space=pltpu.VMEM)
ANY = pl.BlockSpec(memory_space=pl.ANY)


def swapped(x, bit):
    count = lax.axis_size("blk")
    return lax.ppermute(x, "blk", [(i, i ^ bit) for i in range(count)])


def held(values, others, cost=0):
    count = len(values)
    results = pl.pallas_call(
        lambda *refs: None,
        out_shape=[jax.ShapeDtypeStruct(value.shape, value.dtype) for value in values],
        in_specs=[ANY] * (count + len(others)),
        out_specs=[ANY] * count,
        input_output_aliases={place: place for place in range(count)},
        cost_estimate=pl.CostEstimate(flops=cost, bytes_accessed=0, transcendentals=0),
        compiler_params=pltpu.CompilerParams(vmem_limit_bytes=SMALL_VMEM),
    )(*values, *others)
    return list(results)


def unit_rows(values):
    wide = values.astype(jnp.float32)
    inverse = lax.rsqrt(jnp.sum(wide * wide, axis=1, keepdims=True) + 1e-06)
    return (wide * inverse, inverse)


def lane_sums(values):
    rows = jnp.sum(values.reshape(values.shape[0] // 8, 8, values.shape[1]), axis=0)
    total = rows[:, :128]
    for start in range(128, values.shape[1], 128):
        total = total + rows[:, start : start + 128]
    return total


def piece_kernel(value, *refs):
    unit = unit_rows(value[...])[0].astype(jnp.bfloat16)
    start = 0
    for piece in refs:
        piece[...] = unit[start : start + piece.shape[0]]
        start += piece.shape[0]


def piece_skip_kernel(count, value, *refs):
    piece_kernel(value, *refs[-count:])


def unit_pieces(value, cuts, others):
    rows, width = value.shape
    return pl.pallas_call(
        functools.partial(piece_skip_kernel, len(cuts)),
        out_shape=[jax.ShapeDtypeStruct((cut, width), jnp.bfloat16) for cut in cuts],
        in_specs=[VMEM] + [ANY] * len(others),
        out_specs=[VMEM] * len(cuts),
        compiler_params=pltpu.CompilerParams(vmem_limit_bytes=SMALL_VMEM),
        cost_estimate=pl.CostEstimate(
            flops=4 * value.size, bytes_accessed=4 * value.size, transcendentals=rows
        ),
    )(value, *others)


def gathered(image, text, img_bits, txt_bits):
    img_raw = [swapped(image, bit) for bit in img_bits]
    txt_raw = swapped(text, txt_bits[0])
    rows = image.shape[0]
    cuts = [rows * 5 // 8, rows * 3 // 8]
    imgs, txts = {}, {}
    others = []
    for place in reversed(range(1, len(img_bits))):
        imgs[1 << place] = unit_pieces(img_raw[place], cuts, others)
        others = imgs[1 << place][:1]
    txts[0] = unit_pieces(text, [rows], others)
    imgs[0] = unit_pieces(image, [rows], txts[0])
    for place in range(1, len(txt_bits)):
        txts[1 << place] = [swapped(txts[0][0], txt_bits[place])]
    imgs[1] = unit_pieces(img_raw[0], cuts, imgs[0])
    txts[1] = unit_pieces(txt_raw, [rows], imgs[1][:1])
    for offset in range(1 << len(img_bits)):
        if offset not in imgs:
            high = offset.bit_length() - 1
            low = (offset & -offset).bit_length() - 1
            imgs[offset] = [
                swapped(imgs[offset ^ 1 << high][0], img_bits[high]),
                swapped(imgs[offset ^ 1 << low][1], img_bits[low]),
            ]
    for offset in range(1 << len(txt_bits)):
        if offset not in txts:
            high = offset.bit_length() - 1
            txts[offset] = [swapped(txts[offset ^ 1 << high][0], txt_bits[high])]
    imgs = [imgs[offset] for offset in range(1 << len(img_bits))]
    txts = [txts[offset] for offset in range(1 << len(txt_bits))]
    last = held(imgs[-1][1:], [], GATHER_COST)
    imgs[-1] = held(imgs[-1][:1], last, GATHER_COST) + last
    txts[-1] = held(txts[-1], imgs[-1][:1])
    return imgs, txts


def store_part(part, start, outs, cuts, rows):
    for at in range(start // rows, (start + part.shape[0]) // rows):
        size = rows // cuts[at]
        for place in range(cuts[at]):
            out = outs[sum(cuts[:at]) + place]
            first = at * rows - start + place * size
            out[...] = part[first : first + size].astype(out.dtype)


def tile_kernel(img_places, txt_places, img_cuts, txt_cuts, rows, *refs):
    n_img, n_txt = len(img_places), len(txt_places)
    taken = 0
    sources = []
    for places in (img_places, txt_places):
        pieces = sum(places)
        sources.append(refs[taken : taken + pieces])
        taken += pieces
    log_temp, bias = refs[taken : taken + 2]
    taken += 2
    img_parts = refs[taken : taken + sum(img_cuts)]
    taken += sum(img_cuts)
    txt_parts = refs[taken : taken + sum(txt_cuts)]
    sums, img_b, txt_b, grad_b = refs[taken + sum(txt_cuts) :]
    for group, held in zip(sources, (img_b, txt_b)):
        start = 0
        for piece in group:
            end = start + piece.shape[0]
            held[start:end] = piece[...]
            start = end
    temp = jnp.exp(log_temp[...])
    shift_b = bias[...]
    sum_g = jnp.zeros((8, 128), jnp.float32)
    sum_gl = jnp.zeros((8, 128), jnp.float32)
    step = 2 * rows
    for start in range(0, n_img * rows, step):
        panel = img_b[start : start + step]
        cosine = lax.dot_general(
            panel, txt_b[...], (((1,), (1,)), ((), ())), preferred_element_type=jnp.float32
        )
        scaled = temp * cosine
        logits = scaled + shift_b
        if start == 0:
            at_row = lax.broadcasted_iota(jnp.int32, logits.shape, 0)
            at_col = lax.broadcasted_iota(jnp.int32, logits.shape, 1)
            own = jnp.logical_and(at_row == at_col, at_row < rows)
            sign = jnp.where(own, 1.0, -1.0)
            grads = -sign * jax.nn.sigmoid(-sign * logits)
        else:
            grads = jax.nn.sigmoid(logits)
        sum_g = sum_g + lane_sums(grads)
        sum_gl = sum_gl + lane_sums(grads * scaled)
        grads_b = grads.astype(jnp.bfloat16)
        grad_b[start : start + step] = grads_b
        part = jnp.dot(grads_b, txt_b[...], preferred_element_type=jnp.float32)
        store_part(temp * part, start, img_parts, img_cuts, rows)
    sums[0:8] = sum_g
    sums[8:16] = sum_gl
    for start in range(0, n_txt * rows, step):
        part = lax.dot_general(
            grad_b[:, start : start + step],
            img_b[...],
            (((0,), (0,)), ((), ())),
            preferred_element_type=jnp.float32,
        )
        store_part(temp * part, start, txt_parts, txt_cuts, rows)


def tile_call(imgs, txts, log_temp, bias):
    rows = sum(piece.shape[0] for piece in imgs[0])
    width = imgs[0][0].shape[1]
    n_img, n_txt = len(imgs), len(txts)
    flat = [piece for block in imgs + txts for piece in block]
    pairs = n_img * n_txt * rows * rows
    img_cuts = [1] * n_img
    txt_cuts = [1] * n_txt
    outs = []
    for cuts in (img_cuts, txt_cuts):
        for at, cut in enumerate(cuts):
            kind = jnp.float32 if at < len(cuts) // 2 else jnp.bfloat16
            outs += [jax.ShapeDtypeStruct((rows // cut, width), kind)] * cut
    results = pl.pallas_call(
        functools.partial(
            tile_kernel,
            [len(block) for block in imgs],
            [len(block) for block in txts],
            img_cuts,
            txt_cuts,
            rows,
        ),
        out_shape=outs + [jax.ShapeDtypeStruct((16, 128), jnp.float32)],
        in_specs=[VMEM] * (len(flat) + 2),
        out_specs=[VMEM] * (len(outs) + 1),
        scratch_shapes=[
            pltpu.VMEM((n_img * rows, width), jnp.bfloat16),
            pltpu.VMEM((n_txt * rows, width), jnp.bfloat16),
            pltpu.VMEM((n_img * rows, n_txt * rows), jnp.bfloat16),
        ],
        compiler_params=pltpu.CompilerParams(vmem_limit_bytes=TILE_VMEM),
        cost_estimate=pl.CostEstimate(
            flops=6 * pairs * width, bytes_accessed=0, transcendentals=2 * pairs
        ),
    )(*flat, log_temp, bias)
    results = list(results)
    sums = results.pop()
    parts = [[results.pop(0) for _ in range(cut)] for cut in img_cuts + txt_cuts]
    return parts[:n_img], parts[n_img:], sums


def finish_kernel(recv_counts, pairs, sums, sums_recv, *refs):
    total = sums[...] + sums_recv[...]
    for place in range(2):
        whole = jnp.sum(total[8 * place : 8 * place + 8], axis=0, keepdims=True)
        refs[place - 2][...] = jnp.sum(whole, axis=1, keepdims=True) / pairs
    outs = refs[-len(recv_counts) - 2 : -2]
    for out, count in zip(outs, recv_counts):
        value, keep = refs[:2]
        rows = value.shape[0]
        total = keep[...]
        start = 0
        pieces = []
        for recv in refs[2 : 2 + count]:
            pieces.append(recv[...].astype(jnp.float32))
            start += recv.shape[0]
            if start % rows == 0:
                total = total + jnp.concatenate(pieces, axis=0)
                pieces = []
        refs = refs[2 + count :]
        unit, inverse = unit_rows(value[...])
        along = jnp.sum(unit * total, axis=1, keepdims=True)
        out[...] = ((total - unit * along) * inverse).astype(jnp.bfloat16)


def finish_call(sums, sums_recv, pairs, sides):
    flat = [array for value, keep, recvs in sides for array in [value, keep] + recvs]
    return pl.pallas_call(
        functools.partial(finish_kernel, [len(recvs) for _, _, recvs in sides], pairs),
        out_shape=[jax.ShapeDtypeStruct(value.shape, jnp.bfloat16) for value, _, _ in sides]
        + [jax.ShapeDtypeStruct((1, 1), jnp.float32)] * 2,
        in_specs=[VMEM] * (2 + len(flat)),
        out_specs=[VMEM] * (2 + len(sides)),
        compiler_params=pltpu.CompilerParams(vmem_limit_bytes=2 * SMALL_VMEM),
    )(sums, sums_recv, *flat)


def add_kernel(keep, recv, *refs):
    out = refs[-1]
    out[...] = (keep[...] + recv[...].astype(jnp.float32)).astype(out.dtype)


def sums_kernel(first, second, *refs):
    refs[-1][...] = first[...] + second[...]


def sums_call(sums, others):
    return pl.pallas_call(
        sums_kernel,
        out_shape=jax.ShapeDtypeStruct(sums[0].shape, sums[0].dtype),
        in_specs=[VMEM] * len(sums) + [ANY] * len(others),
        out_specs=VMEM,
        compiler_params=pltpu.CompilerParams(vmem_limit_bytes=SMALL_VMEM),
        cost_estimate=pl.CostEstimate(flops=SUMS_COST, bytes_accessed=0, transcendentals=0),
    )(*sums, *others)


def add_call(keep, recv, dtype, others):
    return pl.pallas_call(
        add_kernel,
        out_shape=jax.ShapeDtypeStruct(keep.shape, dtype),
        in_specs=[VMEM] * 2 + [ANY] * len(others),
        out_specs=VMEM,
        compiler_params=pltpu.CompilerParams(vmem_limit_bytes=SMALL_VMEM),
        cost_estimate=pl.CostEstimate(
            flops=keep.size, bytes_accessed=keep.size, transcendentals=0
        ),
    )(keep, recv, *others)


def returned(parts, bits, others, wait):
    parts = dict(enumerate(parts))
    recvs = []
    for place in reversed(range(len(bits))):
        arrived = {}
        for offset in range(1, 1 << place):
            arrived[offset] = swapped(parts.pop(offset | 1 << place), bits[place])
        for offset, recv in arrived.items():
            kind = jnp.float32 if offset < 1 << (place - 1) else jnp.bfloat16
            parts[offset] = add_call(parts[offset], recv, kind, others)
            others = [parts[offset]]
        send = parts.pop(1 << place)
        if arrived and wait:
            send = held([send], others)[0]
        recvs.append(swapped(send, bits[place]))
    return parts[0], recvs, others


def shards(image_embeds, text_embeds, log_temp, bias):
    rows, width = image_embeds.shape
    count = lax.axis_size("blk")
    depth = count.bit_length() - 1
    all_bits = [1 << place for place in range(depth)]
    split = 1 + depth // 2
    img_bits = all_bits[1:split][::-1]
    txt_bits = (all_bits[:1] + all_bits[split:])[::-1]
    imgs, txts = gathered(image_embeds, text_embeds, img_bits, txt_bits)
    img_parts, txt_parts, sums = tile_call(imgs, txts, log_temp.reshape(1, 1), bias.reshape(1, 1))
    img_parts, txt_parts = ([part[0] for part in parts] for parts in (img_parts, txt_parts))
    txt_keep, txt_recvs, others = returned(txt_parts, txt_bits, [], False)
    for bit in txt_bits + img_bits[:0:-1]:
        sums = sums_call([sums, swapped(sums, bit)], others)
    img_keep, img_recvs, others = returned(img_parts, img_bits, others + [sums], True)
    sums_recv = swapped(sums, img_bits[0])
    txt_recvs = held(txt_recvs, [], RETURN_COST)
    grad_text, grad_image, grad_bias, grad_temp = finish_call(
        sums,
        sums_recv,
        float(rows * count) * float(rows * count),
        [(text_embeds, txt_keep, txt_recvs), (image_embeds, img_keep, img_recvs)],
    )
    return (grad_image, grad_text, grad_temp.reshape(1), grad_bias.reshape(1))


def solution(mesh):
    in_specs = (P(("groups", "blk"), None), P(("groups", "blk"), None), P(), P())
    out_specs = (P(("groups", "blk"), None), P(("groups", "blk"), None), P("groups"), P("groups"))
    return jax.shard_map(shards, mesh=mesh, in_specs=in_specs, out_specs=out_specs, check_vma=False)
```

```python
import functools

import jax
import jax.numpy as jnp
from jax import lax
from jax.experimental import pallas as pl
from jax.experimental.pallas import tpu as pltpu
from jax.sharding import PartitionSpec as P

TILE_VMEM = 32 * 1024 * 1024
SMALL_VMEM = 4 * 1024 * 1024
GATHER_COST = 20_000_000_000
SUMS_COST = 300_000_000
RETURN_COST = 1_000_000_000
VMEM = pl.BlockSpec(memory_space=pltpu.VMEM)
ANY = pl.BlockSpec(memory_space=pl.ANY)


def swapped(x, bit):
    count = lax.axis_size("blk")
    return lax.ppermute(x, "blk", [(i, i ^ bit) for i in range(count)])


def held(values, others, cost=0):
    count = len(values)
    results = pl.pallas_call(
        lambda *refs: None,
        out_shape=[jax.ShapeDtypeStruct(value.shape, value.dtype) for value in values],
        in_specs=[ANY] * (count + len(others)),
        out_specs=[ANY] * count,
        input_output_aliases={place: place for place in range(count)},
        cost_estimate=pl.CostEstimate(flops=cost, bytes_accessed=0, transcendentals=0),
        compiler_params=pltpu.CompilerParams(vmem_limit_bytes=SMALL_VMEM),
    )(*values, *others)
    return list(results)


def unit_rows(values):
    wide = values.astype(jnp.float32)
    inverse = lax.rsqrt(jnp.sum(wide * wide, axis=1, keepdims=True) + 1e-06)
    return (wide * inverse, inverse)


def lane_sums(values):
    rows = jnp.sum(values.reshape(values.shape[0] // 8, 8, values.shape[1]), axis=0)
    total = rows[:, :128]
    for start in range(128, values.shape[1], 128):
        total = total + rows[:, start : start + 128]
    return total


def piece_kernel(value, *refs):
    unit = unit_rows(value[...])[0].astype(jnp.bfloat16)
    start = 0
    for piece in refs:
        piece[...] = unit[start : start + piece.shape[0]]
        start += piece.shape[0]


def piece_skip_kernel(count, value, *refs):
    piece_kernel(value, *refs[-count:])


def unit_pieces(value, cuts, others):
    rows, width = value.shape
    return pl.pallas_call(
        functools.partial(piece_skip_kernel, len(cuts)),
        out_shape=[jax.ShapeDtypeStruct((cut, width), jnp.bfloat16) for cut in cuts],
        in_specs=[VMEM] + [ANY] * len(others),
        out_specs=[VMEM] * len(cuts),
        compiler_params=pltpu.CompilerParams(vmem_limit_bytes=SMALL_VMEM),
        cost_estimate=pl.CostEstimate(
            flops=4 * value.size, bytes_accessed=4 * value.size, transcendentals=rows
        ),
    )(value, *others)


def gathered(image, text, img_bits, txt_bits):
    img_raw = [swapped(image, bit) for bit in img_bits]
    txt_raw = swapped(text, txt_bits[0])
    rows = image.shape[0]
    cuts = [rows * 5 // 8, rows * 3 // 8]
    imgs, txts = {}, {}
    others = []
    for place in reversed(range(1, len(img_bits))):
        imgs[1 << place] = unit_pieces(img_raw[place], cuts, others)
        others = imgs[1 << place][:1]
    txts[0] = unit_pieces(text, [rows], others)
    imgs[0] = unit_pieces(image, [rows], txts[0])
    for place in range(1, len(txt_bits)):
        txts[1 << place] = [swapped(txts[0][0], txt_bits[place])]
    imgs[1] = unit_pieces(img_raw[0], cuts, imgs[0])
    txts[1] = unit_pieces(txt_raw, [rows], imgs[1][:1])
    for offset in range(1 << len(img_bits)):
        if offset not in imgs:
            high = offset.bit_length() - 1
            low = (offset & -offset).bit_length() - 1
            imgs[offset] = [
                swapped(imgs[offset ^ 1 << high][0], img_bits[high]),
                swapped(imgs[offset ^ 1 << low][1], img_bits[low]),
            ]
    for offset in range(1 << len(txt_bits)):
        if offset not in txts:
            high = offset.bit_length() - 1
            txts[offset] = [swapped(txts[offset ^ 1 << high][0], txt_bits[high])]
    imgs = [imgs[offset] for offset in range(1 << len(img_bits))]
    txts = [txts[offset] for offset in range(1 << len(txt_bits))]
    last = held(imgs[-1][1:], [], GATHER_COST)
    imgs[-1] = held(imgs[-1][:1], last, GATHER_COST) + last
    txts[-1] = held(txts[-1], imgs[-1][:1])
    return imgs, txts


def store_part(part, start, outs, cuts, rows):
    for at in range(start // rows, (start + part.shape[0]) // rows):
        size = rows // cuts[at]
        for place in range(cuts[at]):
            out = outs[sum(cuts[:at]) + place]
            first = at * rows - start + place * size
            out[...] = part[first : first + size].astype(out.dtype)


def tile_kernel(img_places, txt_places, img_cuts, txt_cuts, rows, *refs):
    n_img, n_txt = len(img_places), len(txt_places)
    taken = 0
    sources = []
    for places in (img_places, txt_places):
        pieces = sum(places)
        sources.append(refs[taken : taken + pieces])
        taken += pieces
    log_temp, bias = refs[taken : taken + 2]
    taken += 2
    img_parts = refs[taken : taken + sum(img_cuts)]
    taken += sum(img_cuts)
    txt_parts = refs[taken : taken + sum(txt_cuts)]
    sums, img_b, txt_b, grad_b = refs[taken + sum(txt_cuts) :]
    for group, held in zip(sources, (img_b, txt_b)):
        start = 0
        for piece in group:
            end = start + piece.shape[0]
            held[start:end] = piece[...]
            start = end
    temp = jnp.exp(log_temp[...])
    shift_b = bias[...]
    sum_g = jnp.zeros((8, 128), jnp.float32)
    sum_gl = jnp.zeros((8, 128), jnp.float32)
    step = 2 * rows
    for start in range(0, n_img * rows, step):
        panel = img_b[start : start + step]
        cosine = lax.dot_general(
            panel, txt_b[...], (((1,), (1,)), ((), ())), preferred_element_type=jnp.float32
        )
        scaled = temp * cosine
        logits = scaled + shift_b
        if start == 0:
            at_row = lax.broadcasted_iota(jnp.int32, logits.shape, 0)
            at_col = lax.broadcasted_iota(jnp.int32, logits.shape, 1)
            own = jnp.logical_and(at_row == at_col, at_row < rows)
            sign = jnp.where(own, 1.0, -1.0)
            grads = -sign * jax.nn.sigmoid(-sign * logits)
        else:
            grads = jax.nn.sigmoid(logits)
        sum_g = sum_g + lane_sums(grads)
        sum_gl = sum_gl + lane_sums(grads * scaled)
        grads_b = grads.astype(jnp.bfloat16)
        grad_b[start : start + step] = grads_b
        part = jnp.dot(grads_b, txt_b[...], preferred_element_type=jnp.float32)
        store_part(temp * part, start, img_parts, img_cuts, rows)
    sums[0:8] = sum_g
    sums[8:16] = sum_gl
    for start in range(0, n_txt * rows, step):
        part = lax.dot_general(
            grad_b[:, start : start + step],
            img_b[...],
            (((0,), (0,)), ((), ())),
            preferred_element_type=jnp.float32,
        )
        store_part(temp * part, start, txt_parts, txt_cuts, rows)


def tile_call(imgs, txts, log_temp, bias):
    rows = sum(piece.shape[0] for piece in imgs[0])
    width = imgs[0][0].shape[1]
    n_img, n_txt = len(imgs), len(txts)
    flat = [piece for block in imgs + txts for piece in block]
    pairs = n_img * n_txt * rows * rows
    img_cuts = [1] * n_img
    txt_cuts = [1] * n_txt
    outs = []
    for cuts in (img_cuts, txt_cuts):
        for at, cut in enumerate(cuts):
            kind = jnp.float32 if at < len(cuts) // 2 else jnp.bfloat16
            outs += [jax.ShapeDtypeStruct((rows // cut, width), kind)] * cut
    results = pl.pallas_call(
        functools.partial(
            tile_kernel,
            [len(block) for block in imgs],
            [len(block) for block in txts],
            img_cuts,
            txt_cuts,
            rows,
        ),
        out_shape=outs + [jax.ShapeDtypeStruct((16, 128), jnp.float32)],
        in_specs=[VMEM] * (len(flat) + 2),
        out_specs=[VMEM] * (len(outs) + 1),
        scratch_shapes=[
            pltpu.VMEM((n_img * rows, width), jnp.bfloat16),
            pltpu.VMEM((n_txt * rows, width), jnp.bfloat16),
            pltpu.VMEM((n_img * rows, n_txt * rows), jnp.bfloat16),
        ],
        compiler_params=pltpu.CompilerParams(vmem_limit_bytes=TILE_VMEM),
        cost_estimate=pl.CostEstimate(
            flops=6 * pairs * width, bytes_accessed=0, transcendentals=2 * pairs
        ),
    )(*flat, log_temp, bias)
    results = list(results)
    sums = results.pop()
    parts = [[results.pop(0) for _ in range(cut)] for cut in img_cuts + txt_cuts]
    return parts[:n_img], parts[n_img:], sums


def finish_kernel(recv_counts, pairs, sums, sums_recv, *refs):
    total = sums[...] + sums_recv[...]
    for place in range(2):
        whole = jnp.sum(total[8 * place : 8 * place + 8], axis=0, keepdims=True)
        refs[place - 2][...] = jnp.sum(whole, axis=1, keepdims=True) / pairs
    outs = refs[-len(recv_counts) - 2 : -2]
    for out, count in zip(outs, recv_counts):
        value, keep = refs[:2]
        rows = value.shape[0]
        total = keep[...]
        start = 0
        pieces = []
        for recv in refs[2 : 2 + count]:
            pieces.append(recv[...].astype(jnp.float32))
            start += recv.shape[0]
            if start % rows == 0:
                total = total + jnp.concatenate(pieces, axis=0)
                pieces = []
        refs = refs[2 + count :]
        unit, inverse = unit_rows(value[...])
        along = jnp.sum(unit * total, axis=1, keepdims=True)
        out[...] = ((total - unit * along) * inverse).astype(jnp.bfloat16)


def finish_call(sums, sums_recv, pairs, sides):
    flat = [array for value, keep, recvs in sides for array in [value, keep] + recvs]
    return pl.pallas_call(
        functools.partial(finish_kernel, [len(recvs) for _, _, recvs in sides], pairs),
        out_shape=[jax.ShapeDtypeStruct(value.shape, jnp.bfloat16) for value, _, _ in sides]
        + [jax.ShapeDtypeStruct((1, 1), jnp.float32)] * 2,
        in_specs=[VMEM] * (2 + len(flat)),
        out_specs=[VMEM] * (2 + len(sides)),
        compiler_params=pltpu.CompilerParams(vmem_limit_bytes=2 * SMALL_VMEM),
    )(sums, sums_recv, *flat)


def add_kernel(keep, recv, *refs):
    out = refs[-1]
    out[...] = (keep[...] + recv[...].astype(jnp.float32)).astype(out.dtype)


def sums_kernel(first, second, *refs):
    refs[-1][...] = first[...] + second[...]


def sums_call(sums, others):
    return pl.pallas_call(
        sums_kernel,
        out_shape=jax.ShapeDtypeStruct(sums[0].shape, sums[0].dtype),
        in_specs=[VMEM] * len(sums) + [ANY] * len(others),
        out_specs=VMEM,
        compiler_params=pltpu.CompilerParams(vmem_limit_bytes=SMALL_VMEM),
        cost_estimate=pl.CostEstimate(flops=SUMS_COST, bytes_accessed=0, transcendentals=0),
    )(*sums, *others)


def add_call(keep, recv, dtype, others):
    return pl.pallas_call(
        add_kernel,
        out_shape=jax.ShapeDtypeStruct(keep.shape, dtype),
        in_specs=[VMEM] * 2 + [ANY] * len(others),
        out_specs=VMEM,
        compiler_params=pltpu.CompilerParams(vmem_limit_bytes=SMALL_VMEM),
        cost_estimate=pl.CostEstimate(
            flops=keep.size, bytes_accessed=keep.size, transcendentals=0
        ),
    )(keep, recv, *others)


def returned(parts, bits, others, wait):
    parts = dict(enumerate(parts))
    recvs = []
    for place in reversed(range(len(bits))):
        arrived = {}
        for offset in range(1, 1 << place):
            arrived[offset] = swapped(parts.pop(offset | 1 << place), bits[place])
        for offset, recv in arrived.items():
            kind = jnp.float32 if offset < 1 << (place - 1) else jnp.bfloat16
            parts[offset] = add_call(parts[offset], recv, kind, others)
            others = [parts[offset]]
        send = parts.pop(1 << place)
        if arrived and wait:
            send = held([send], others)[0]
        recvs.append(swapped(send, bits[place]))
    return parts[0], recvs, others


def shards(image_embeds, text_embeds, log_temp, bias):
    rows, width = image_embeds.shape
    count = lax.axis_size("blk")
    depth = count.bit_length() - 1
    all_bits = [1 << place for place in range(depth)]
    split = 1 + depth // 2
    img_bits = all_bits[1:split][::-1]
    txt_bits = (all_bits[:1] + all_bits[split:])[::-1]
    imgs, txts = gathered(image_embeds, text_embeds, img_bits, txt_bits)
    img_parts, txt_parts, sums = tile_call(imgs, txts, log_temp.reshape(1, 1), bias.reshape(1, 1))
    img_parts, txt_parts = ([part[0] for part in parts] for parts in (img_parts, txt_parts))
    txt_keep, txt_recvs, others = returned(txt_parts, txt_bits, [], False)
    for bit in img_bits[:1] + txt_bits[1:] + img_bits[:0:-1]:
        sums = sums_call([sums, swapped(sums, bit)], others)
    img_keep, img_recvs, others = returned(img_parts, img_bits, others + [sums], True)
    sums_recv = swapped(sums, txt_bits[0])
    txt_recvs = held(txt_recvs, [], RETURN_COST)
    grad_text, grad_image, grad_bias, grad_temp = finish_call(
        sums,
        sums_recv,
        float(rows * count) * float(rows * count),
        [(text_embeds, txt_keep, txt_recvs), (image_embeds, img_keep, img_recvs)],
    )
    return (grad_image, grad_text, grad_temp.reshape(1), grad_bias.reshape(1))


def solution(mesh):
    in_specs = (P(("groups", "blk"), None), P(("groups", "blk"), None), P(), P())
    out_specs = (P(("groups", "blk"), None), P(("groups", "blk"), None), P("groups"), P("groups"))
    return jax.shard_map(shards, mesh=mesh, in_specs=in_specs, out_specs=out_specs, check_vma=False)
```

```python
import functools

import jax
import jax.numpy as jnp
from jax import lax
from jax.experimental import pallas as pl
from jax.experimental.pallas import tpu as pltpu
from jax.sharding import PartitionSpec as P

TILE_VMEM = 32 * 1024 * 1024
SMALL_VMEM = 4 * 1024 * 1024
GATHER_COST = 20_000_000_000
SUMS_COST = 300_000_000
RETURN_COST = 1_000_000_000
VMEM = pl.BlockSpec(memory_space=pltpu.VMEM)
ANY = pl.BlockSpec(memory_space=pl.ANY)


def swapped(x, bit):
    count = lax.axis_size("blk")
    return lax.ppermute(x, "blk", [(i, i ^ bit) for i in range(count)])


def held(values, others, cost=0):
    count = len(values)
    results = pl.pallas_call(
        lambda *refs: None,
        out_shape=[jax.ShapeDtypeStruct(value.shape, value.dtype) for value in values],
        in_specs=[ANY] * (count + len(others)),
        out_specs=[ANY] * count,
        input_output_aliases={place: place for place in range(count)},
        cost_estimate=pl.CostEstimate(flops=cost, bytes_accessed=0, transcendentals=0),
        compiler_params=pltpu.CompilerParams(vmem_limit_bytes=SMALL_VMEM),
    )(*values, *others)
    return list(results)


def unit_rows(values):
    wide = values.astype(jnp.float32)
    inverse = lax.rsqrt(jnp.sum(wide * wide, axis=1, keepdims=True) + 1e-06)
    return (wide * inverse, inverse)


def lane_sums(values):
    rows = jnp.sum(values.reshape(values.shape[0] // 8, 8, values.shape[1]), axis=0)
    total = rows[:, :128]
    for start in range(128, values.shape[1], 128):
        total = total + rows[:, start : start + 128]
    return total


def piece_kernel(value, *refs):
    unit = unit_rows(value[...])[0].astype(jnp.bfloat16)
    start = 0
    for piece in refs:
        piece[...] = unit[start : start + piece.shape[0]]
        start += piece.shape[0]


def piece_skip_kernel(count, value, *refs):
    piece_kernel(value, *refs[-count:])


def unit_pieces(value, cuts, others):
    rows, width = value.shape
    return pl.pallas_call(
        functools.partial(piece_skip_kernel, len(cuts)),
        out_shape=[jax.ShapeDtypeStruct((cut, width), jnp.bfloat16) for cut in cuts],
        in_specs=[VMEM] + [ANY] * len(others),
        out_specs=[VMEM] * len(cuts),
        compiler_params=pltpu.CompilerParams(vmem_limit_bytes=SMALL_VMEM),
        cost_estimate=pl.CostEstimate(
            flops=4 * value.size, bytes_accessed=4 * value.size, transcendentals=rows
        ),
    )(value, *others)


def gathered(image, text, img_bits, txt_bits):
    img_raw = [swapped(image, bit) for bit in img_bits]
    txt_raw = swapped(text, txt_bits[0])
    rows = image.shape[0]
    cuts = [rows * 5 // 8, rows * 3 // 8]
    imgs, txts = {}, {}
    others = []
    for place in reversed(range(1, len(img_bits))):
        imgs[1 << place] = unit_pieces(img_raw[place], cuts, others)
        others = imgs[1 << place][:1]
    txts[0] = unit_pieces(text, [rows], others)
    imgs[0] = unit_pieces(image, [rows], txts[0])
    for place in range(1, len(txt_bits)):
        txts[1 << place] = [swapped(txts[0][0], txt_bits[place])]
    imgs[1] = unit_pieces(img_raw[0], cuts, imgs[0])
    txts[1] = unit_pieces(txt_raw, [rows], imgs[1][:1])
    for offset in range(1 << len(img_bits)):
        if offset not in imgs:
            high = offset.bit_length() - 1
            low = (offset & -offset).bit_length() - 1
            imgs[offset] = [
                swapped(imgs[offset ^ 1 << high][0], img_bits[high]),
                swapped(imgs[offset ^ 1 << low][1], img_bits[low]),
            ]
    for offset in range(1 << len(txt_bits)):
        if offset not in txts:
            high = offset.bit_length() - 1
            txts[offset] = [swapped(txts[offset ^ 1 << high][0], txt_bits[high])]
    imgs = [imgs[offset] for offset in range(1 << len(img_bits))]
    txts = [txts[offset] for offset in range(1 << len(txt_bits))]
    last = held(imgs[-1][1:], [], GATHER_COST)
    imgs[-1] = held(imgs[-1][:1], last, GATHER_COST) + last
    txts[-1] = held(txts[-1], imgs[-1][:1])
    return imgs, txts


def store_part(part, start, outs, cuts, rows):
    for at in range(start // rows, (start + part.shape[0]) // rows):
        size = rows // cuts[at]
        for place in range(cuts[at]):
            out = outs[sum(cuts[:at]) + place]
            first = at * rows - start + place * size
            out[...] = part[first : first + size].astype(out.dtype)


def tile_kernel(img_places, txt_places, img_cuts, txt_cuts, rows, *refs):
    n_img, n_txt = len(img_places), len(txt_places)
    taken = 0
    sources = []
    for places in (img_places, txt_places):
        pieces = sum(places)
        sources.append(refs[taken : taken + pieces])
        taken += pieces
    log_temp, bias = refs[taken : taken + 2]
    taken += 2
    img_parts = refs[taken : taken + sum(img_cuts)]
    taken += sum(img_cuts)
    txt_parts = refs[taken : taken + sum(txt_cuts)]
    sums, img_b, txt_b, grad_b = refs[taken + sum(txt_cuts) :]
    for group, held in zip(sources, (img_b, txt_b)):
        start = 0
        for piece in group:
            end = start + piece.shape[0]
            held[start:end] = piece[...]
            start = end
    temp = jnp.exp(log_temp[...])
    shift_b = bias[...]
    sum_g = jnp.zeros((8, 128), jnp.float32)
    sum_gl = jnp.zeros((8, 128), jnp.float32)
    step = 2 * rows
    for start in range(0, n_img * rows, step):
        panel = img_b[start : start + step]
        cosine = lax.dot_general(
            panel, txt_b[...], (((1,), (1,)), ((), ())), preferred_element_type=jnp.float32
        )
        scaled = temp * cosine
        logits = scaled + shift_b
        if start == 0:
            at_row = lax.broadcasted_iota(jnp.int32, logits.shape, 0)
            at_col = lax.broadcasted_iota(jnp.int32, logits.shape, 1)
            own = jnp.logical_and(at_row == at_col, at_row < rows)
            sign = jnp.where(own, 1.0, -1.0)
            grads = -sign * jax.nn.sigmoid(-sign * logits)
        else:
            grads = jax.nn.sigmoid(logits)
        sum_g = sum_g + lane_sums(grads)
        sum_gl = sum_gl + lane_sums(grads * scaled)
        grads_b = grads.astype(jnp.bfloat16)
        grad_b[start : start + step] = grads_b
        part = jnp.dot(grads_b, txt_b[...], preferred_element_type=jnp.float32)
        store_part(temp * part, start, img_parts, img_cuts, rows)
    sums[0:8] = sum_g
    sums[8:16] = sum_gl
    for start in range(0, n_txt * rows, step):
        part = lax.dot_general(
            grad_b[:, start : start + step],
            img_b[...],
            (((0,), (0,)), ((), ())),
            preferred_element_type=jnp.float32,
        )
        store_part(temp * part, start, txt_parts, txt_cuts, rows)


def tile_call(imgs, txts, log_temp, bias):
    rows = sum(piece.shape[0] for piece in imgs[0])
    width = imgs[0][0].shape[1]
    n_img, n_txt = len(imgs), len(txts)
    flat = [piece for block in imgs + txts for piece in block]
    pairs = n_img * n_txt * rows * rows
    img_cuts = [1] * n_img
    txt_cuts = [1] * n_txt
    outs = []
    for cuts in (img_cuts, txt_cuts):
        for at, cut in enumerate(cuts):
            kind = jnp.float32 if at < len(cuts) // 2 else jnp.bfloat16
            outs += [jax.ShapeDtypeStruct((rows // cut, width), kind)] * cut
    results = pl.pallas_call(
        functools.partial(
            tile_kernel,
            [len(block) for block in imgs],
            [len(block) for block in txts],
            img_cuts,
            txt_cuts,
            rows,
        ),
        out_shape=outs + [jax.ShapeDtypeStruct((16, 128), jnp.float32)],
        in_specs=[VMEM] * (len(flat) + 2),
        out_specs=[VMEM] * (len(outs) + 1),
        scratch_shapes=[
            pltpu.VMEM((n_img * rows, width), jnp.bfloat16),
            pltpu.VMEM((n_txt * rows, width), jnp.bfloat16),
            pltpu.VMEM((n_img * rows, n_txt * rows), jnp.bfloat16),
        ],
        compiler_params=pltpu.CompilerParams(vmem_limit_bytes=TILE_VMEM),
        cost_estimate=pl.CostEstimate(
            flops=6 * pairs * width, bytes_accessed=0, transcendentals=2 * pairs
        ),
    )(*flat, log_temp, bias)
    results = list(results)
    sums = results.pop()
    parts = [[results.pop(0) for _ in range(cut)] for cut in img_cuts + txt_cuts]
    return parts[:n_img], parts[n_img:], sums


def finish_kernel(recv_counts, pairs, sums, sums_recv, *refs):
    total = sums[...] + sums_recv[...]
    for place in range(2):
        whole = jnp.sum(total[8 * place : 8 * place + 8], axis=0, keepdims=True)
        refs[place - 2][...] = jnp.sum(whole, axis=1, keepdims=True) / pairs
    outs = refs[-len(recv_counts) - 2 : -2]
    for out, count in zip(outs, recv_counts):
        value, keep = refs[:2]
        rows = value.shape[0]
        total = keep[...]
        start = 0
        pieces = []
        for recv in refs[2 : 2 + count]:
            pieces.append(recv[...].astype(jnp.float32))
            start += recv.shape[0]
            if start % rows == 0:
                total = total + jnp.concatenate(pieces, axis=0)
                pieces = []
        refs = refs[2 + count :]
        unit, inverse = unit_rows(value[...])
        along = jnp.sum(unit * total, axis=1, keepdims=True)
        out[...] = ((total - unit * along) * inverse).astype(jnp.bfloat16)


def finish_call(sums, sums_recv, pairs, sides):
    flat = [array for value, keep, recvs in sides for array in [value, keep] + recvs]
    return pl.pallas_call(
        functools.partial(finish_kernel, [len(recvs) for _, _, recvs in sides], pairs),
        out_shape=[jax.ShapeDtypeStruct(value.shape, jnp.bfloat16) for value, _, _ in sides]
        + [jax.ShapeDtypeStruct((1, 1), jnp.float32)] * 2,
        in_specs=[VMEM] * (2 + len(flat)),
        out_specs=[VMEM] * (2 + len(sides)),
        compiler_params=pltpu.CompilerParams(vmem_limit_bytes=2 * SMALL_VMEM),
    )(sums, sums_recv, *flat)


def add_kernel(keep, recv, *refs):
    out = refs[-1]
    out[...] = (keep[...] + recv[...].astype(jnp.float32)).astype(out.dtype)


def sums_kernel(first, second, *refs):
    refs[-1][...] = first[...] + second[...]


def sums_call(sums, others):
    return pl.pallas_call(
        sums_kernel,
        out_shape=jax.ShapeDtypeStruct(sums[0].shape, sums[0].dtype),
        in_specs=[VMEM] * len(sums) + [ANY] * len(others),
        out_specs=VMEM,
        compiler_params=pltpu.CompilerParams(vmem_limit_bytes=SMALL_VMEM),
        cost_estimate=pl.CostEstimate(flops=SUMS_COST, bytes_accessed=0, transcendentals=0),
    )(*sums, *others)


def add_call(keep, recv, dtype, others):
    return pl.pallas_call(
        add_kernel,
        out_shape=jax.ShapeDtypeStruct(keep.shape, dtype),
        in_specs=[VMEM] * 2 + [ANY] * len(others),
        out_specs=VMEM,
        compiler_params=pltpu.CompilerParams(vmem_limit_bytes=SMALL_VMEM),
        cost_estimate=pl.CostEstimate(
            flops=keep.size, bytes_accessed=keep.size, transcendentals=0
        ),
    )(keep, recv, *others)


def returned(parts, bits, others, wait):
    parts = dict(enumerate(parts))
    recvs = []
    for place in reversed(range(len(bits))):
        arrived = {}
        for offset in range(1, 1 << place):
            arrived[offset] = swapped(parts.pop(offset | 1 << place), bits[place])
        for offset, recv in arrived.items():
            kind = jnp.float32 if offset < 1 << (place - 1) else jnp.bfloat16
            parts[offset] = add_call(parts[offset], recv, kind, others)
            others = [parts[offset]]
        send = parts.pop(1 << place)
        if arrived and wait:
            send = held([send], others)[0]
        recvs.append(swapped(send, bits[place]))
    return parts[0], recvs, others


def shards(image_embeds, text_embeds, log_temp, bias):
    rows, width = image_embeds.shape
    count = lax.axis_size("blk")
    depth = count.bit_length() - 1
    all_bits = [1 << place for place in range(depth)]
    split = 1 + depth // 2
    img_bits = all_bits[1:split][::-1]
    txt_bits = (all_bits[:1] + all_bits[split:])[::-1]
    txt_bits[0] |= img_bits[0]
    imgs, txts = gathered(image_embeds, text_embeds, img_bits, txt_bits)
    img_parts, txt_parts, sums = tile_call(imgs, txts, log_temp.reshape(1, 1), bias.reshape(1, 1))
    img_parts, txt_parts = ([part[0] for part in parts] for parts in (img_parts, txt_parts))
    txt_keep, txt_recvs, others = returned(txt_parts, txt_bits, [], False)
    for bit in img_bits[:1] + txt_bits[1:] + img_bits[:0:-1]:
        sums = sums_call([sums, swapped(sums, bit)], others)
    img_keep, img_recvs, others = returned(img_parts, img_bits, others + [sums], True)
    sums_recv = swapped(sums, txt_bits[0])
    txt_recvs = held(txt_recvs, [], RETURN_COST)
    grad_text, grad_image, grad_bias, grad_temp = finish_call(
        sums,
        sums_recv,
        float(rows * count) * float(rows * count),
        [(text_embeds, txt_keep, txt_recvs), (image_embeds, img_keep, img_recvs)],
    )
    return (grad_image, grad_text, grad_temp.reshape(1), grad_bias.reshape(1))


def solution(mesh):
    in_specs = (P(("groups", "blk"), None), P(("groups", "blk"), None), P(), P())
    out_specs = (P(("groups", "blk"), None), P(("groups", "blk"), None), P("groups"), P("groups"))
    return jax.shard_map(shards, mesh=mesh, in_specs=in_specs, out_specs=out_specs, check_vma=False)
```

```python
import functools

import jax
import jax.numpy as jnp
from jax import lax
from jax.experimental import pallas as pl
from jax.experimental.pallas import tpu as pltpu
from jax.sharding import PartitionSpec as P

TILE_VMEM = 32 * 1024 * 1024
SMALL_VMEM = 4 * 1024 * 1024
GATHER_COST = 20_000_000_000
SUMS_COST = 300_000_000
RETURN_COST = 1_000_000_000
VMEM = pl.BlockSpec(memory_space=pltpu.VMEM)
ANY = pl.BlockSpec(memory_space=pl.ANY)


def swapped(x, bit):
    count = lax.axis_size("blk")
    return lax.ppermute(x, "blk", [(i, i ^ bit) for i in range(count)])


def held(values, others, cost=0):
    count = len(values)
    results = pl.pallas_call(
        lambda *refs: None,
        out_shape=[jax.ShapeDtypeStruct(value.shape, value.dtype) for value in values],
        in_specs=[ANY] * (count + len(others)),
        out_specs=[ANY] * count,
        input_output_aliases={place: place for place in range(count)},
        cost_estimate=pl.CostEstimate(flops=cost, bytes_accessed=0, transcendentals=0),
        compiler_params=pltpu.CompilerParams(vmem_limit_bytes=SMALL_VMEM),
    )(*values, *others)
    return list(results)


def unit_rows(values):
    wide = values.astype(jnp.float32)
    inverse = lax.rsqrt(jnp.sum(wide * wide, axis=1, keepdims=True) + 1e-06)
    return (wide * inverse, inverse)


def lane_sums(values):
    rows = jnp.sum(values.reshape(values.shape[0] // 8, 8, values.shape[1]), axis=0)
    total = rows[:, :128]
    for start in range(128, values.shape[1], 128):
        total = total + rows[:, start : start + 128]
    return total


def unit_kernel(value, *refs):
    refs[-1][...] = unit_rows(value[...])[0].astype(jnp.bfloat16)


def unit_block(value, others):
    return [
        pl.pallas_call(
            unit_kernel,
            out_shape=jax.ShapeDtypeStruct(value.shape, jnp.bfloat16),
            in_specs=[VMEM] + [ANY] * len(others),
            out_specs=VMEM,
            compiler_params=pltpu.CompilerParams(vmem_limit_bytes=SMALL_VMEM),
            cost_estimate=pl.CostEstimate(
                flops=4 * value.size, bytes_accessed=4 * value.size, transcendentals=0
            ),
        )(value, *others)
    ]


def gathered(image, text, img_bits, txt_bits):
    img_raw = [swapped(image, bit) for bit in img_bits]
    txt_raw = swapped(text, txt_bits[0])
    imgs, txts = {}, {}
    imgs[1] = unit_block(img_raw[0], [])
    txts[0] = unit_block(text, imgs[1])
    imgs[0] = unit_block(image, txts[0])
    for place in range(1, len(txt_bits)):
        txts[1 << place] = [swapped(txts[0][0], txt_bits[place])]
    txts[1] = others = unit_block(txt_raw, imgs[0])
    for place in range(1, len(img_bits)):
        imgs[1 << place] = others = unit_block(img_raw[place], others)
    for blocks, bits in ((imgs, img_bits), (txts, txt_bits)):
        for offset in range(1 << len(bits)):
            if offset not in blocks:
                high = offset.bit_length() - 1
                blocks[offset] = [swapped(blocks[offset ^ 1 << high][0], bits[high])]
    imgs = [imgs[offset] for offset in range(1 << len(img_bits))]
    txts = [txts[offset] for offset in range(1 << len(txt_bits))]
    imgs[-1] = held(imgs[-1], [], GATHER_COST)
    txts[-1] = held(txts[-1], imgs[-1])
    return imgs, txts


def store_part(part, start, outs, cuts, rows):
    for at in range(start // rows, (start + part.shape[0]) // rows):
        size = rows // cuts[at]
        for place in range(cuts[at]):
            out = outs[sum(cuts[:at]) + place]
            first = at * rows - start + place * size
            out[...] = part[first : first + size].astype(out.dtype)


def tile_kernel(img_places, txt_places, img_cuts, txt_cuts, rows, *refs):
    n_img, n_txt = len(img_places), len(txt_places)
    taken = 0
    sources = []
    for places in (img_places, txt_places):
        pieces = sum(places)
        sources.append(refs[taken : taken + pieces])
        taken += pieces
    log_temp, bias = refs[taken : taken + 2]
    taken += 2
    img_parts = refs[taken : taken + sum(img_cuts)]
    taken += sum(img_cuts)
    txt_parts = refs[taken : taken + sum(txt_cuts)]
    sums, img_b, txt_b, grad_b = refs[taken + sum(txt_cuts) :]
    for group, held in zip(sources, (img_b, txt_b)):
        start = 0
        for piece in group:
            end = start + piece.shape[0]
            held[start:end] = piece[...]
            start = end
    temp = jnp.exp(log_temp[...])
    shift_b = bias[...]
    sum_g = jnp.zeros((8, 128), jnp.float32)
    sum_gl = jnp.zeros((8, 128), jnp.float32)
    step = 2 * rows
    for start in range(0, n_img * rows, step):
        panel = img_b[start : start + step]
        cosine = lax.dot_general(
            panel, txt_b[...], (((1,), (1,)), ((), ())), preferred_element_type=jnp.float32
        )
        scaled = temp * cosine
        logits = scaled + shift_b
        if start == 0:
            at_row = lax.broadcasted_iota(jnp.int32, logits.shape, 0)
            at_col = lax.broadcasted_iota(jnp.int32, logits.shape, 1)
            own = jnp.logical_and(at_row == at_col, at_row < rows)
            sign = jnp.where(own, 1.0, -1.0)
            grads = -sign * jax.nn.sigmoid(-sign * logits)
        else:
            grads = jax.nn.sigmoid(logits)
        sum_g = sum_g + lane_sums(grads)
        sum_gl = sum_gl + lane_sums(grads * scaled)
        grads_b = grads.astype(jnp.bfloat16)
        grad_b[start : start + step] = grads_b
        part = jnp.dot(grads_b, txt_b[...], preferred_element_type=jnp.float32)
        store_part(temp * part, start, img_parts, img_cuts, rows)
    sums[0:8] = sum_g
    sums[8:16] = sum_gl
    for start in range(0, n_txt * rows, step):
        part = lax.dot_general(
            grad_b[:, start : start + step],
            img_b[...],
            (((0,), (0,)), ((), ())),
            preferred_element_type=jnp.float32,
        )
        store_part(temp * part, start, txt_parts, txt_cuts, rows)


def tile_call(imgs, txts, log_temp, bias):
    rows = sum(piece.shape[0] for piece in imgs[0])
    width = imgs[0][0].shape[1]
    n_img, n_txt = len(imgs), len(txts)
    flat = [piece for block in imgs + txts for piece in block]
    pairs = n_img * n_txt * rows * rows
    img_cuts = [1] * n_img
    txt_cuts = [1] * n_txt
    outs = []
    for cuts in (img_cuts, txt_cuts):
        for at, cut in enumerate(cuts):
            kind = jnp.float32 if at < len(cuts) // 2 else jnp.bfloat16
            outs += [jax.ShapeDtypeStruct((rows // cut, width), kind)] * cut
    results = pl.pallas_call(
        functools.partial(
            tile_kernel,
            [len(block) for block in imgs],
            [len(block) for block in txts],
            img_cuts,
            txt_cuts,
            rows,
        ),
        out_shape=outs + [jax.ShapeDtypeStruct((16, 128), jnp.float32)],
        in_specs=[VMEM] * (len(flat) + 2),
        out_specs=[VMEM] * (len(outs) + 1),
        scratch_shapes=[
            pltpu.VMEM((n_img * rows, width), jnp.bfloat16),
            pltpu.VMEM((n_txt * rows, width), jnp.bfloat16),
            pltpu.VMEM((n_img * rows, n_txt * rows), jnp.bfloat16),
        ],
        compiler_params=pltpu.CompilerParams(vmem_limit_bytes=TILE_VMEM),
        cost_estimate=pl.CostEstimate(
            flops=6 * pairs * width, bytes_accessed=0, transcendentals=2 * pairs
        ),
    )(*flat, log_temp, bias)
    results = list(results)
    sums = results.pop()
    parts = [[results.pop(0) for _ in range(cut)] for cut in img_cuts + txt_cuts]
    return parts[:n_img], parts[n_img:], sums


def finish_kernel(recv_counts, pairs, sums, sums_recv, *refs):
    total = sums[...] + sums_recv[...]
    for place in range(2):
        whole = jnp.sum(total[8 * place : 8 * place + 8], axis=0, keepdims=True)
        refs[place - 2][...] = jnp.sum(whole, axis=1, keepdims=True) / pairs
    outs = refs[-len(recv_counts) - 2 : -2]
    for out, count in zip(outs, recv_counts):
        value, keep = refs[:2]
        rows = value.shape[0]
        total = keep[...]
        start = 0
        pieces = []
        for recv in refs[2 : 2 + count]:
            pieces.append(recv[...].astype(jnp.float32))
            start += recv.shape[0]
            if start % rows == 0:
                total = total + jnp.concatenate(pieces, axis=0)
                pieces = []
        refs = refs[2 + count :]
        unit, inverse = unit_rows(value[...])
        along = jnp.sum(unit * total, axis=1, keepdims=True)
        out[...] = ((total - unit * along) * inverse).astype(jnp.bfloat16)


def finish_call(sums, sums_recv, pairs, sides):
    flat = [array for value, keep, recvs in sides for array in [value, keep] + recvs]
    return pl.pallas_call(
        functools.partial(finish_kernel, [len(recvs) for _, _, recvs in sides], pairs),
        out_shape=[jax.ShapeDtypeStruct(value.shape, jnp.bfloat16) for value, _, _ in sides]
        + [jax.ShapeDtypeStruct((1, 1), jnp.float32)] * 2,
        in_specs=[VMEM] * (2 + len(flat)),
        out_specs=[VMEM] * (2 + len(sides)),
        compiler_params=pltpu.CompilerParams(vmem_limit_bytes=2 * SMALL_VMEM),
    )(sums, sums_recv, *flat)


def add_kernel(keep, recv, *refs):
    out = refs[-1]
    out[...] = (keep[...] + recv[...].astype(jnp.float32)).astype(out.dtype)


def sums_kernel(first, second, *refs):
    refs[-1][...] = first[...] + second[...]


def sums_call(sums, others):
    return pl.pallas_call(
        sums_kernel,
        out_shape=jax.ShapeDtypeStruct(sums[0].shape, sums[0].dtype),
        in_specs=[VMEM] * len(sums) + [ANY] * len(others),
        out_specs=VMEM,
        compiler_params=pltpu.CompilerParams(vmem_limit_bytes=SMALL_VMEM),
        cost_estimate=pl.CostEstimate(flops=SUMS_COST, bytes_accessed=0, transcendentals=0),
    )(*sums, *others)


def add_call(keep, recv, dtype, others):
    return pl.pallas_call(
        add_kernel,
        out_shape=jax.ShapeDtypeStruct(keep.shape, dtype),
        in_specs=[VMEM] * 2 + [ANY] * len(others),
        out_specs=VMEM,
        compiler_params=pltpu.CompilerParams(vmem_limit_bytes=SMALL_VMEM),
        cost_estimate=pl.CostEstimate(
            flops=keep.size, bytes_accessed=keep.size, transcendentals=0
        ),
    )(keep, recv, *others)


def returned(parts, bits, others, wait):
    parts = dict(enumerate(parts))
    recvs = []
    for place in reversed(range(len(bits))):
        arrived = {}
        for offset in range(1, 1 << place):
            arrived[offset] = swapped(parts.pop(offset | 1 << place), bits[place])
        for offset, recv in arrived.items():
            kind = jnp.float32 if offset < 1 << (place - 1) else jnp.bfloat16
            parts[offset] = add_call(parts[offset], recv, kind, others)
            others = [parts[offset]]
        send = parts.pop(1 << place)
        if arrived and wait:
            send = held([send], others)[0]
        recvs.append(swapped(send, bits[place]))
    return parts[0], recvs, others


def shards(image_embeds, text_embeds, log_temp, bias):
    rows, width = image_embeds.shape
    count = lax.axis_size("blk")
    depth = count.bit_length() - 1
    all_bits = [1 << place for place in range(depth)]
    split = 1 + depth // 2
    img_bits = all_bits[1:split][::-1]
    txt_bits = (all_bits[:1] + all_bits[split:])[::-1]
    txt_bits[0] |= img_bits[0]
    imgs, txts = gathered(image_embeds, text_embeds, img_bits, txt_bits)
    img_parts, txt_parts, sums = tile_call(imgs, txts, log_temp.reshape(1, 1), bias.reshape(1, 1))
    img_parts, txt_parts = ([part[0] for part in parts] for parts in (img_parts, txt_parts))
    txt_keep, txt_recvs, others = returned(txt_parts, txt_bits, [], False)
    for bit in img_bits[:1] + txt_bits[1:] + img_bits[:0:-1]:
        sums = sums_call([sums, swapped(sums, bit)], others)
    img_keep, img_recvs, others = returned(img_parts, img_bits, others + [sums], True)
    sums_recv = swapped(sums, txt_bits[0])
    txt_recvs = held(txt_recvs, [], RETURN_COST)
    grad_text, grad_image, grad_bias, grad_temp = finish_call(
        sums,
        sums_recv,
        float(rows * count) * float(rows * count),
        [(text_embeds, txt_keep, txt_recvs), (image_embeds, img_keep, img_recvs)],
    )
    return (grad_image, grad_text, grad_temp.reshape(1), grad_bias.reshape(1))


def solution(mesh):
    in_specs = (P(("groups", "blk"), None), P(("groups", "blk"), None), P(), P())
    out_specs = (P(("groups", "blk"), None), P(("groups", "blk"), None), P("groups"), P("groups"))
    return jax.shard_map(shards, mesh=mesh, in_specs=in_specs, out_specs=out_specs, check_vma=False)
```

```python
import functools

import jax
import jax.numpy as jnp
from jax import lax
from jax.experimental import pallas as pl
from jax.experimental.pallas import tpu as pltpu
from jax.sharding import PartitionSpec as P

TILE_VMEM = 32 * 1024 * 1024
SMALL_VMEM = 4 * 1024 * 1024
GATHER_COST = 20_000_000_000
SUMS_COST = 300_000_000
RETURN_COST = 1_000_000_000
VMEM = pl.BlockSpec(memory_space=pltpu.VMEM)
ANY = pl.BlockSpec(memory_space=pl.ANY)


def swapped(x, bit):
    count = lax.axis_size("blk")
    return lax.ppermute(x, "blk", [(i, i ^ bit) for i in range(count)])


def held(values, others, cost=0):
    count = len(values)
    results = pl.pallas_call(
        lambda *refs: None,
        out_shape=[jax.ShapeDtypeStruct(value.shape, value.dtype) for value in values],
        in_specs=[ANY] * (count + len(others)),
        out_specs=[ANY] * count,
        input_output_aliases={place: place for place in range(count)},
        cost_estimate=pl.CostEstimate(flops=cost, bytes_accessed=0, transcendentals=0),
        compiler_params=pltpu.CompilerParams(vmem_limit_bytes=SMALL_VMEM),
    )(*values, *others)
    return list(results)


def unit_rows(values):
    wide = values.astype(jnp.float32)
    inverse = lax.rsqrt(jnp.sum(wide * wide, axis=1, keepdims=True) + 1e-06)
    return (wide * inverse, inverse)


def lane_sums(values):
    rows = jnp.sum(values.reshape(values.shape[0] // 8, 8, values.shape[1]), axis=0)
    total = rows[:, :128]
    for start in range(128, values.shape[1], 128):
        total = total + rows[:, start : start + 128]
    return total


def unit_kernel(value, *refs):
    refs[-1][...] = unit_rows(value[...])[0].astype(jnp.bfloat16)


def unit_block(value, others):
    return [
        pl.pallas_call(
            unit_kernel,
            out_shape=jax.ShapeDtypeStruct(value.shape, jnp.bfloat16),
            in_specs=[VMEM] + [ANY] * len(others),
            out_specs=VMEM,
            compiler_params=pltpu.CompilerParams(vmem_limit_bytes=SMALL_VMEM),
            cost_estimate=pl.CostEstimate(
                flops=4 * value.size, bytes_accessed=4 * value.size, transcendentals=0
            ),
        )(value, *others)
    ]


def gathered(image, text, img_bits, txt_bits):
    img_raw = [swapped(image, bit) for bit in img_bits]
    txt_raw = swapped(text, txt_bits[0])
    imgs, txts = {}, {}
    imgs[1] = unit_block(img_raw[0], [])
    txts[0] = unit_block(text, imgs[1])
    imgs[0] = unit_block(image, txts[0])
    for place in range(1, len(txt_bits)):
        txts[1 << place] = [swapped(txts[0][0], txt_bits[place])]
    others = imgs[0]
    for place in range(1, len(img_bits)):
        imgs[1 << place] = others = unit_block(img_raw[place], others)
    txts[1] = unit_block(txt_raw, others)
    for blocks, bits in ((imgs, img_bits), (txts, txt_bits)):
        for offset in range(1 << len(bits)):
            if offset not in blocks:
                high = offset.bit_length() - 1
                blocks[offset] = [swapped(blocks[offset ^ 1 << high][0], bits[high])]
    imgs = [imgs[offset] for offset in range(1 << len(img_bits))]
    txts = [txts[offset] for offset in range(1 << len(txt_bits))]
    imgs[-1] = held(imgs[-1], [], GATHER_COST)
    txts[-1] = held(txts[-1], imgs[-1])
    return imgs, txts


def store_part(part, start, outs, cuts, rows):
    for at in range(start // rows, (start + part.shape[0]) // rows):
        size = rows // cuts[at]
        for place in range(cuts[at]):
            out = outs[sum(cuts[:at]) + place]
            first = at * rows - start + place * size
            out[...] = part[first : first + size].astype(out.dtype)


def tile_kernel(img_places, txt_places, img_cuts, txt_cuts, rows, *refs):
    n_img, n_txt = len(img_places), len(txt_places)
    taken = 0
    sources = []
    for places in (img_places, txt_places):
        pieces = sum(places)
        sources.append(refs[taken : taken + pieces])
        taken += pieces
    log_temp, bias = refs[taken : taken + 2]
    taken += 2
    img_parts = refs[taken : taken + sum(img_cuts)]
    taken += sum(img_cuts)
    txt_parts = refs[taken : taken + sum(txt_cuts)]
    sums, img_b, txt_b, grad_b = refs[taken + sum(txt_cuts) :]
    for group, held in zip(sources, (img_b, txt_b)):
        start = 0
        for piece in group:
            end = start + piece.shape[0]
            held[start:end] = piece[...]
            start = end
    temp = jnp.exp(log_temp[...])
    shift_b = bias[...]
    sum_g = jnp.zeros((8, 128), jnp.float32)
    sum_gl = jnp.zeros((8, 128), jnp.float32)
    step = 2 * rows
    for start in range(0, n_img * rows, step):
        panel = img_b[start : start + step]
        cosine = lax.dot_general(
            panel, txt_b[...], (((1,), (1,)), ((), ())), preferred_element_type=jnp.float32
        )
        scaled = temp * cosine
        logits = scaled + shift_b
        if start == 0:
            at_row = lax.broadcasted_iota(jnp.int32, logits.shape, 0)
            at_col = lax.broadcasted_iota(jnp.int32, logits.shape, 1)
            own = jnp.logical_and(at_row == at_col, at_row < rows)
            sign = jnp.where(own, 1.0, -1.0)
            grads = -sign * jax.nn.sigmoid(-sign * logits)
        else:
            grads = jax.nn.sigmoid(logits)
        sum_g = sum_g + lane_sums(grads)
        sum_gl = sum_gl + lane_sums(grads * scaled)
        grads_b = grads.astype(jnp.bfloat16)
        grad_b[start : start + step] = grads_b
        part = jnp.dot(grads_b, txt_b[...], preferred_element_type=jnp.float32)
        store_part(temp * part, start, img_parts, img_cuts, rows)
    sums[0:8] = sum_g
    sums[8:16] = sum_gl
    for start in range(0, n_txt * rows, step):
        part = lax.dot_general(
            grad_b[:, start : start + step],
            img_b[...],
            (((0,), (0,)), ((), ())),
            preferred_element_type=jnp.float32,
        )
        store_part(temp * part, start, txt_parts, txt_cuts, rows)


def tile_call(imgs, txts, log_temp, bias):
    rows = sum(piece.shape[0] for piece in imgs[0])
    width = imgs[0][0].shape[1]
    n_img, n_txt = len(imgs), len(txts)
    flat = [piece for block in imgs + txts for piece in block]
    pairs = n_img * n_txt * rows * rows
    img_cuts = [1] * n_img
    txt_cuts = [1] * n_txt
    outs = []
    for cuts in (img_cuts, txt_cuts):
        for at, cut in enumerate(cuts):
            kind = jnp.float32 if at < len(cuts) // 2 else jnp.bfloat16
            outs += [jax.ShapeDtypeStruct((rows // cut, width), kind)] * cut
    results = pl.pallas_call(
        functools.partial(
            tile_kernel,
            [len(block) for block in imgs],
            [len(block) for block in txts],
            img_cuts,
            txt_cuts,
            rows,
        ),
        out_shape=outs + [jax.ShapeDtypeStruct((16, 128), jnp.float32)],
        in_specs=[VMEM] * (len(flat) + 2),
        out_specs=[VMEM] * (len(outs) + 1),
        scratch_shapes=[
            pltpu.VMEM((n_img * rows, width), jnp.bfloat16),
            pltpu.VMEM((n_txt * rows, width), jnp.bfloat16),
            pltpu.VMEM((n_img * rows, n_txt * rows), jnp.bfloat16),
        ],
        compiler_params=pltpu.CompilerParams(vmem_limit_bytes=TILE_VMEM),
        cost_estimate=pl.CostEstimate(
            flops=6 * pairs * width, bytes_accessed=0, transcendentals=2 * pairs
        ),
    )(*flat, log_temp, bias)
    results = list(results)
    sums = results.pop()
    parts = [[results.pop(0) for _ in range(cut)] for cut in img_cuts + txt_cuts]
    return parts[:n_img], parts[n_img:], sums


def finish_kernel(recv_counts, pairs, sums, sums_recv, *refs):
    total = sums[...] + sums_recv[...]
    for place in range(2):
        whole = jnp.sum(total[8 * place : 8 * place + 8], axis=0, keepdims=True)
        refs[place - 2][...] = jnp.sum(whole, axis=1, keepdims=True) / pairs
    outs = refs[-len(recv_counts) - 2 : -2]
    for out, count in zip(outs, recv_counts):
        value, keep = refs[:2]
        rows = value.shape[0]
        total = keep[...]
        start = 0
        pieces = []
        for recv in refs[2 : 2 + count]:
            pieces.append(recv[...].astype(jnp.float32))
            start += recv.shape[0]
            if start % rows == 0:
                total = total + jnp.concatenate(pieces, axis=0)
                pieces = []
        refs = refs[2 + count :]
        unit, inverse = unit_rows(value[...])
        along = jnp.sum(unit * total, axis=1, keepdims=True)
        out[...] = ((total - unit * along) * inverse).astype(jnp.bfloat16)


def finish_call(sums, sums_recv, pairs, sides):
    flat = [array for value, keep, recvs in sides for array in [value, keep] + recvs]
    return pl.pallas_call(
        functools.partial(finish_kernel, [len(recvs) for _, _, recvs in sides], pairs),
        out_shape=[jax.ShapeDtypeStruct(value.shape, jnp.bfloat16) for value, _, _ in sides]
        + [jax.ShapeDtypeStruct((1, 1), jnp.float32)] * 2,
        in_specs=[VMEM] * (2 + len(flat)),
        out_specs=[VMEM] * (2 + len(sides)),
        compiler_params=pltpu.CompilerParams(vmem_limit_bytes=2 * SMALL_VMEM),
    )(sums, sums_recv, *flat)


def add_kernel(keep, recv, *refs):
    out = refs[-1]
    out[...] = (keep[...] + recv[...].astype(jnp.float32)).astype(out.dtype)


def sums_kernel(first, second, *refs):
    refs[-1][...] = first[...] + second[...]


def sums_call(sums, others):
    return pl.pallas_call(
        sums_kernel,
        out_shape=jax.ShapeDtypeStruct(sums[0].shape, sums[0].dtype),
        in_specs=[VMEM] * len(sums) + [ANY] * len(others),
        out_specs=VMEM,
        compiler_params=pltpu.CompilerParams(vmem_limit_bytes=SMALL_VMEM),
        cost_estimate=pl.CostEstimate(flops=SUMS_COST, bytes_accessed=0, transcendentals=0),
    )(*sums, *others)


def add_call(keep, recv, dtype, others):
    return pl.pallas_call(
        add_kernel,
        out_shape=jax.ShapeDtypeStruct(keep.shape, dtype),
        in_specs=[VMEM] * 2 + [ANY] * len(others),
        out_specs=VMEM,
        compiler_params=pltpu.CompilerParams(vmem_limit_bytes=SMALL_VMEM),
        cost_estimate=pl.CostEstimate(
            flops=keep.size, bytes_accessed=keep.size, transcendentals=0
        ),
    )(keep, recv, *others)


def returned(parts, bits, others, wait):
    parts = dict(enumerate(parts))
    recvs = []
    for place in reversed(range(len(bits))):
        arrived = {}
        for offset in range(1, 1 << place):
            arrived[offset] = swapped(parts.pop(offset | 1 << place), bits[place])
        for offset, recv in arrived.items():
            kind = jnp.float32 if offset < 1 << (place - 1) else jnp.bfloat16
            parts[offset] = add_call(parts[offset], recv, kind, others)
            others = [parts[offset]]
        send = parts.pop(1 << place)
        if arrived and wait:
            send = held([send], others)[0]
        recvs.append(swapped(send, bits[place]))
    return parts[0], recvs, others


def shards(image_embeds, text_embeds, log_temp, bias):
    rows, width = image_embeds.shape
    count = lax.axis_size("blk")
    depth = count.bit_length() - 1
    all_bits = [1 << place for place in range(depth)]
    split = 1 + depth // 2
    img_bits = all_bits[1:split][::-1]
    txt_bits = (all_bits[:1] + all_bits[split:])[::-1]
    txt_bits[0] |= img_bits[0]
    imgs, txts = gathered(image_embeds, text_embeds, img_bits, txt_bits)
    img_parts, txt_parts, sums = tile_call(imgs, txts, log_temp.reshape(1, 1), bias.reshape(1, 1))
    img_parts, txt_parts = ([part[0] for part in parts] for parts in (img_parts, txt_parts))
    txt_keep, txt_recvs, others = returned(txt_parts, txt_bits, [], False)
    for bit in img_bits[:1] + txt_bits[1:] + img_bits[:0:-1]:
        sums = sums_call([sums, swapped(sums, bit)], others)
    img_keep, img_recvs, others = returned(img_parts, img_bits, others + [sums], True)
    sums_recv = swapped(sums, txt_bits[0])
    txt_recvs = held(txt_recvs, [], RETURN_COST)
    grad_text, grad_image, grad_bias, grad_temp = finish_call(
        sums,
        sums_recv,
        float(rows * count) * float(rows * count),
        [(text_embeds, txt_keep, txt_recvs), (image_embeds, img_keep, img_recvs)],
    )
    return (grad_image, grad_text, grad_temp.reshape(1), grad_bias.reshape(1))


def solution(mesh):
    in_specs = (P(("groups", "blk"), None), P(("groups", "blk"), None), P(), P())
    out_specs = (P(("groups", "blk"), None), P(("groups", "blk"), None), P("groups"), P("groups"))
    return jax.shard_map(shards, mesh=mesh, in_specs=in_specs, out_specs=out_specs, check_vma=False)
```

```python
import functools

import jax
import jax.numpy as jnp
from jax import lax
from jax.experimental import pallas as pl
from jax.experimental.pallas import tpu as pltpu
from jax.sharding import PartitionSpec as P

TILE_VMEM = 32 * 1024 * 1024
SMALL_VMEM = 4 * 1024 * 1024
GATHER_COST = 20_000_000_000
SUMS_COST = 300_000_000
RETURN_COST = 1_000_000_000
VMEM = pl.BlockSpec(memory_space=pltpu.VMEM)
ANY = pl.BlockSpec(memory_space=pl.ANY)


def swapped(x, bit):
    count = lax.axis_size("blk")
    return lax.ppermute(x, "blk", [(i, i ^ bit) for i in range(count)])


def held(values, others, cost=0):
    count = len(values)
    results = pl.pallas_call(
        lambda *refs: None,
        out_shape=[jax.ShapeDtypeStruct(value.shape, value.dtype) for value in values],
        in_specs=[ANY] * (count + len(others)),
        out_specs=[ANY] * count,
        input_output_aliases={place: place for place in range(count)},
        cost_estimate=pl.CostEstimate(flops=cost, bytes_accessed=0, transcendentals=0),
        compiler_params=pltpu.CompilerParams(vmem_limit_bytes=SMALL_VMEM),
    )(*values, *others)
    return list(results)


def unit_rows(values):
    wide = values.astype(jnp.float32)
    inverse = lax.rsqrt(jnp.sum(wide * wide, axis=1, keepdims=True) + 1e-06)
    return (wide * inverse, inverse)


def lane_sums(values):
    rows = jnp.sum(values.reshape(values.shape[0] // 8, 8, values.shape[1]), axis=0)
    total = rows[:, :128]
    for start in range(128, values.shape[1], 128):
        total = total + rows[:, start : start + 128]
    return total


def piece_kernel(value, *refs):
    unit = unit_rows(value[...])[0].astype(jnp.bfloat16)
    start = 0
    for piece in refs:
        piece[...] = unit[start : start + piece.shape[0]]
        start += piece.shape[0]


def piece_skip_kernel(count, value, *refs):
    piece_kernel(value, *refs[-count:])


def unit_pieces(value, cuts, others):
    rows, width = value.shape
    return pl.pallas_call(
        functools.partial(piece_skip_kernel, len(cuts)),
        out_shape=[jax.ShapeDtypeStruct((cut, width), jnp.bfloat16) for cut in cuts],
        in_specs=[VMEM] + [ANY] * len(others),
        out_specs=[VMEM] * len(cuts),
        compiler_params=pltpu.CompilerParams(vmem_limit_bytes=SMALL_VMEM),
        cost_estimate=pl.CostEstimate(
            flops=4 * value.size, bytes_accessed=4 * value.size, transcendentals=rows
        ),
    )(value, *others)


def gathered(image, text, img_bits, txt_bits):
    img_raw = [swapped(image, bit) for bit in img_bits]
    txt_raw = swapped(text, txt_bits[0])
    rows = image.shape[0]
    cuts = [rows * 5 // 8, rows * 3 // 8]
    imgs, txts = {}, {}
    others = []
    for place in reversed(range(1, len(img_bits))):
        imgs[1 << place] = unit_pieces(img_raw[place], cuts, others)
        others = imgs[1 << place][:1]
    txts[0] = unit_pieces(text, [rows], others)
    imgs[0] = unit_pieces(image, [rows], txts[0])
    for place in range(1, len(txt_bits)):
        txts[1 << place] = [swapped(txts[0][0], txt_bits[place])]
    imgs[1] = unit_pieces(img_raw[0], cuts, imgs[0])
    txts[1] = unit_pieces(txt_raw, [rows], imgs[1][:1])
    for offset in range(1 << len(img_bits)):
        if offset not in imgs:
            high = offset.bit_length() - 1
            low = (offset & -offset).bit_length() - 1
            imgs[offset] = [
                swapped(imgs[offset ^ 1 << high][0], img_bits[high]),
                swapped(imgs[offset ^ 1 << low][1], img_bits[low]),
            ]
    for offset in range(1 << len(txt_bits)):
        if offset not in txts:
            high = offset.bit_length() - 1
            txts[offset] = [swapped(txts[offset ^ 1 << high][0], txt_bits[high])]
    imgs = [imgs[offset] for offset in range(1 << len(img_bits))]
    txts = [txts[offset] for offset in range(1 << len(txt_bits))]
    last = held(imgs[-1][1:], [], GATHER_COST)
    imgs[-1] = held(imgs[-1][:1], last, GATHER_COST) + last
    txts[-1] = held(txts[-1], imgs[-1][:1])
    return imgs, txts


def store_part(part, start, outs, cuts, rows):
    for at in range(start // rows, (start + part.shape[0]) // rows):
        size = rows // cuts[at]
        for place in range(cuts[at]):
            out = outs[sum(cuts[:at]) + place]
            first = at * rows - start + place * size
            out[...] = part[first : first + size].astype(out.dtype)


def tile_kernel(img_places, txt_places, img_cuts, txt_cuts, rows, *refs):
    n_img, n_txt = len(img_places), len(txt_places)
    taken = 0
    sources = []
    for places in (img_places, txt_places):
        pieces = sum(places)
        sources.append(refs[taken : taken + pieces])
        taken += pieces
    log_temp, bias = refs[taken : taken + 2]
    taken += 2
    img_parts = refs[taken : taken + sum(img_cuts)]
    taken += sum(img_cuts)
    txt_parts = refs[taken : taken + sum(txt_cuts)]
    sums, img_b, txt_b, grad_b = refs[taken + sum(txt_cuts) :]
    for group, held in zip(sources, (img_b, txt_b)):
        start = 0
        for piece in group:
            end = start + piece.shape[0]
            held[start:end] = piece[...]
            start = end
    temp = jnp.exp(log_temp[...])
    shift_b = bias[...]
    sum_g = jnp.zeros((8, 128), jnp.float32)
    sum_gl = jnp.zeros((8, 128), jnp.float32)
    step = 2 * rows
    for start in range(0, n_img * rows, step):
        panel = img_b[start : start + step]
        cosine = lax.dot_general(
            panel, txt_b[...], (((1,), (1,)), ((), ())), preferred_element_type=jnp.float32
        )
        scaled = temp * cosine
        logits = scaled + shift_b
        if start == 0:
            at_row = lax.broadcasted_iota(jnp.int32, logits.shape, 0)
            at_col = lax.broadcasted_iota(jnp.int32, logits.shape, 1)
            own = jnp.logical_and(at_row == at_col, at_row < rows)
            sign = jnp.where(own, 1.0, -1.0)
            grads = -sign * jax.nn.sigmoid(-sign * logits)
        else:
            grads = jax.nn.sigmoid(logits)
        sum_g = sum_g + lane_sums(grads)
        sum_gl = sum_gl + lane_sums(grads * scaled)
        grads_b = grads.astype(jnp.bfloat16)
        grad_b[start : start + step] = grads_b
        part = jnp.dot(grads_b, txt_b[...], preferred_element_type=jnp.float32)
        store_part(temp * part, start, img_parts, img_cuts, rows)
    sums[0:8] = sum_g
    sums[8:16] = sum_gl
    for start in range(0, n_txt * rows, step):
        part = lax.dot_general(
            grad_b[:, start : start + step],
            img_b[...],
            (((0,), (0,)), ((), ())),
            preferred_element_type=jnp.float32,
        )
        store_part(temp * part, start, txt_parts, txt_cuts, rows)


def tile_call(imgs, txts, log_temp, bias):
    rows = sum(piece.shape[0] for piece in imgs[0])
    width = imgs[0][0].shape[1]
    n_img, n_txt = len(imgs), len(txts)
    flat = [piece for block in imgs + txts for piece in block]
    pairs = n_img * n_txt * rows * rows
    img_cuts = [1] * n_img
    txt_cuts = [1] * n_txt
    outs = []
    for cuts in (img_cuts, txt_cuts):
        for at, cut in enumerate(cuts):
            kind = jnp.float32 if at < len(cuts) // 2 else jnp.bfloat16
            outs += [jax.ShapeDtypeStruct((rows // cut, width), kind)] * cut
    results = pl.pallas_call(
        functools.partial(
            tile_kernel,
            [len(block) for block in imgs],
            [len(block) for block in txts],
            img_cuts,
            txt_cuts,
            rows,
        ),
        out_shape=outs + [jax.ShapeDtypeStruct((16, 128), jnp.float32)],
        in_specs=[VMEM] * (len(flat) + 2),
        out_specs=[VMEM] * (len(outs) + 1),
        scratch_shapes=[
            pltpu.VMEM((n_img * rows, width), jnp.bfloat16),
            pltpu.VMEM((n_txt * rows, width), jnp.bfloat16),
            pltpu.VMEM((n_img * rows, n_txt * rows), jnp.bfloat16),
        ],
        compiler_params=pltpu.CompilerParams(vmem_limit_bytes=TILE_VMEM),
        cost_estimate=pl.CostEstimate(
            flops=6 * pairs * width, bytes_accessed=0, transcendentals=2 * pairs
        ),
    )(*flat, log_temp, bias)
    results = list(results)
    sums = results.pop()
    parts = [[results.pop(0) for _ in range(cut)] for cut in img_cuts + txt_cuts]
    return parts[:n_img], parts[n_img:], sums


def finish_rows(value, keep, recvs, out):
    total = keep[...]
    for recv in recvs:
        total = total + recv[...].astype(jnp.float32)
    unit, inverse = unit_rows(value[...])
    along = jnp.sum(unit * total, axis=1, keepdims=True)
    out[...] = ((total - unit * along) * inverse).astype(jnp.bfloat16)


def finish_first_kernel(value, keep, *refs):
    finish_rows(value, keep, refs[:-2], refs[-2])
    refs[-1][...] = jnp.zeros(refs[-1].shape, jnp.float32)


def finish_first(value, keep, recvs):
    return pl.pallas_call(
        finish_first_kernel,
        out_shape=(
            jax.ShapeDtypeStruct(value.shape, jnp.bfloat16),
            jax.ShapeDtypeStruct((8, 128), jnp.float32),
        ),
        in_specs=[VMEM] * (2 + len(recvs)),
        out_specs=[VMEM] * 2,
        compiler_params=pltpu.CompilerParams(vmem_limit_bytes=SMALL_VMEM),
        cost_estimate=pl.CostEstimate(flops=RETURN_COST, bytes_accessed=0, transcendentals=0),
    )(value, keep, *recvs)


def finish_last_kernel(pairs, token, sums, sums_recv, value, keep, *refs):
    total = sums[...] + sums_recv[...]
    for place in range(2):
        whole = jnp.sum(total[8 * place : 8 * place + 8], axis=0, keepdims=True)
        refs[place - 2][...] = jnp.sum(whole, axis=1, keepdims=True) / pairs
    finish_rows(value, keep, refs[:-3], refs[-3])


def finish_last(token, sums, sums_recv, pairs, value, keep, recvs):
    return pl.pallas_call(
        functools.partial(finish_last_kernel, pairs),
        out_shape=[jax.ShapeDtypeStruct(value.shape, jnp.bfloat16)]
        + [jax.ShapeDtypeStruct((1, 1), jnp.float32)] * 2,
        in_specs=[ANY] + [VMEM] * (4 + len(recvs)),
        out_specs=[VMEM] * 3,
        compiler_params=pltpu.CompilerParams(vmem_limit_bytes=SMALL_VMEM),
    )(token, sums, sums_recv, value, keep, *recvs)


def add_kernel(keep, recv, *refs):
    out = refs[-1]
    out[...] = (keep[...] + recv[...].astype(jnp.float32)).astype(out.dtype)


def sums_kernel(first, second, *refs):
    refs[-1][...] = first[...] + second[...]


def sums_call(sums, others):
    return pl.pallas_call(
        sums_kernel,
        out_shape=jax.ShapeDtypeStruct(sums[0].shape, sums[0].dtype),
        in_specs=[VMEM] * len(sums) + [ANY] * len(others),
        out_specs=VMEM,
        compiler_params=pltpu.CompilerParams(vmem_limit_bytes=SMALL_VMEM),
        cost_estimate=pl.CostEstimate(flops=SUMS_COST, bytes_accessed=0, transcendentals=0),
    )(*sums, *others)


def add_call(keep, recv, dtype, others):
    return pl.pallas_call(
        add_kernel,
        out_shape=jax.ShapeDtypeStruct(keep.shape, dtype),
        in_specs=[VMEM] * 2 + [ANY] * len(others),
        out_specs=VMEM,
        compiler_params=pltpu.CompilerParams(vmem_limit_bytes=SMALL_VMEM),
        cost_estimate=pl.CostEstimate(
            flops=keep.size, bytes_accessed=keep.size, transcendentals=0
        ),
    )(keep, recv, *others)


def returned(parts, bits, others, wait):
    parts = dict(enumerate(parts))
    recvs = []
    for place in reversed(range(len(bits))):
        arrived = {}
        for offset in range(1, 1 << place):
            arrived[offset] = swapped(parts.pop(offset | 1 << place), bits[place])
        for offset, recv in arrived.items():
            kind = jnp.float32 if offset < 1 << (place - 1) else jnp.bfloat16
            parts[offset] = add_call(parts[offset], recv, kind, others)
            others = [parts[offset]]
        send = parts.pop(1 << place)
        if arrived and wait:
            send = held([send], others)[0]
        recvs.append(swapped(send, bits[place]))
    return parts[0], recvs, others


def shards(image_embeds, text_embeds, log_temp, bias):
    rows, width = image_embeds.shape
    count = lax.axis_size("blk")
    depth = count.bit_length() - 1
    all_bits = [1 << place for place in range(depth)]
    split = 1 + depth // 2
    img_bits = all_bits[1:split][::-1]
    txt_bits = (all_bits[:1] + all_bits[split:])[::-1]
    txt_bits[0] |= img_bits[0]
    imgs, txts = gathered(image_embeds, text_embeds, img_bits, txt_bits)
    img_parts, txt_parts, sums = tile_call(imgs, txts, log_temp.reshape(1, 1), bias.reshape(1, 1))
    img_parts, txt_parts = ([part[0] for part in parts] for parts in (img_parts, txt_parts))
    txt_keep, txt_recvs, others = returned(txt_parts, txt_bits, [], False)
    for bit in img_bits[:1] + txt_bits[1:] + img_bits[:0:-1]:
        sums = sums_call([sums, swapped(sums, bit)], others)
    img_keep, img_recvs, others = returned(img_parts, img_bits, others + [sums], True)
    sums_recv = swapped(sums, txt_bits[0])
    grad_text, token = finish_first(text_embeds, txt_keep, txt_recvs)
    pairs = float(rows * count) * float(rows * count)
    grad_image, grad_bias, grad_temp = finish_last(
        token, sums, sums_recv, pairs, image_embeds, img_keep, img_recvs
    )
    return (grad_image, grad_text, grad_temp.reshape(1), grad_bias.reshape(1))


def solution(mesh):
    in_specs = (P(("groups", "blk"), None), P(("groups", "blk"), None), P(), P())
    out_specs = (P(("groups", "blk"), None), P(("groups", "blk"), None), P("groups"), P("groups"))
    return jax.shard_map(shards, mesh=mesh, in_specs=in_specs, out_specs=out_specs, check_vma=False)
```

```python
import functools

import jax
import jax.numpy as jnp
from jax import lax
from jax.experimental import pallas as pl
from jax.experimental.pallas import tpu as pltpu
from jax.sharding import PartitionSpec as P

TILE_VMEM = 32 * 1024 * 1024
SMALL_VMEM = 4 * 1024 * 1024
GATHER_COST = 20_000_000_000
SUMS_COST = 300_000_000
RETURN_COST = 1_000_000_000
VMEM = pl.BlockSpec(memory_space=pltpu.VMEM)
ANY = pl.BlockSpec(memory_space=pl.ANY)


def swapped(x, bit):
    count = lax.axis_size("blk")
    return lax.ppermute(x, "blk", [(i, i ^ bit) for i in range(count)])


def held(values, others, cost=0):
    count = len(values)
    results = pl.pallas_call(
        lambda *refs: None,
        out_shape=[jax.ShapeDtypeStruct(value.shape, value.dtype) for value in values],
        in_specs=[ANY] * (count + len(others)),
        out_specs=[ANY] * count,
        input_output_aliases={place: place for place in range(count)},
        cost_estimate=pl.CostEstimate(flops=cost, bytes_accessed=0, transcendentals=0),
        compiler_params=pltpu.CompilerParams(vmem_limit_bytes=SMALL_VMEM),
    )(*values, *others)
    return list(results)


def unit_rows(values):
    wide = values.astype(jnp.float32)
    inverse = lax.rsqrt(jnp.sum(wide * wide, axis=1, keepdims=True) + 1e-06)
    return (wide * inverse, inverse)


def lane_sums(values):
    rows = jnp.sum(values.reshape(values.shape[0] // 8, 8, values.shape[1]), axis=0)
    total = rows[:, :128]
    for start in range(128, values.shape[1], 128):
        total = total + rows[:, start : start + 128]
    return total


def piece_kernel(value, *refs):
    unit = unit_rows(value[...])[0].astype(jnp.bfloat16)
    start = 0
    for piece in refs:
        piece[...] = unit[start : start + piece.shape[0]]
        start += piece.shape[0]


def piece_skip_kernel(count, value, *refs):
    piece_kernel(value, *refs[-count:])


def unit_pieces(value, cuts, others):
    rows, width = value.shape
    return pl.pallas_call(
        functools.partial(piece_skip_kernel, len(cuts)),
        out_shape=[jax.ShapeDtypeStruct((cut, width), jnp.bfloat16) for cut in cuts],
        in_specs=[VMEM] + [ANY] * len(others),
        out_specs=[VMEM] * len(cuts),
        compiler_params=pltpu.CompilerParams(vmem_limit_bytes=SMALL_VMEM),
        cost_estimate=pl.CostEstimate(
            flops=4 * value.size, bytes_accessed=4 * value.size, transcendentals=rows
        ),
    )(value, *others)


def gathered(image, text, img_bits, txt_bits):
    img_raw = [swapped(image, bit) for bit in img_bits]
    txt_raw = swapped(text, txt_bits[0])
    rows = image.shape[0]
    cuts = [rows * 5 // 8, rows * 3 // 8]
    imgs, txts = {}, {}
    others = []
    for place in reversed(range(1, len(img_bits))):
        imgs[1 << place] = unit_pieces(img_raw[place], cuts, others)
        others = imgs[1 << place][:1]
    txts[0] = unit_pieces(text, [rows], others)
    imgs[0] = unit_pieces(image, [rows], txts[0])
    for place in range(1, len(txt_bits)):
        txts[1 << place] = [swapped(txts[0][0], txt_bits[place])]
    imgs[1] = unit_pieces(img_raw[0], cuts, imgs[0])
    txts[1] = unit_pieces(txt_raw, [rows], imgs[1][:1])
    for offset in range(1 << len(img_bits)):
        if offset not in imgs:
            high = offset.bit_length() - 1
            low = (offset & -offset).bit_length() - 1
            imgs[offset] = [
                swapped(imgs[offset ^ 1 << high][0], img_bits[high]),
                swapped(imgs[offset ^ 1 << low][1], img_bits[low]),
            ]
    for offset in range(1 << len(txt_bits)):
        if offset not in txts:
            high = offset.bit_length() - 1
            txts[offset] = [swapped(txts[offset ^ 1 << high][0], txt_bits[high])]
    imgs = [imgs[offset] for offset in range(1 << len(img_bits))]
    txts = [txts[offset] for offset in range(1 << len(txt_bits))]
    last = held(imgs[-1][1:], [], GATHER_COST)
    imgs[-1] = held(imgs[-1][:1], last, GATHER_COST) + last
    txts[-1] = held(txts[-1], imgs[-1][:1])
    return imgs, txts


def store_part(part, start, outs, cuts, rows):
    for at in range(start // rows, (start + part.shape[0]) // rows):
        size = rows // cuts[at]
        for place in range(cuts[at]):
            out = outs[sum(cuts[:at]) + place]
            first = at * rows - start + place * size
            out[...] = part[first : first + size].astype(out.dtype)


def tile_kernel(img_places, txt_places, img_cuts, txt_cuts, rows, *refs):
    n_img, n_txt = len(img_places), len(txt_places)
    taken = 0
    sources = []
    for places in (img_places, txt_places):
        pieces = sum(places)
        sources.append(refs[taken : taken + pieces])
        taken += pieces
    log_temp, bias = refs[taken : taken + 2]
    taken += 2
    img_parts = refs[taken : taken + sum(img_cuts)]
    taken += sum(img_cuts)
    txt_parts = refs[taken : taken + sum(txt_cuts)]
    sums, scale, img_b, txt_b, grad_b = refs[taken + sum(txt_cuts) :]
    for group, held in zip(sources, (img_b, txt_b)):
        start = 0
        for piece in group:
            end = start + piece.shape[0]
            held[start:end] = piece[...]
            start = end
    temp = jnp.exp(log_temp[...])
    shift_b = bias[...]
    sum_g = jnp.zeros((8, 128), jnp.float32)
    sum_gl = jnp.zeros((8, 128), jnp.float32)
    step = 2 * rows
    for start in range(0, n_img * rows, step):
        panel = img_b[start : start + step]
        cosine = lax.dot_general(
            panel, txt_b[...], (((1,), (1,)), ((), ())), preferred_element_type=jnp.float32
        )
        scaled = temp * cosine
        logits = scaled + shift_b
        grads = jax.nn.sigmoid(logits)
        if start == 0:
            corner = (rows, rows)
            at_row = lax.broadcasted_iota(jnp.int32, corner, 0)
            at_col = lax.broadcasted_iota(jnp.int32, corner, 1)
            own = jnp.where(
                at_row == at_col, -jax.nn.sigmoid(-logits[:rows, :rows]), grads[:rows, :rows]
            )
            top = jnp.concatenate([own, grads[:rows, rows:]], axis=1)
            grads = jnp.concatenate([top, grads[rows:]], axis=0)
        sum_g = sum_g + lane_sums(grads)
        sum_gl = sum_gl + lane_sums(grads * scaled)
        grads_b = grads.astype(jnp.bfloat16)
        grad_b[start : start + step] = grads_b
        part = jnp.dot(grads_b, txt_b[...], preferred_element_type=jnp.float32)
        store_part(part, start, img_parts, img_cuts, rows)
    sums[0:8] = sum_g
    sums[8:16] = sum_gl
    scale[...] = jnp.broadcast_to(temp, scale.shape)
    for start in range(0, n_txt * rows, step):
        part = lax.dot_general(
            grad_b[:, start : start + step],
            img_b[...],
            (((0,), (0,)), ((), ())),
            preferred_element_type=jnp.float32,
        )
        store_part(part, start, txt_parts, txt_cuts, rows)


def tile_call(imgs, txts, log_temp, bias):
    rows = sum(piece.shape[0] for piece in imgs[0])
    width = imgs[0][0].shape[1]
    n_img, n_txt = len(imgs), len(txts)
    flat = [piece for block in imgs + txts for piece in block]
    pairs = n_img * n_txt * rows * rows
    img_cuts = [1] * n_img
    txt_cuts = [1] * n_txt
    outs = []
    for cuts in (img_cuts, txt_cuts):
        for at, cut in enumerate(cuts):
            kind = jnp.float32 if at < len(cuts) // 2 else jnp.bfloat16
            outs += [jax.ShapeDtypeStruct((rows // cut, width), kind)] * cut
    results = pl.pallas_call(
        functools.partial(
            tile_kernel,
            [len(block) for block in imgs],
            [len(block) for block in txts],
            img_cuts,
            txt_cuts,
            rows,
        ),
        out_shape=outs
        + [
            jax.ShapeDtypeStruct((16, 128), jnp.float32),
            jax.ShapeDtypeStruct((8, 128), jnp.float32),
        ],
        in_specs=[VMEM] * (len(flat) + 2),
        out_specs=[VMEM] * (len(outs) + 2),
        scratch_shapes=[
            pltpu.VMEM((n_img * rows, width), jnp.bfloat16),
            pltpu.VMEM((n_txt * rows, width), jnp.bfloat16),
            pltpu.VMEM((n_img * rows, n_txt * rows), jnp.bfloat16),
        ],
        compiler_params=pltpu.CompilerParams(vmem_limit_bytes=TILE_VMEM),
        cost_estimate=pl.CostEstimate(
            flops=6 * pairs * width, bytes_accessed=0, transcendentals=2 * pairs
        ),
    )(*flat, log_temp, bias)
    results = list(results)
    scale = results.pop()
    sums = results.pop()
    parts = [[results.pop(0) for _ in range(cut)] for cut in img_cuts + txt_cuts]
    return parts[:n_img], parts[n_img:], sums, scale


def finish_rows(scale, value, keep, recvs, out):
    total = keep[...]
    for recv in recvs:
        total = total + recv[...].astype(jnp.float32)
    unit, inverse = unit_rows(value[...])
    inverse = inverse * scale[:1, :1]
    along = jnp.sum(unit * total, axis=1, keepdims=True)
    out[...] = ((total - unit * along) * inverse).astype(jnp.bfloat16)


def finish_first_kernel(scale, value, keep, *refs):
    finish_rows(scale, value, keep, refs[:-2], refs[-2])
    refs[-1][...] = jnp.zeros(refs[-1].shape, jnp.float32)


def finish_first(scale, value, keep, recvs):
    return pl.pallas_call(
        finish_first_kernel,
        out_shape=(
            jax.ShapeDtypeStruct(value.shape, jnp.bfloat16),
            jax.ShapeDtypeStruct((8, 128), jnp.float32),
        ),
        in_specs=[VMEM] * (3 + len(recvs)),
        out_specs=[VMEM] * 2,
        compiler_params=pltpu.CompilerParams(vmem_limit_bytes=SMALL_VMEM),
        cost_estimate=pl.CostEstimate(flops=RETURN_COST, bytes_accessed=0, transcendentals=0),
    )(scale, value, keep, *recvs)


def finish_last_kernel(pairs, token, sums, sums_recv, scale, value, keep, *refs):
    total = sums[...] + sums_recv[...]
    for place in range(2):
        whole = jnp.sum(total[8 * place : 8 * place + 8], axis=0, keepdims=True)
        refs[place - 2][...] = jnp.sum(whole, axis=1, keepdims=True) / pairs
    finish_rows(scale, value, keep, refs[:-3], refs[-3])


def finish_last(token, sums, sums_recv, pairs, scale, value, keep, recvs):
    return pl.pallas_call(
        functools.partial(finish_last_kernel, pairs),
        out_shape=[jax.ShapeDtypeStruct(value.shape, jnp.bfloat16)]
        + [jax.ShapeDtypeStruct((1, 1), jnp.float32)] * 2,
        in_specs=[ANY] + [VMEM] * (5 + len(recvs)),
        out_specs=[VMEM] * 3,
        compiler_params=pltpu.CompilerParams(vmem_limit_bytes=SMALL_VMEM),
    )(token, sums, sums_recv, scale, value, keep, *recvs)


def add_kernel(keep, recv, *refs):
    out = refs[-1]
    out[...] = (keep[...] + recv[...].astype(jnp.float32)).astype(out.dtype)


def sums_kernel(first, second, *refs):
    refs[-1][...] = first[...] + second[...]


def sums_call(sums, others):
    return pl.pallas_call(
        sums_kernel,
        out_shape=jax.ShapeDtypeStruct(sums[0].shape, sums[0].dtype),
        in_specs=[VMEM] * len(sums) + [ANY] * len(others),
        out_specs=VMEM,
        compiler_params=pltpu.CompilerParams(vmem_limit_bytes=SMALL_VMEM),
        cost_estimate=pl.CostEstimate(flops=SUMS_COST, bytes_accessed=0, transcendentals=0),
    )(*sums, *others)


def add_call(keep, recv, dtype, others):
    return pl.pallas_call(
        add_kernel,
        out_shape=jax.ShapeDtypeStruct(keep.shape, dtype),
        in_specs=[VMEM] * 2 + [ANY] * len(others),
        out_specs=VMEM,
        compiler_params=pltpu.CompilerParams(vmem_limit_bytes=SMALL_VMEM),
        cost_estimate=pl.CostEstimate(
            flops=keep.size, bytes_accessed=keep.size, transcendentals=0
        ),
    )(keep, recv, *others)


def returned(parts, bits, others, wait):
    parts = dict(enumerate(parts))
    recvs = []
    for place in reversed(range(len(bits))):
        arrived = {}
        for offset in range(1, 1 << place):
            arrived[offset] = swapped(parts.pop(offset | 1 << place), bits[place])
        for offset, recv in arrived.items():
            kind = jnp.float32 if offset < 1 << (place - 1) else jnp.bfloat16
            parts[offset] = add_call(parts[offset], recv, kind, others)
            others = [parts[offset]]
        send = parts.pop(1 << place)
        if arrived and wait:
            send = held([send], others)[0]
        recvs.append(swapped(send, bits[place]))
    return parts[0], recvs, others


def shards(image_embeds, text_embeds, log_temp, bias):
    rows, width = image_embeds.shape
    count = lax.axis_size("blk")
    depth = count.bit_length() - 1
    all_bits = [1 << place for place in range(depth)]
    split = 1 + depth // 2
    img_bits = all_bits[1:split][::-1]
    txt_bits = (all_bits[:1] + all_bits[split:])[::-1]
    txt_bits[0] |= img_bits[0]
    imgs, txts = gathered(image_embeds, text_embeds, img_bits, txt_bits)
    img_parts, txt_parts, sums, scale = tile_call(
        imgs, txts, log_temp.reshape(1, 1), bias.reshape(1, 1)
    )
    img_parts, txt_parts = ([part[0] for part in parts] for parts in (img_parts, txt_parts))
    txt_keep, txt_recvs, others = returned(txt_parts, txt_bits, [], False)
    for bit in img_bits[:1] + txt_bits[1:] + img_bits[:0:-1]:
        sums = sums_call([sums, swapped(sums, bit)], others)
    img_keep, img_recvs, others = returned(img_parts, img_bits, others + [sums], True)
    sums_recv = swapped(sums, txt_bits[0])
    grad_text, token = finish_first(scale, text_embeds, txt_keep, txt_recvs)
    pairs = float(rows * count) * float(rows * count)
    grad_image, grad_bias, grad_temp = finish_last(
        token, sums, sums_recv, pairs, scale, image_embeds, img_keep, img_recvs
    )
    return (grad_image, grad_text, grad_temp.reshape(1), grad_bias.reshape(1))


def solution(mesh):
    in_specs = (P(("groups", "blk"), None), P(("groups", "blk"), None), P(), P())
    out_specs = (P(("groups", "blk"), None), P(("groups", "blk"), None), P("groups"), P("groups"))
    return jax.shard_map(shards, mesh=mesh, in_specs=in_specs, out_specs=out_specs, check_vma=False)
```

```python
import functools

import jax
import jax.numpy as jnp
from jax import lax
from jax.experimental import pallas as pl
from jax.experimental.pallas import tpu as pltpu
from jax.sharding import PartitionSpec as P

TILE_VMEM = 32 * 1024 * 1024
SMALL_VMEM = 4 * 1024 * 1024
GATHER_COST = 20_000_000_000
SUMS_COST = 300_000_000
RETURN_COST = 1_000_000_000
VMEM = pl.BlockSpec(memory_space=pltpu.VMEM)
ANY = pl.BlockSpec(memory_space=pl.ANY)


def swapped(x, bit):
    count = lax.axis_size("blk")
    return lax.ppermute(x, "blk", [(i, i ^ bit) for i in range(count)])


def held(values, others, cost=0):
    count = len(values)
    results = pl.pallas_call(
        lambda *refs: None,
        out_shape=[jax.ShapeDtypeStruct(value.shape, value.dtype) for value in values],
        in_specs=[ANY] * (count + len(others)),
        out_specs=[ANY] * count,
        input_output_aliases={place: place for place in range(count)},
        cost_estimate=pl.CostEstimate(flops=cost, bytes_accessed=0, transcendentals=0),
        compiler_params=pltpu.CompilerParams(vmem_limit_bytes=SMALL_VMEM),
    )(*values, *others)
    return list(results)


def unit_rows(values):
    wide = values.astype(jnp.float32)
    inverse = lax.rsqrt(jnp.sum(wide * wide, axis=1, keepdims=True) + 1e-06)
    return (wide * inverse, inverse)


def lane_sums(values):
    rows = jnp.sum(values.reshape(values.shape[0] // 8, 8, values.shape[1]), axis=0)
    total = rows[:, :128]
    for start in range(128, values.shape[1], 128):
        total = total + rows[:, start : start + 128]
    return total


def piece_kernel(value, *refs):
    unit = unit_rows(value[...])[0].astype(jnp.bfloat16)
    start = 0
    for piece in refs:
        piece[...] = unit[start : start + piece.shape[0]]
        start += piece.shape[0]


def piece_skip_kernel(count, value, *refs):
    piece_kernel(value, *refs[-count:])


def unit_pieces(value, cuts, others):
    rows, width = value.shape
    return pl.pallas_call(
        functools.partial(piece_skip_kernel, len(cuts)),
        out_shape=[jax.ShapeDtypeStruct((cut, width), jnp.bfloat16) for cut in cuts],
        in_specs=[VMEM] + [ANY] * len(others),
        out_specs=[VMEM] * len(cuts),
        compiler_params=pltpu.CompilerParams(vmem_limit_bytes=SMALL_VMEM),
        cost_estimate=pl.CostEstimate(
            flops=4 * value.size, bytes_accessed=4 * value.size, transcendentals=rows
        ),
    )(value, *others)


def gathered(image, text, img_bits, txt_bits):
    img_raw = [swapped(image, bit) for bit in img_bits]
    txt_raw = swapped(text, txt_bits[0])
    rows = image.shape[0]
    cuts = [rows * 3 // 4, rows // 4]
    imgs, txts = {}, {}
    others = []
    for place in reversed(range(1, len(img_bits))):
        imgs[1 << place] = unit_pieces(img_raw[place], cuts, others)
        others = imgs[1 << place][:1]
    txts[0] = unit_pieces(text, [rows], others)
    imgs[0] = unit_pieces(image, [rows], txts[0])
    for place in range(1, len(txt_bits)):
        txts[1 << place] = [swapped(txts[0][0], txt_bits[place])]
    imgs[1] = unit_pieces(img_raw[0], cuts, imgs[0])
    txts[1] = unit_pieces(txt_raw, [rows], imgs[1][:1])
    for offset in range(1 << len(img_bits)):
        if offset not in imgs:
            high = offset.bit_length() - 1
            low = (offset & -offset).bit_length() - 1
            imgs[offset] = [
                swapped(imgs[offset ^ 1 << high][0], img_bits[high]),
                swapped(imgs[offset ^ 1 << low][1], img_bits[low]),
            ]
    for offset in range(1 << len(txt_bits)):
        if offset not in txts:
            high = offset.bit_length() - 1
            txts[offset] = [swapped(txts[offset ^ 1 << high][0], txt_bits[high])]
    imgs = [imgs[offset] for offset in range(1 << len(img_bits))]
    txts = [txts[offset] for offset in range(1 << len(txt_bits))]
    last = held(imgs[-1][1:], [], GATHER_COST)
    imgs[-1] = held(imgs[-1][:1], last, GATHER_COST) + last
    txts[-1] = held(txts[-1], imgs[-1][:1])
    return imgs, txts


def store_part(part, start, outs, cuts, rows):
    for at in range(start // rows, (start + part.shape[0]) // rows):
        size = rows // cuts[at]
        for place in range(cuts[at]):
            out = outs[sum(cuts[:at]) + place]
            first = at * rows - start + place * size
            out[...] = part[first : first + size].astype(out.dtype)


def tile_kernel(img_places, txt_places, img_cuts, txt_cuts, rows, *refs):
    n_img, n_txt = len(img_places), len(txt_places)
    taken = 0
    sources = []
    for places in (img_places, txt_places):
        pieces = sum(places)
        sources.append(refs[taken : taken + pieces])
        taken += pieces
    log_temp, bias = refs[taken : taken + 2]
    taken += 2
    img_parts = refs[taken : taken + sum(img_cuts)]
    taken += sum(img_cuts)
    txt_parts = refs[taken : taken + sum(txt_cuts)]
    sums, img_b, txt_b, grad_b = refs[taken + sum(txt_cuts) :]
    for group, held in zip(sources, (img_b, txt_b)):
        start = 0
        for piece in group:
            end = start + piece.shape[0]
            held[start:end] = piece[...]
            start = end
    temp = jnp.exp(log_temp[...])
    shift_b = bias[...]
    sum_g = jnp.zeros((8, 128), jnp.float32)
    sum_gl = jnp.zeros((8, 128), jnp.float32)
    step = 2 * rows
    for start in range(0, n_img * rows, step):
        panel = img_b[start : start + step]
        cosine = lax.dot_general(
            panel, txt_b[...], (((1,), (1,)), ((), ())), preferred_element_type=jnp.float32
        )
        scaled = temp * cosine
        logits = scaled + shift_b
        if start == 0:
            at_row = lax.broadcasted_iota(jnp.int32, logits.shape, 0)
            at_col = lax.broadcasted_iota(jnp.int32, logits.shape, 1)
            own = jnp.logical_and(at_row == at_col, at_row < rows)
            sign = jnp.where(own, 1.0, -1.0)
            grads = -sign * jax.nn.sigmoid(-sign * logits)
        else:
            grads = jax.nn.sigmoid(logits)
        sum_g = sum_g + lane_sums(grads)
        sum_gl = sum_gl + lane_sums(grads * scaled)
        grads_b = grads.astype(jnp.bfloat16)
        grad_b[start : start + step] = grads_b
        part = jnp.dot(grads_b, txt_b[...], preferred_element_type=jnp.float32)
        store_part(temp * part, start, img_parts, img_cuts, rows)
    sums[0:8] = sum_g
    sums[8:16] = sum_gl
    for start in range(0, n_txt * rows, step):
        part = lax.dot_general(
            grad_b[:, start : start + step],
            img_b[...],
            (((0,), (0,)), ((), ())),
            preferred_element_type=jnp.float32,
        )
        store_part(temp * part, start, txt_parts, txt_cuts, rows)


def tile_call(imgs, txts, log_temp, bias):
    rows = sum(piece.shape[0] for piece in imgs[0])
    width = imgs[0][0].shape[1]
    n_img, n_txt = len(imgs), len(txts)
    flat = [piece for block in imgs + txts for piece in block]
    pairs = n_img * n_txt * rows * rows
    img_cuts = [1] * n_img
    txt_cuts = [1] * n_txt
    outs = []
    for cuts in (img_cuts, txt_cuts):
        for at, cut in enumerate(cuts):
            kind = jnp.float32 if at < len(cuts) // 2 else jnp.bfloat16
            outs += [jax.ShapeDtypeStruct((rows // cut, width), kind)] * cut
    results = pl.pallas_call(
        functools.partial(
            tile_kernel,
            [len(block) for block in imgs],
            [len(block) for block in txts],
            img_cuts,
            txt_cuts,
            rows,
        ),
        out_shape=outs + [jax.ShapeDtypeStruct((16, 128), jnp.float32)],
        in_specs=[VMEM] * (len(flat) + 2),
        out_specs=[VMEM] * (len(outs) + 1),
        scratch_shapes=[
            pltpu.VMEM((n_img * rows, width), jnp.bfloat16),
            pltpu.VMEM((n_txt * rows, width), jnp.bfloat16),
            pltpu.VMEM((n_img * rows, n_txt * rows), jnp.bfloat16),
        ],
        compiler_params=pltpu.CompilerParams(vmem_limit_bytes=TILE_VMEM),
        cost_estimate=pl.CostEstimate(
            flops=6 * pairs * width, bytes_accessed=0, transcendentals=2 * pairs
        ),
    )(*flat, log_temp, bias)
    results = list(results)
    sums = results.pop()
    parts = [[results.pop(0) for _ in range(cut)] for cut in img_cuts + txt_cuts]
    return parts[:n_img], parts[n_img:], sums


def finish_rows(value, keep, recvs, out):
    total = keep[...]
    for recv in recvs:
        total = total + recv[...].astype(jnp.float32)
    unit, inverse = unit_rows(value[...])
    along = jnp.sum(unit * total, axis=1, keepdims=True)
    out[...] = ((total - unit * along) * inverse).astype(jnp.bfloat16)


def finish_first_kernel(value, keep, *refs):
    finish_rows(value, keep, refs[:-2], refs[-2])
    refs[-1][...] = jnp.zeros(refs[-1].shape, jnp.float32)


def finish_first(value, keep, recvs):
    return pl.pallas_call(
        finish_first_kernel,
        out_shape=(
            jax.ShapeDtypeStruct(value.shape, jnp.bfloat16),
            jax.ShapeDtypeStruct((8, 128), jnp.float32),
        ),
        in_specs=[VMEM] * (2 + len(recvs)),
        out_specs=[VMEM] * 2,
        compiler_params=pltpu.CompilerParams(vmem_limit_bytes=SMALL_VMEM),
        cost_estimate=pl.CostEstimate(flops=RETURN_COST, bytes_accessed=0, transcendentals=0),
    )(value, keep, *recvs)


def finish_last_kernel(pairs, token, sums, sums_recv, value, keep, *refs):
    total = sums[...] + sums_recv[...]
    for place in range(2):
        whole = jnp.sum(total[8 * place : 8 * place + 8], axis=0, keepdims=True)
        refs[place - 2][...] = jnp.sum(whole, axis=1, keepdims=True) / pairs
    finish_rows(value, keep, refs[:-3], refs[-3])


def finish_last(token, sums, sums_recv, pairs, value, keep, recvs):
    return pl.pallas_call(
        functools.partial(finish_last_kernel, pairs),
        out_shape=[jax.ShapeDtypeStruct(value.shape, jnp.bfloat16)]
        + [jax.ShapeDtypeStruct((1, 1), jnp.float32)] * 2,
        in_specs=[ANY] + [VMEM] * (4 + len(recvs)),
        out_specs=[VMEM] * 3,
        compiler_params=pltpu.CompilerParams(vmem_limit_bytes=SMALL_VMEM),
    )(token, sums, sums_recv, value, keep, *recvs)


def add_kernel(keep, recv, *refs):
    out = refs[-1]
    out[...] = (keep[...] + recv[...].astype(jnp.float32)).astype(out.dtype)


def sums_kernel(first, second, *refs):
    refs[-1][...] = first[...] + second[...]


def sums_call(sums, others):
    return pl.pallas_call(
        sums_kernel,
        out_shape=jax.ShapeDtypeStruct(sums[0].shape, sums[0].dtype),
        in_specs=[VMEM] * len(sums) + [ANY] * len(others),
        out_specs=VMEM,
        compiler_params=pltpu.CompilerParams(vmem_limit_bytes=SMALL_VMEM),
        cost_estimate=pl.CostEstimate(flops=SUMS_COST, bytes_accessed=0, transcendentals=0),
    )(*sums, *others)


def add_call(keep, recv, dtype, others):
    return pl.pallas_call(
        add_kernel,
        out_shape=jax.ShapeDtypeStruct(keep.shape, dtype),
        in_specs=[VMEM] * 2 + [ANY] * len(others),
        out_specs=VMEM,
        compiler_params=pltpu.CompilerParams(vmem_limit_bytes=SMALL_VMEM),
        cost_estimate=pl.CostEstimate(
            flops=keep.size, bytes_accessed=keep.size, transcendentals=0
        ),
    )(keep, recv, *others)


def returned(parts, bits, others, wait):
    parts = dict(enumerate(parts))
    recvs = []
    for place in reversed(range(len(bits))):
        arrived = {}
        for offset in range(1, 1 << place):
            arrived[offset] = swapped(parts.pop(offset | 1 << place), bits[place])
        for offset, recv in arrived.items():
            kind = jnp.float32 if offset < 1 << (place - 1) else jnp.bfloat16
            parts[offset] = add_call(parts[offset], recv, kind, others)
            others = [parts[offset]]
        send = parts.pop(1 << place)
        if arrived and wait:
            send = held([send], others)[0]
        recvs.append(swapped(send, bits[place]))
    return parts[0], recvs, others


def shards(image_embeds, text_embeds, log_temp, bias):
    rows, width = image_embeds.shape
    count = lax.axis_size("blk")
    depth = count.bit_length() - 1
    all_bits = [1 << place for place in range(depth)]
    split = 1 + depth // 2
    img_bits = all_bits[1:split][::-1]
    txt_bits = (all_bits[:1] + all_bits[split:])[::-1]
    txt_bits[0] |= img_bits[0]
    imgs, txts = gathered(image_embeds, text_embeds, img_bits, txt_bits)
    img_parts, txt_parts, sums = tile_call(imgs, txts, log_temp.reshape(1, 1), bias.reshape(1, 1))
    img_parts, txt_parts = ([part[0] for part in parts] for parts in (img_parts, txt_parts))
    txt_keep, txt_recvs, others = returned(txt_parts, txt_bits, [], False)
    for bit in img_bits[:1] + txt_bits[1:] + img_bits[:0:-1]:
        sums = sums_call([sums, swapped(sums, bit)], others)
    img_keep, img_recvs, others = returned(img_parts, img_bits, others + [sums], True)
    sums_recv = swapped(sums, txt_bits[0])
    grad_text, token = finish_first(text_embeds, txt_keep, txt_recvs)
    pairs = float(rows * count) * float(rows * count)
    grad_image, grad_bias, grad_temp = finish_last(
        token, sums, sums_recv, pairs, image_embeds, img_keep, img_recvs
    )
    return (grad_image, grad_text, grad_temp.reshape(1), grad_bias.reshape(1))


def solution(mesh):
    in_specs = (P(("groups", "blk"), None), P(("groups", "blk"), None), P(), P())
    out_specs = (P(("groups", "blk"), None), P(("groups", "blk"), None), P("groups"), P("groups"))
    return jax.shard_map(shards, mesh=mesh, in_specs=in_specs, out_specs=out_specs, check_vma=False)
```

```python
import functools

import jax
import jax.numpy as jnp
from jax import lax
from jax.experimental import pallas as pl
from jax.experimental.pallas import tpu as pltpu
from jax.sharding import PartitionSpec as P

TILE_VMEM = 32 * 1024 * 1024
SMALL_VMEM = 4 * 1024 * 1024
GATHER_COST = 20_000_000_000
SUMS_COST = 300_000_000
RETURN_COST = 1_000_000_000
VMEM = pl.BlockSpec(memory_space=pltpu.VMEM)
ANY = pl.BlockSpec(memory_space=pl.ANY)


def swapped(x, bit):
    count = lax.axis_size("blk")
    return lax.ppermute(x, "blk", [(i, i ^ bit) for i in range(count)])


def held(values, others, cost=0):
    count = len(values)
    results = pl.pallas_call(
        lambda *refs: None,
        out_shape=[jax.ShapeDtypeStruct(value.shape, value.dtype) for value in values],
        in_specs=[ANY] * (count + len(others)),
        out_specs=[ANY] * count,
        input_output_aliases={place: place for place in range(count)},
        cost_estimate=pl.CostEstimate(flops=cost, bytes_accessed=0, transcendentals=0),
        compiler_params=pltpu.CompilerParams(vmem_limit_bytes=SMALL_VMEM),
    )(*values, *others)
    return list(results)


def unit_rows(values):
    wide = values.astype(jnp.float32)
    inverse = lax.rsqrt(jnp.sum(wide * wide, axis=1, keepdims=True) + 1e-06)
    return (wide * inverse, inverse)


def lane_sums(values):
    rows = jnp.sum(values.reshape(values.shape[0] // 8, 8, values.shape[1]), axis=0)
    total = rows[:, :128]
    for start in range(128, values.shape[1], 128):
        total = total + rows[:, start : start + 128]
    return total


def piece_kernel(value, *refs):
    unit = unit_rows(value[...])[0].astype(jnp.bfloat16)
    start = 0
    for piece in refs:
        piece[...] = unit[start : start + piece.shape[0]]
        start += piece.shape[0]


def piece_skip_kernel(count, value, *refs):
    piece_kernel(value, *refs[-count:])


def unit_pieces(value, cuts, others):
    rows, width = value.shape
    return pl.pallas_call(
        functools.partial(piece_skip_kernel, len(cuts)),
        out_shape=[jax.ShapeDtypeStruct((cut, width), jnp.bfloat16) for cut in cuts],
        in_specs=[VMEM] + [ANY] * len(others),
        out_specs=[VMEM] * len(cuts),
        compiler_params=pltpu.CompilerParams(vmem_limit_bytes=SMALL_VMEM),
        cost_estimate=pl.CostEstimate(
            flops=4 * value.size, bytes_accessed=4 * value.size, transcendentals=rows
        ),
    )(value, *others)


def gathered(image, text, img_bits, txt_bits):
    img_raw = [swapped(image, bit) for bit in img_bits]
    txt_raw = swapped(text, txt_bits[0])
    rows = image.shape[0]
    cuts = [rows // 2, rows // 2]
    imgs, txts = {}, {}
    others = []
    for place in reversed(range(1, len(img_bits))):
        imgs[1 << place] = unit_pieces(img_raw[place], cuts, others)
        others = imgs[1 << place][:1]
    txts[0] = unit_pieces(text, [rows], others)
    imgs[0] = unit_pieces(image, [rows], txts[0])
    for place in range(1, len(txt_bits)):
        txts[1 << place] = [swapped(txts[0][0], txt_bits[place])]
    imgs[1] = unit_pieces(img_raw[0], cuts, imgs[0])
    txts[1] = unit_pieces(txt_raw, [rows], imgs[1][:1])
    for offset in range(1 << len(img_bits)):
        if offset not in imgs:
            high = offset.bit_length() - 1
            low = (offset & -offset).bit_length() - 1
            imgs[offset] = [
                swapped(imgs[offset ^ 1 << high][0], img_bits[high]),
                swapped(imgs[offset ^ 1 << low][1], img_bits[low]),
            ]
    for offset in range(1 << len(txt_bits)):
        if offset not in txts:
            high = offset.bit_length() - 1
            txts[offset] = [swapped(txts[offset ^ 1 << high][0], txt_bits[high])]
    imgs = [imgs[offset] for offset in range(1 << len(img_bits))]
    txts = [txts[offset] for offset in range(1 << len(txt_bits))]
    last = held(imgs[-1][1:], [], GATHER_COST)
    imgs[-1] = held(imgs[-1][:1], last, GATHER_COST) + last
    txts[-1] = held(txts[-1], imgs[-1][:1])
    return imgs, txts


def store_part(part, start, outs, cuts, rows):
    for at in range(start // rows, (start + part.shape[0]) // rows):
        size = rows // cuts[at]
        for place in range(cuts[at]):
            out = outs[sum(cuts[:at]) + place]
            first = at * rows - start + place * size
            out[...] = part[first : first + size].astype(out.dtype)


def tile_kernel(img_places, txt_places, img_cuts, txt_cuts, rows, *refs):
    n_img, n_txt = len(img_places), len(txt_places)
    taken = 0
    sources = []
    for places in (img_places, txt_places):
        pieces = sum(places)
        sources.append(refs[taken : taken + pieces])
        taken += pieces
    log_temp, bias = refs[taken : taken + 2]
    taken += 2
    img_parts = refs[taken : taken + sum(img_cuts)]
    taken += sum(img_cuts)
    txt_parts = refs[taken : taken + sum(txt_cuts)]
    sums, img_b, txt_b, grad_b = refs[taken + sum(txt_cuts) :]
    for group, held in zip(sources, (img_b, txt_b)):
        start = 0
        for piece in group:
            end = start + piece.shape[0]
            held[start:end] = piece[...]
            start = end
    temp = jnp.exp(log_temp[...])
    shift_b = bias[...]
    sum_g = jnp.zeros((8, 128), jnp.float32)
    sum_gl = jnp.zeros((8, 128), jnp.float32)
    step = 2 * rows
    for start in range(0, n_img * rows, step):
        panel = img_b[start : start + step]
        cosine = lax.dot_general(
            panel, txt_b[...], (((1,), (1,)), ((), ())), preferred_element_type=jnp.float32
        )
        scaled = temp * cosine
        logits = scaled + shift_b
        if start == 0:
            at_row = lax.broadcasted_iota(jnp.int32, logits.shape, 0)
            at_col = lax.broadcasted_iota(jnp.int32, logits.shape, 1)
            own = jnp.logical_and(at_row == at_col, at_row < rows)
            sign = jnp.where(own, 1.0, -1.0)
            grads = -sign * jax.nn.sigmoid(-sign * logits)
        else:
            grads = jax.nn.sigmoid(logits)
        sum_g = sum_g + lane_sums(grads)
        sum_gl = sum_gl + lane_sums(grads * scaled)
        grads_b = grads.astype(jnp.bfloat16)
        grad_b[start : start + step] = grads_b
        part = jnp.dot(grads_b, txt_b[...], preferred_element_type=jnp.float32)
        store_part(temp * part, start, img_parts, img_cuts, rows)
    sums[0:8] = sum_g
    sums[8:16] = sum_gl
    for start in range(0, n_txt * rows, step):
        part = lax.dot_general(
            grad_b[:, start : start + step],
            img_b[...],
            (((0,), (0,)), ((), ())),
            preferred_element_type=jnp.float32,
        )
        store_part(temp * part, start, txt_parts, txt_cuts, rows)


def tile_call(imgs, txts, log_temp, bias):
    rows = sum(piece.shape[0] for piece in imgs[0])
    width = imgs[0][0].shape[1]
    n_img, n_txt = len(imgs), len(txts)
    flat = [piece for block in imgs + txts for piece in block]
    pairs = n_img * n_txt * rows * rows
    img_cuts = [1] * n_img
    txt_cuts = [1] * n_txt
    outs = []
    for cuts in (img_cuts, txt_cuts):
        for at, cut in enumerate(cuts):
            kind = jnp.float32 if at < len(cuts) // 2 else jnp.bfloat16
            outs += [jax.ShapeDtypeStruct((rows // cut, width), kind)] * cut
    results = pl.pallas_call(
        functools.partial(
            tile_kernel,
            [len(block) for block in imgs],
            [len(block) for block in txts],
            img_cuts,
            txt_cuts,
            rows,
        ),
        out_shape=outs + [jax.ShapeDtypeStruct((16, 128), jnp.float32)],
        in_specs=[VMEM] * (len(flat) + 2),
        out_specs=[VMEM] * (len(outs) + 1),
        scratch_shapes=[
            pltpu.VMEM((n_img * rows, width), jnp.bfloat16),
            pltpu.VMEM((n_txt * rows, width), jnp.bfloat16),
            pltpu.VMEM((n_img * rows, n_txt * rows), jnp.bfloat16),
        ],
        compiler_params=pltpu.CompilerParams(vmem_limit_bytes=TILE_VMEM),
        cost_estimate=pl.CostEstimate(
            flops=6 * pairs * width, bytes_accessed=0, transcendentals=2 * pairs
        ),
    )(*flat, log_temp, bias)
    results = list(results)
    sums = results.pop()
    parts = [[results.pop(0) for _ in range(cut)] for cut in img_cuts + txt_cuts]
    return parts[:n_img], parts[n_img:], sums


def finish_rows(value, keep, recvs, out):
    total = keep[...]
    for recv in recvs:
        total = total + recv[...].astype(jnp.float32)
    unit, inverse = unit_rows(value[...])
    along = jnp.sum(unit * total, axis=1, keepdims=True)
    out[...] = ((total - unit * along) * inverse).astype(jnp.bfloat16)


def finish_first_kernel(value, keep, *refs):
    finish_rows(value, keep, refs[:-2], refs[-2])
    refs[-1][...] = jnp.zeros(refs[-1].shape, jnp.float32)


def finish_first(value, keep, recvs):
    return pl.pallas_call(
        finish_first_kernel,
        out_shape=(
            jax.ShapeDtypeStruct(value.shape, jnp.bfloat16),
            jax.ShapeDtypeStruct((8, 128), jnp.float32),
        ),
        in_specs=[VMEM] * (2 + len(recvs)),
        out_specs=[VMEM] * 2,
        compiler_params=pltpu.CompilerParams(vmem_limit_bytes=SMALL_VMEM),
        cost_estimate=pl.CostEstimate(flops=RETURN_COST, bytes_accessed=0, transcendentals=0),
    )(value, keep, *recvs)


def finish_last_kernel(pairs, token, sums, sums_recv, value, keep, *refs):
    total = sums[...] + sums_recv[...]
    for place in range(2):
        whole = jnp.sum(total[8 * place : 8 * place + 8], axis=0, keepdims=True)
        refs[place - 2][...] = jnp.sum(whole, axis=1, keepdims=True) / pairs
    finish_rows(value, keep, refs[:-3], refs[-3])


def finish_last(token, sums, sums_recv, pairs, value, keep, recvs):
    return pl.pallas_call(
        functools.partial(finish_last_kernel, pairs),
        out_shape=[jax.ShapeDtypeStruct(value.shape, jnp.bfloat16)]
        + [jax.ShapeDtypeStruct((1, 1), jnp.float32)] * 2,
        in_specs=[ANY] + [VMEM] * (4 + len(recvs)),
        out_specs=[VMEM] * 3,
        compiler_params=pltpu.CompilerParams(vmem_limit_bytes=SMALL_VMEM),
    )(token, sums, sums_recv, value, keep, *recvs)


def add_kernel(keep, recv, *refs):
    out = refs[-1]
    out[...] = (keep[...] + recv[...].astype(jnp.float32)).astype(out.dtype)


def sums_kernel(first, second, *refs):
    refs[-1][...] = first[...] + second[...]


def sums_call(sums, others):
    return pl.pallas_call(
        sums_kernel,
        out_shape=jax.ShapeDtypeStruct(sums[0].shape, sums[0].dtype),
        in_specs=[VMEM] * len(sums) + [ANY] * len(others),
        out_specs=VMEM,
        compiler_params=pltpu.CompilerParams(vmem_limit_bytes=SMALL_VMEM),
        cost_estimate=pl.CostEstimate(flops=SUMS_COST, bytes_accessed=0, transcendentals=0),
    )(*sums, *others)


def add_call(keep, recv, dtype, others):
    return pl.pallas_call(
        add_kernel,
        out_shape=jax.ShapeDtypeStruct(keep.shape, dtype),
        in_specs=[VMEM] * 2 + [ANY] * len(others),
        out_specs=VMEM,
        compiler_params=pltpu.CompilerParams(vmem_limit_bytes=SMALL_VMEM),
        cost_estimate=pl.CostEstimate(
            flops=keep.size, bytes_accessed=keep.size, transcendentals=0
        ),
    )(keep, recv, *others)


def returned(parts, bits, others, wait):
    parts = dict(enumerate(parts))
    recvs = []
    for place in reversed(range(len(bits))):
        arrived = {}
        for offset in range(1, 1 << place):
            arrived[offset] = swapped(parts.pop(offset | 1 << place), bits[place])
        for offset, recv in arrived.items():
            kind = jnp.float32 if offset < 1 << (place - 1) else jnp.bfloat16
            parts[offset] = add_call(parts[offset], recv, kind, others)
            others = [parts[offset]]
        send = parts.pop(1 << place)
        if arrived and wait:
            send = held([send], others)[0]
        recvs.append(swapped(send, bits[place]))
    return parts[0], recvs, others


def shards(image_embeds, text_embeds, log_temp, bias):
    rows, width = image_embeds.shape
    count = lax.axis_size("blk")
    depth = count.bit_length() - 1
    all_bits = [1 << place for place in range(depth)]
    split = 1 + depth // 2
    img_bits = all_bits[1:split][::-1]
    txt_bits = (all_bits[:1] + all_bits[split:])[::-1]
    txt_bits[0] |= img_bits[0]
    imgs, txts = gathered(image_embeds, text_embeds, img_bits, txt_bits)
    img_parts, txt_parts, sums = tile_call(imgs, txts, log_temp.reshape(1, 1), bias.reshape(1, 1))
    img_parts, txt_parts = ([part[0] for part in parts] for parts in (img_parts, txt_parts))
    txt_keep, txt_recvs, others = returned(txt_parts, txt_bits, [], False)
    for bit in img_bits[:1] + txt_bits[1:] + img_bits[:0:-1]:
        sums = sums_call([sums, swapped(sums, bit)], others)
    img_keep, img_recvs, others = returned(img_parts, img_bits, others + [sums], True)
    sums_recv = swapped(sums, txt_bits[0])
    grad_text, token = finish_first(text_embeds, txt_keep, txt_recvs)
    pairs = float(rows * count) * float(rows * count)
    grad_image, grad_bias, grad_temp = finish_last(
        token, sums, sums_recv, pairs, image_embeds, img_keep, img_recvs
    )
    return (grad_image, grad_text, grad_temp.reshape(1), grad_bias.reshape(1))


def solution(mesh):
    in_specs = (P(("groups", "blk"), None), P(("groups", "blk"), None), P(), P())
    out_specs = (P(("groups", "blk"), None), P(("groups", "blk"), None), P("groups"), P("groups"))
    return jax.shard_map(shards, mesh=mesh, in_specs=in_specs, out_specs=out_specs, check_vma=False)
```

```python
import functools

import jax
import jax.numpy as jnp
from jax import lax
from jax.experimental import pallas as pl
from jax.experimental.pallas import tpu as pltpu
from jax.sharding import PartitionSpec as P

TILE_VMEM = 32 * 1024 * 1024
SMALL_VMEM = 4 * 1024 * 1024
GATHER_COST = 20_000_000_000
SUMS_COST = 300_000_000
RETURN_COST = 1_000_000_000
VMEM = pl.BlockSpec(memory_space=pltpu.VMEM)
ANY = pl.BlockSpec(memory_space=pl.ANY)


def swapped(x, bit):
    count = lax.axis_size("blk")
    return lax.ppermute(x, "blk", [(i, i ^ bit) for i in range(count)])


def held(values, others, cost=0):
    count = len(values)
    results = pl.pallas_call(
        lambda *refs: None,
        out_shape=[jax.ShapeDtypeStruct(value.shape, value.dtype) for value in values],
        in_specs=[ANY] * (count + len(others)),
        out_specs=[ANY] * count,
        input_output_aliases={place: place for place in range(count)},
        cost_estimate=pl.CostEstimate(flops=cost, bytes_accessed=0, transcendentals=0),
        compiler_params=pltpu.CompilerParams(vmem_limit_bytes=SMALL_VMEM),
    )(*values, *others)
    return list(results)


def unit_rows(values):
    wide = values.astype(jnp.float32)
    inverse = lax.rsqrt(jnp.sum(wide * wide, axis=1, keepdims=True) + 1e-06)
    return (wide * inverse, inverse)


def lane_sums(values):
    rows = jnp.sum(values.reshape(values.shape[0] // 8, 8, values.shape[1]), axis=0)
    total = rows[:, :128]
    for start in range(128, values.shape[1], 128):
        total = total + rows[:, start : start + 128]
    return total


def piece_kernel(value, *refs):
    unit = unit_rows(value[...])[0].astype(jnp.bfloat16)
    start = 0
    for piece in refs:
        piece[...] = unit[start : start + piece.shape[0]]
        start += piece.shape[0]


def piece_skip_kernel(count, value, *refs):
    piece_kernel(value, *refs[-count:])


def unit_pieces(value, cuts, others):
    rows, width = value.shape
    return pl.pallas_call(
        functools.partial(piece_skip_kernel, len(cuts)),
        out_shape=[jax.ShapeDtypeStruct((cut, width), jnp.bfloat16) for cut in cuts],
        in_specs=[VMEM] + [ANY] * len(others),
        out_specs=[VMEM] * len(cuts),
        compiler_params=pltpu.CompilerParams(vmem_limit_bytes=SMALL_VMEM),
        cost_estimate=pl.CostEstimate(
            flops=4 * value.size, bytes_accessed=4 * value.size, transcendentals=rows
        ),
    )(value, *others)


def gathered(image, text, img_bits, txt_bits):
    img_raw = [swapped(image, bit) for bit in img_bits]
    txt_raw = swapped(text, txt_bits[0])
    rows = image.shape[0]
    cuts = [rows * 3 // 8, rows * 5 // 8]
    imgs, txts = {}, {}
    others = []
    for place in reversed(range(1, len(img_bits))):
        imgs[1 << place] = unit_pieces(img_raw[place], cuts, others)
        others = imgs[1 << place][:1]
    txts[0] = unit_pieces(text, [rows], others)
    imgs[0] = unit_pieces(image, [rows], txts[0])
    for place in range(1, len(txt_bits)):
        txts[1 << place] = [swapped(txts[0][0], txt_bits[place])]
    imgs[1] = unit_pieces(img_raw[0], cuts, imgs[0])
    txts[1] = unit_pieces(txt_raw, [rows], imgs[1][:1])
    for offset in range(1 << len(img_bits)):
        if offset not in imgs:
            high = offset.bit_length() - 1
            low = (offset & -offset).bit_length() - 1
            imgs[offset] = [
                swapped(imgs[offset ^ 1 << high][0], img_bits[high]),
                swapped(imgs[offset ^ 1 << low][1], img_bits[low]),
            ]
    for offset in range(1 << len(txt_bits)):
        if offset not in txts:
            high = offset.bit_length() - 1
            txts[offset] = [swapped(txts[offset ^ 1 << high][0], txt_bits[high])]
    imgs = [imgs[offset] for offset in range(1 << len(img_bits))]
    txts = [txts[offset] for offset in range(1 << len(txt_bits))]
    last = held(imgs[-1][1:], [], GATHER_COST)
    imgs[-1] = held(imgs[-1][:1], last, GATHER_COST) + last
    txts[-1] = held(txts[-1], imgs[-1][:1])
    return imgs, txts


def store_part(part, start, outs, cuts, rows):
    for at in range(start // rows, (start + part.shape[0]) // rows):
        size = rows // cuts[at]
        for place in range(cuts[at]):
            out = outs[sum(cuts[:at]) + place]
            first = at * rows - start + place * size
            out[...] = part[first : first + size].astype(out.dtype)


def tile_kernel(img_places, txt_places, img_cuts, txt_cuts, rows, *refs):
    n_img, n_txt = len(img_places), len(txt_places)
    taken = 0
    sources = []
    for places in (img_places, txt_places):
        pieces = sum(places)
        sources.append(refs[taken : taken + pieces])
        taken += pieces
    log_temp, bias = refs[taken : taken + 2]
    taken += 2
    img_parts = refs[taken : taken + sum(img_cuts)]
    taken += sum(img_cuts)
    txt_parts = refs[taken : taken + sum(txt_cuts)]
    sums, img_b, txt_b, grad_b = refs[taken + sum(txt_cuts) :]
    for group, held in zip(sources, (img_b, txt_b)):
        start = 0
        for piece in group:
            end = start + piece.shape[0]
            held[start:end] = piece[...]
            start = end
    temp = jnp.exp(log_temp[...])
    shift_b = bias[...]
    sum_g = jnp.zeros((8, 128), jnp.float32)
    sum_gl = jnp.zeros((8, 128), jnp.float32)
    step = 2 * rows
    for start in range(0, n_img * rows, step):
        panel = img_b[start : start + step]
        cosine = lax.dot_general(
            panel, txt_b[...], (((1,), (1,)), ((), ())), preferred_element_type=jnp.float32
        )
        scaled = temp * cosine
        logits = scaled + shift_b
        if start == 0:
            at_row = lax.broadcasted_iota(jnp.int32, logits.shape, 0)
            at_col = lax.broadcasted_iota(jnp.int32, logits.shape, 1)
            own = jnp.logical_and(at_row == at_col, at_row < rows)
            sign = jnp.where(own, 1.0, -1.0)
            grads = -sign * jax.nn.sigmoid(-sign * logits)
        else:
            grads = jax.nn.sigmoid(logits)
        sum_g = sum_g + lane_sums(grads)
        sum_gl = sum_gl + lane_sums(grads * scaled)
        grads_b = grads.astype(jnp.bfloat16)
        grad_b[start : start + step] = grads_b
        part = jnp.dot(grads_b, txt_b[...], preferred_element_type=jnp.float32)
        store_part(temp * part, start, img_parts, img_cuts, rows)
    sums[0:8] = sum_g
    sums[8:16] = sum_gl
    for start in range(0, n_txt * rows, step):
        part = lax.dot_general(
            grad_b[:, start : start + step],
            img_b[...],
            (((0,), (0,)), ((), ())),
            preferred_element_type=jnp.float32,
        )
        store_part(temp * part, start, txt_parts, txt_cuts, rows)


def tile_call(imgs, txts, log_temp, bias):
    rows = sum(piece.shape[0] for piece in imgs[0])
    width = imgs[0][0].shape[1]
    n_img, n_txt = len(imgs), len(txts)
    flat = [piece for block in imgs + txts for piece in block]
    pairs = n_img * n_txt * rows * rows
    img_cuts = [1] * n_img
    txt_cuts = [1] * n_txt
    outs = []
    for cuts in (img_cuts, txt_cuts):
        for at, cut in enumerate(cuts):
            kind = jnp.float32 if at < len(cuts) // 2 else jnp.bfloat16
            outs += [jax.ShapeDtypeStruct((rows // cut, width), kind)] * cut
    results = pl.pallas_call(
        functools.partial(
            tile_kernel,
            [len(block) for block in imgs],
            [len(block) for block in txts],
            img_cuts,
            txt_cuts,
            rows,
        ),
        out_shape=outs + [jax.ShapeDtypeStruct((16, 128), jnp.float32)],
        in_specs=[VMEM] * (len(flat) + 2),
        out_specs=[VMEM] * (len(outs) + 1),
        scratch_shapes=[
            pltpu.VMEM((n_img * rows, width), jnp.bfloat16),
            pltpu.VMEM((n_txt * rows, width), jnp.bfloat16),
            pltpu.VMEM((n_img * rows, n_txt * rows), jnp.bfloat16),
        ],
        compiler_params=pltpu.CompilerParams(vmem_limit_bytes=TILE_VMEM),
        cost_estimate=pl.CostEstimate(
            flops=6 * pairs * width, bytes_accessed=0, transcendentals=2 * pairs
        ),
    )(*flat, log_temp, bias)
    results = list(results)
    sums = results.pop()
    parts = [[results.pop(0) for _ in range(cut)] for cut in img_cuts + txt_cuts]
    return parts[:n_img], parts[n_img:], sums


def finish_rows(value, keep, recvs, out):
    total = keep[...]
    for recv in recvs:
        total = total + recv[...].astype(jnp.float32)
    unit, inverse = unit_rows(value[...])
    along = jnp.sum(unit * total, axis=1, keepdims=True)
    out[...] = ((total - unit * along) * inverse).astype(jnp.bfloat16)


def finish_first_kernel(value, keep, *refs):
    finish_rows(value, keep, refs[:-2], refs[-2])
    refs[-1][...] = jnp.zeros(refs[-1].shape, jnp.float32)


def finish_first(value, keep, recvs):
    return pl.pallas_call(
        finish_first_kernel,
        out_shape=(
            jax.ShapeDtypeStruct(value.shape, jnp.bfloat16),
            jax.ShapeDtypeStruct((8, 128), jnp.float32),
        ),
        in_specs=[VMEM] * (2 + len(recvs)),
        out_specs=[VMEM] * 2,
        compiler_params=pltpu.CompilerParams(vmem_limit_bytes=SMALL_VMEM),
        cost_estimate=pl.CostEstimate(flops=RETURN_COST, bytes_accessed=0, transcendentals=0),
    )(value, keep, *recvs)


def finish_last_kernel(pairs, token, sums, sums_recv, value, keep, *refs):
    total = sums[...] + sums_recv[...]
    for place in range(2):
        whole = jnp.sum(total[8 * place : 8 * place + 8], axis=0, keepdims=True)
        refs[place - 2][...] = jnp.sum(whole, axis=1, keepdims=True) / pairs
    finish_rows(value, keep, refs[:-3], refs[-3])


def finish_last(token, sums, sums_recv, pairs, value, keep, recvs):
    return pl.pallas_call(
        functools.partial(finish_last_kernel, pairs),
        out_shape=[jax.ShapeDtypeStruct(value.shape, jnp.bfloat16)]
        + [jax.ShapeDtypeStruct((1, 1), jnp.float32)] * 2,
        in_specs=[ANY] + [VMEM] * (4 + len(recvs)),
        out_specs=[VMEM] * 3,
        compiler_params=pltpu.CompilerParams(vmem_limit_bytes=SMALL_VMEM),
    )(token, sums, sums_recv, value, keep, *recvs)


def add_kernel(keep, recv, *refs):
    out = refs[-1]
    out[...] = (keep[...] + recv[...].astype(jnp.float32)).astype(out.dtype)


def sums_kernel(first, second, *refs):
    refs[-1][...] = first[...] + second[...]


def sums_call(sums, others):
    return pl.pallas_call(
        sums_kernel,
        out_shape=jax.ShapeDtypeStruct(sums[0].shape, sums[0].dtype),
        in_specs=[VMEM] * len(sums) + [ANY] * len(others),
        out_specs=VMEM,
        compiler_params=pltpu.CompilerParams(vmem_limit_bytes=SMALL_VMEM),
        cost_estimate=pl.CostEstimate(flops=SUMS_COST, bytes_accessed=0, transcendentals=0),
    )(*sums, *others)


def add_call(keep, recv, dtype, others):
    return pl.pallas_call(
        add_kernel,
        out_shape=jax.ShapeDtypeStruct(keep.shape, dtype),
        in_specs=[VMEM] * 2 + [ANY] * len(others),
        out_specs=VMEM,
        compiler_params=pltpu.CompilerParams(vmem_limit_bytes=SMALL_VMEM),
        cost_estimate=pl.CostEstimate(
            flops=keep.size, bytes_accessed=keep.size, transcendentals=0
        ),
    )(keep, recv, *others)


def returned(parts, bits, others, wait):
    parts = dict(enumerate(parts))
    recvs = []
    for place in reversed(range(len(bits))):
        arrived = {}
        for offset in range(1, 1 << place):
            arrived[offset] = swapped(parts.pop(offset | 1 << place), bits[place])
        for offset, recv in arrived.items():
            kind = jnp.float32 if offset < 1 << (place - 1) else jnp.bfloat16
            parts[offset] = add_call(parts[offset], recv, kind, others)
            others = [parts[offset]]
        send = parts.pop(1 << place)
        if arrived and wait:
            send = held([send], others)[0]
        recvs.append(swapped(send, bits[place]))
    return parts[0], recvs, others


def shards(image_embeds, text_embeds, log_temp, bias):
    rows, width = image_embeds.shape
    count = lax.axis_size("blk")
    depth = count.bit_length() - 1
    all_bits = [1 << place for place in range(depth)]
    split = 1 + depth // 2
    img_bits = all_bits[1:split][::-1]
    txt_bits = (all_bits[:1] + all_bits[split:])[::-1]
    txt_bits[0] |= img_bits[0]
    imgs, txts = gathered(image_embeds, text_embeds, img_bits, txt_bits)
    img_parts, txt_parts, sums = tile_call(imgs, txts, log_temp.reshape(1, 1), bias.reshape(1, 1))
    img_parts, txt_parts = ([part[0] for part in parts] for parts in (img_parts, txt_parts))
    txt_keep, txt_recvs, others = returned(txt_parts, txt_bits, [], False)
    for bit in img_bits[:1] + txt_bits[1:] + img_bits[:0:-1]:
        sums = sums_call([sums, swapped(sums, bit)], others)
    img_keep, img_recvs, others = returned(img_parts, img_bits, others + [sums], True)
    sums_recv = swapped(sums, txt_bits[0])
    grad_text, token = finish_first(text_embeds, txt_keep, txt_recvs)
    pairs = float(rows * count) * float(rows * count)
    grad_image, grad_bias, grad_temp = finish_last(
        token, sums, sums_recv, pairs, image_embeds, img_keep, img_recvs
    )
    return (grad_image, grad_text, grad_temp.reshape(1), grad_bias.reshape(1))


def solution(mesh):
    in_specs = (P(("groups", "blk"), None), P(("groups", "blk"), None), P(), P())
    out_specs = (P(("groups", "blk"), None), P(("groups", "blk"), None), P("groups"), P("groups"))
    return jax.shard_map(shards, mesh=mesh, in_specs=in_specs, out_specs=out_specs, check_vma=False)
```
